256 devices in a mesh: dp: 8 (over y, core), ctx: 8 (over z), mp: 4 (over x).
Axes of the slice: x: 4, y: 4, z: 8, core: 2. Of those that a mesh axis runs over, the one named last changes fastest.
Arguments:
- text_rows: bfloat16 [32768, 4096], P(('dp', 'ctx'), 'mp'), may hold values from -210 to 210
- visual_rows: bfloat16 [4096, 4096], P(('dp', 'ctx'), 'mp'), may hold values from -210 to 210, as said below
- image_counts: int32 [8], replicated, may hold values from 1 to 8, as said below
- image_starts: int32 [8, 8], replicated, may hold values from -1 to 4032, as said below
- norm_gain: float32 [4096], replicated, may hold values from 0.5 to 8
- w_query: bfloat16 [4096, 4096], P(None, 'mp'), may hold values from -0.09375 to 0.09375
- w_key: bfloat16 [4096, 512], P(None, 'mp'), may hold values from -0.09375 to 0.09375
- w_value: bfloat16 [4096, 512], P(None, 'mp'), may hold values from -0.09375 to 0.09375
Outputs:
- attn_mix: bfloat16 [32768, 4096], P(('dp', 'ctx'), 'mp')
The draws below stay inside these ranges and needn't reach their ends.
Inputs may be any that keep to these rules, and one draw needn't show every extreme that they name: `image_counts`: every draw has a sample with 8 images. `image_starts`: for k below image_counts[s], image k of sample s starts at this position, a multiple of 64, rising with k, images never intersecting; the other entries are -1. Every sample with 8 images has one in its last 64 positions. `visual_rows`: visual rows; rows of slots past the last image are not read.
All inputs are finite; a program needn't handle non-finite values.
Results may differ from the reference program's by a relative error of at most 0.0075.
The reference program's roundings to bfloat16 on the way (of `context`, `normed`, `queries` and `weights`) count: a program that leaves them out, or rounds other values in their place, can miss the bound.
Values may be sent and summed in bfloat16 or wider, within the bound.
No kernel may reach another device: no remote copies, remote signals or barrier semaphores. Data moves between devices by JAX's collectives and lax.ppermute only.
A program may use at most 192 MiB of HBM per device.

```python
import math
import jax
import jax.numpy as jnp
from jax import lax

D = 4096
HD = 128
Q_HEADS = 32
KV_HEADS = 4
TOK_DEV = 512
IMG_TOK = 64
MAX_IMG = 8
SAMPLES = 8
SEQ = 4096


def order_starts(picks, count_one):
    block_total = SEQ // IMG_TOK
    slot_index = jnp.arange(MAX_IMG, dtype=jnp.int32)
    alive = slot_index < count_one
    ordered = jnp.sort(jnp.where(alive, picks, block_total))
    return jnp.where(alive, ordered * IMG_TOK, -1)


def image_layout(key):
    key = jax.random.fold_in(key, 11)
    total_key, spread_key, last_key, first_key, rest_key = jax.random.split(key, 5)
    before = SAMPLES - 1
    half_dp = SAMPLES // 2
    shard_total = SEQ // TOK_DEV
    slot_width = MAX_IMG // shard_total
    lowest = (half_dp - 1) * MAX_IMG
    offset_last = jax.random.randint(total_key, (), max(before, lowest), lowest + MAX_IMG).astype(jnp.int32)
    extra = offset_last - before
    ranks = jax.random.permutation(spread_key, before * (MAX_IMG - 1))
    chosen = (ranks < extra).astype(jnp.int32).reshape(before, MAX_IMG - 1)
    first_counts = 1 + jnp.sum(chosen, axis=1)
    has_full = jnp.any(first_counts == MAX_IMG)
    last_count = jnp.where(has_full, jax.random.randint(last_key, (), 1, MAX_IMG + 1), MAX_IMG)
    counts = jnp.concatenate([first_counts, last_count[None]]).astype(jnp.int32)
    block_total = SEQ // IMG_TOK
    per_shard = TOK_DEV // IMG_TOK
    slot_index = jnp.arange(MAX_IMG, dtype=jnp.int32)

    def first_sample(sample_seed, count_one):
        picks = jax.random.permutation(sample_seed, block_total - 1)[:MAX_IMG].astype(jnp.int32)
        picks = jnp.where((count_one == MAX_IMG) & (slot_index == 0), block_total - 1, picks)
        return order_starts(picks, count_one)
    first_starts = jax.vmap(first_sample)(jax.random.split(first_key, before), first_counts)
    target_shard = offset_last // slot_width - (half_dp - 1) * shard_total
    first_block = (target_shard * per_shard).astype(jnp.int32)
    blocks = jnp.arange(block_total, dtype=jnp.int32)
    block_ranks = jax.random.permutation(rest_key, block_total).astype(jnp.int32)
    usable = (blocks > first_block) & (blocks < block_total - 1)
    order = jnp.argsort(jnp.where(usable, block_ranks, block_ranks + block_total), stable=True).astype(jnp.int32)
    picks = jnp.concatenate([first_block[None], order[:MAX_IMG - 1]])
    picks = jnp.where((last_count == MAX_IMG) & (slot_index == 1), block_total - 1, picks)
    last_starts = order_starts(picks, last_count)
    starts = jnp.concatenate([first_starts, last_starts[None]], axis=0)
    return (counts, starts.astype(jnp.int32))


def draw_image_counts(key, part):
    return image_layout(key)[0]


def draw_image_starts(key, part):
    return image_layout(key)[1]


def scaled_rows(key, row_count):
    base_key, row_key, col_key = jax.random.split(key, 3)
    normal_part = jnp.clip(jax.random.normal(base_key, (row_count, D), jnp.float32), -5.0, 5.0)
    base = normal_part
    row_scale = jnp.exp(jax.random.uniform(row_key, (row_count, 1), jnp.float32, 0.0, math.log(10.0)))
    col_scale = jnp.exp(jax.random.uniform(col_key, (1, D), jnp.float32, math.log(0.3), math.log(3.0)))
    return (base * row_scale * col_scale).astype(jnp.bfloat16)


def draw_text_rows(key, part):
    key = jax.random.fold_in(key, 3)
    return scaled_rows(key, SAMPLES * SEQ)


def draw_visual_rows(key, part):
    key = jax.random.fold_in(key, 5)
    return scaled_rows(key, SAMPLES * MAX_IMG * IMG_TOK)


def draw_norm_gain(key, part):
    key = jax.random.fold_in(key, 7)
    return jax.random.uniform(key, (D,), jnp.float32, 0.5, 1.5)


def block_scale(own_key, extent, cuts, low, largest):
    def one(axis_at, shards_of):
        steps = jax.random.uniform(jax.random.fold_in(jax.random.fold_in(own_key, 6), axis_at), (shards_of,), jnp.float32, low / len(cuts), largest / len(cuts))
        return jnp.repeat(jnp.exp(steps), extent[axis_at] // shards_of).reshape((-1,) + (1,) * (len(extent) - axis_at - 1))

    loudness = one(*cuts[0])
    for cut in cuts[1:]:
        loudness = loudness * one(*cut)
    return loudness


def gaussian(key, dims, scale, most, pieces=(), kind=jnp.bfloat16):
    level = block_scale(key, dims, pieces, -0.22, 0.18) if pieces else 1.0
    drawn = jax.random.normal(key, dims, jnp.float32) * scale * level
    return jnp.minimum(jnp.maximum(drawn, -most), most).astype(kind)


def setup_inputs(seed: int = 0) -> dict:
    keys = jax.random.split(jax.random.key(seed), 9)
    return {
        "text_rows": draw_text_rows(jax.random.fold_in(keys[8], 71), 0),
        "visual_rows": draw_visual_rows(jax.random.fold_in(keys[8], 71), 0),
        "image_counts": draw_image_counts(jax.random.fold_in(keys[8], 71), 0),
        "image_starts": draw_image_starts(jax.random.fold_in(keys[8], 71), 0),
        "norm_gain": draw_norm_gain(jax.random.fold_in(keys[8], 71), 0),
        "w_query": gaussian(keys[5], (D, Q_HEADS * HD), D ** -0.5, 0.09375, ((1, 4),)),
        "w_key": gaussian(keys[6], (D, KV_HEADS * HD), D ** -0.5, 0.09375, ((1, 4),)),
        "w_value": gaussian(keys[7], (D, KV_HEADS * HD), D ** -0.5, 0.09375, ((1, 4),)),
    }


rope_base = 500000.0
eps = 1e-05

def rotary(vectors, positions):
    half_size = vectors.shape[-1] // 2
    exponent = jnp.arange(half_size, dtype=jnp.float32) * (2.0 / vectors.shape[-1])
    frequency = jnp.exp(-exponent * math.log(rope_base))
    angles = positions.astype(jnp.float32)[:, None] * frequency[None, :]
    cosine = jnp.cos(angles)[:, None, :]
    sine = jnp.sin(angles)[:, None, :]
    first = vectors[..., :half_size]
    second = vectors[..., half_size:]
    return jnp.concatenate([first * cosine - second * sine, second * cosine + first * sine], axis=-1)

def assemble(text_rows, visual_rows, image_counts, image_starts):
    offsets = (jnp.cumsum(image_counts) - image_counts).astype(jnp.int32)
    positions = jnp.arange(SEQ, dtype=jnp.int32)
    image_index = jnp.arange(MAX_IMG, dtype=jnp.int32)
    alive = image_index[None, :] < image_counts[:, None]
    inside = alive[:, None, :] & (positions[None, :, None] >= image_starts[:, None, :]) & (positions[None, :, None] < image_starts[:, None, :] + IMG_TOK)
    is_visual = jnp.any(inside, axis=2)
    which_image = lax.optimization_barrier(jnp.sum(jnp.where(inside, image_index[None, None, :], 0), axis=2))
    image_start = lax.optimization_barrier(jnp.sum(jnp.where(inside, image_starts[:, None, :], 0), axis=2))
    source_row = (offsets[:, None] + which_image) * IMG_TOK + positions[None, :] - image_start
    source_row = jnp.where(is_visual, source_row, 0).astype(jnp.int32).reshape(-1)
    picked = jnp.take(visual_rows, source_row, axis=0)
    return jnp.where(is_visual.reshape(-1, 1), picked, text_rows)

def attend(queries, keys_all, values_all):
    group_size = Q_HEADS // KV_HEADS
    positions = jnp.arange(SEQ, dtype=jnp.int32)
    visible = positions[None, :] <= positions[:, None]
    score_scale = 1.0 / math.sqrt(HD)

    def one_head(head_index):
        q_head = lax.dynamic_index_in_dim(queries, head_index, 1, keepdims=False)
        k_head = lax.dynamic_index_in_dim(keys_all, head_index // group_size, 1, keepdims=False)
        v_head = lax.dynamic_index_in_dim(values_all, head_index // group_size, 1, keepdims=False)
        scores = jnp.dot(q_head, k_head.T, preferred_element_type=jnp.float32) * score_scale
        masked = jnp.where(visible, scores, -1e+30)
        row_top = lax.optimization_barrier(jnp.max(masked, axis=1, keepdims=True))
        weights = jnp.where(visible, jnp.exp(masked - row_top), 0.0)
        weight_total = lax.optimization_barrier(jnp.sum(weights, axis=1, keepdims=True))
        mixed_out = jnp.dot(weights.astype(jnp.bfloat16), v_head, preferred_element_type=jnp.float32)
        return (mixed_out / weight_total).astype(jnp.bfloat16)
    heads_out = lax.map(one_head, jnp.arange(Q_HEADS, dtype=jnp.int32))
    return jnp.transpose(heads_out, (1, 0, 2)).reshape(SEQ, Q_HEADS * HD)

def reference(text_rows, visual_rows, image_counts, image_starts, norm_gain, w_query, w_key, w_value):
    context = assemble(text_rows, visual_rows, image_counts, image_starts)
    widened = context.astype(jnp.float32)
    mean_square = lax.optimization_barrier(jnp.mean(widened * widened, axis=1, keepdims=True))
    normed = (widened * lax.rsqrt(mean_square + eps) * norm_gain[None, :]).astype(jnp.bfloat16)
    query_lin = jnp.dot(normed, w_query, preferred_element_type=jnp.float32)
    key_lin = jnp.dot(normed, w_key, preferred_element_type=jnp.float32)
    value_lin = jnp.dot(normed, w_value, preferred_element_type=jnp.float32)
    positions = jnp.tile(jnp.arange(SEQ, dtype=jnp.int32), SAMPLES)
    queries = rotary(query_lin.reshape(-1, Q_HEADS, HD), positions).astype(jnp.bfloat16)
    keys_all = rotary(key_lin.reshape(-1, KV_HEADS, HD), positions).astype(jnp.bfloat16)
    values_all = value_lin.reshape(-1, KV_HEADS, HD).astype(jnp.bfloat16)

    def per_sample(triple):
        return attend(triple[0], triple[1], triple[2])
    mixed_all = lax.map(per_sample, (queries.reshape(SAMPLES, SEQ, Q_HEADS, HD), keys_all.reshape(SAMPLES, SEQ, KV_HEADS, HD), values_all.reshape(SAMPLES, SEQ, KV_HEADS, HD)))
    return mixed_all.reshape(SAMPLES * SEQ, Q_HEADS * HD)
```

```python
import functools
import math

import jax
import jax.numpy as jnp
from jax import lax
from jax.experimental import pallas as pl
from jax.experimental.pallas import tpu as pltpu
from jax.sharding import PartitionSpec as P

HD = 128
IMG_TOK = 64
MAX_IMG = 8
D = 4096
SHARDS = 8
rope_base = 500000.0
eps = 1e-05
BF16 = jnp.bfloat16
F32 = jnp.float32
VMEM = pltpu.VMEM
SMEM = pltpu.SMEM


def rotary_tables(positions):
    half_size = HD // 2
    exponent = jnp.arange(half_size, dtype=F32) * (2.0 / HD)
    frequency = jnp.exp(-exponent * math.log(rope_base))
    angles = positions.astype(F32)[:, None] * frequency[None, :]
    cosine, sine = jnp.cos(angles), jnp.sin(angles)
    return jnp.concatenate([cosine, cosine], axis=1), jnp.concatenate([-sine, sine], axis=1)


def rotate(u, cosine, sine):
    return u * cosine + pltpu.roll(u, HD // 2, 1) * sine


def exchange(x, mask):
    return lax.ppermute(x, "mp", [(i, i ^ mask) for i in range(4)])


def first_hop(x):
    return exchange(x, 1), exchange(x, 3)


def second_hop(a, b):
    half = a.shape[0] // 2
    return exchange(a[:half], 3), exchange(b[half:], 1)


def key_value_kernel(row_counts, mp_ref, *refs):
    groups = len(row_counts)
    gain_ref, w_ref, cos_ref, sin_ref = refs[5 * groups : 5 * groups + 4]
    normed_ref, kv_ref = refs[5 * groups + 4 :]
    mp = mp_ref[0]
    base = 0
    for g, rows in enumerate(row_counts):
        own, one, three, two_lo, two_hi = refs[5 * g : 5 * g + 5]
        half = rows // 2
        for part, two in ((0, two_lo), (1, two_hi)):
            span = pl.ds(part * half, half)
            pieces = [(0, own[span, :]), (1, one[span, :]), (3, three[span, :]), (2, two[...])]
            total = jnp.zeros((half, 1), F32)
            for _, piece in pieces:
                wide = piece.astype(F32)
                total = total + jnp.sum(wide * wide, axis=1, keepdims=True)
            scale = lax.rsqrt(total * (1.0 / D) + eps)
            for mask, piece in pieces:
                columns = pl.ds(pl.multiple_of((mp ^ mask) * 1024, 1024), 1024)
                value = piece.astype(F32) * scale * gain_ref[:, columns]
                normed_ref[pl.ds(base + part * half, half), columns] = value.astype(BF16)
        base += rows
    product = jnp.dot(normed_ref[...], w_ref[...], preferred_element_type=F32)
    kv_ref[:, :HD] = rotate(product[:, :HD], cos_ref[...], sin_ref[...]).astype(BF16)
    kv_ref[:, HD:] = product[:, HD:].astype(BF16)


def key_value(mp, groups, gain, w_kv, cosine, sine):
    row_counts = tuple(g[0].shape[0] for g in groups)
    rows = sum(row_counts)
    arrays = [a for g in groups for a in g]
    return pl.pallas_call(
        functools.partial(key_value_kernel, row_counts),
        out_shape=(
            jax.ShapeDtypeStruct((rows, D), BF16),
            jax.ShapeDtypeStruct((rows, 2 * HD), BF16),
        ),
        in_specs=[pl.BlockSpec(memory_space=SMEM)]
        + [pl.BlockSpec(memory_space=VMEM)] * (len(arrays) + 4),
        out_specs=[pl.BlockSpec(memory_space=VMEM)] * 2,
        compiler_params=pltpu.CompilerParams(vmem_limit_bytes=40 * 2**20),
        cost_estimate=pl.CostEstimate(
            flops=2 * rows * D * 2 * HD, bytes_accessed=rows * D * 4 + D * 512, transcendentals=0
        ),
        name="key_value",
    )(mp, *arrays, gain, w_kv, cosine, sine)


def query_kernel(x_ref, w_ref, cos_ref, sin_ref, q_ref):
    product = jnp.dot(x_ref[...], w_ref[...], preferred_element_type=F32)
    for h in range(2):
        span = slice(h * HD, (h + 1) * HD)
        q_ref[:, span] = rotate(product[:, span], cos_ref[...], sin_ref[...]).astype(BF16)


def query(normed, w_query, cosine, sine):
    rows, columns = normed.shape[0], w_query.shape[1]
    tile = 2 * HD
    return pl.pallas_call(
        query_kernel,
        out_shape=jax.ShapeDtypeStruct((rows, columns), BF16),
        grid=(columns // tile,),
        in_specs=[
            pl.BlockSpec((rows, D), lambda n: (0, 0)),
            pl.BlockSpec((D, tile), lambda n: (0, n)),
            pl.BlockSpec((rows, HD), lambda n: (0, 0)),
            pl.BlockSpec((rows, HD), lambda n: (0, 0)),
        ],
        out_specs=pl.BlockSpec((rows, tile), lambda n: (0, n)),
        compiler_params=pltpu.CompilerParams(vmem_limit_bytes=40 * 2**20),
        cost_estimate=pl.CostEstimate(
            flops=2 * rows * D * columns, bytes_accessed=D * columns * 2 + rows * D * 2, transcendentals=0
        ),
        name="query",
    )(normed, w_query, cosine, sine)


def attention_kernel(
    tok, heads, info_ref, *refs
):
    q_refs = refs[:2]
    own_refs = refs[2:4]
    far_refs = refs[4 : 4 + SHARDS - 1]
    img_ref = refs[4 + SHARDS - 1]
    out_ref = refs[5 + SHARDS - 1]
    q_buf, kt_buf, v_buf, s_buf, max_buf, sum_buf, acc_buf = refs[6 + SHARDS - 1 :]
    step = pl.program_id(0)
    ctx = info_ref[0]
    factor = math.log2(math.e) / math.sqrt(HD)
    half = tok // 2

    @pl.when(step == 0)
    def _():
        for part in range(2):
            q_buf[pl.ds(part * half, half), :] = q_refs[part][...]
            rows = pl.ds(pl.multiple_of(ctx * tok + part * half, half), half)
            v_buf[rows, :] = own_refs[part][...]
        for d in range(1, SHARDS):
            @pl.when(ctx >= d)
            def _():
                rows = pl.ds(pl.multiple_of((ctx - d) * tok, tok), tok)
                v_buf[rows, :] = far_refs[d - 1][...]
        for c in range(MAX_IMG):
            start = info_ref[1 + c]

            @pl.when(start >= 0)
            def _():
                v_buf[pl.ds(pl.multiple_of(start, IMG_TOK), IMG_TOK), :] = img_ref[c, :, heads * HD :]

            @pl.when((start >= ctx * tok) & (start < ctx * tok + tok))
            def _():
                rows = pl.ds(pl.multiple_of(start - ctx * tok, IMG_TOK), IMG_TOK)
                q_buf[rows, :] = img_ref[c, :, : heads * HD]

        @pl.loop(0, ctx + 1)
        def _(j):
            rows = pl.ds(pl.multiple_of(j * tok, tok), tok)
            kt_buf[j] = v_buf[rows, :HD].astype(F32).T.astype(BF16)

    def score(j, slot, q_head, masked):
        s = jnp.dot(q_head, kt_buf[j], preferred_element_type=F32)
        if masked:
            row = lax.broadcasted_iota(jnp.int32, (tok, tok), 0)
            column = lax.broadcasted_iota(jnp.int32, (tok, tok), 1)
            s = jnp.where(column <= row, s, -1e30)
        s_buf[slot, j] = s
        top = s[:, :HD]
        for g in range(1, tok // HD):
            top = jnp.maximum(top, s[:, g * HD : (g + 1) * HD])
        return top

    def mix(j, slot):
        top = max_buf[slot]
        weights = []
        total = None
        for g in range(tok // HD):
            w = jnp.exp2(s_buf[slot, j, :, g * HD : (g + 1) * HD] * factor - top)
            total = w if total is None else total + w
            weights.append(w.astype(BF16))
        rows = pl.ds(pl.multiple_of(j * tok, tok), tok)
        acc = jnp.dot(
            jnp.concatenate(weights, axis=1), v_buf[rows, HD:], preferred_element_type=F32
        )
        return total, acc

    def phase(do_score, do_mix):
        slot = lax.rem(step, 2)
        other = 1 - slot
        if do_score:
            columns = pl.ds(pl.multiple_of(step * HD, HD), HD)
            q_head = q_buf[:, columns]
            top = score(ctx, slot, q_head, True)
            max_buf[slot] = top
        if do_mix:
            total, acc = mix(ctx, other)
            sum_buf[...] = total
            acc_buf[...] = acc

        @pl.loop(0, ctx)
        def _(j):
            if do_score:
                max_buf[slot] = jnp.maximum(max_buf[slot], score(j, slot, q_head, False))
            if do_mix:
                total, acc = mix(j, other)
                sum_buf[...] += total
                acc_buf[...] += acc

        if do_score:
            top = jnp.max(max_buf[slot], axis=1, keepdims=True) * factor
            max_buf[slot] = jnp.broadcast_to(top, (tok, HD))
        if do_mix:
            total = jnp.sum(sum_buf[...], axis=1, keepdims=True)
            out_ref[...] = (acc_buf[...] / total).astype(BF16)

    pl.when(step == 0)(lambda: phase(True, False))
    pl.when((step > 0) & (step < heads))(lambda: phase(True, True))
    pl.when(step == heads)(lambda: phase(False, True))


def attention(info, q_parts, own_parts, far_parts, img_all, tok, heads):
    whole = pl.BlockSpec(memory_space=VMEM)
    count = len(q_parts) + len(own_parts) + len(far_parts) + 1
    return pl.pallas_call(
        functools.partial(attention_kernel, tok, heads),
        out_shape=jax.ShapeDtypeStruct((tok, heads * HD), BF16),
        grid=(heads + 1,),
        in_specs=[pl.BlockSpec(memory_space=SMEM)] + [whole] * count,
        out_specs=pl.BlockSpec((tok, HD), lambda t: (0, jnp.maximum(t - 1, 0))),
        scratch_shapes=[
            pltpu.VMEM((tok, heads * HD), BF16),
            pltpu.VMEM((SHARDS, HD, tok), BF16),
            pltpu.VMEM((SHARDS * tok, 2 * HD), BF16),
            pltpu.VMEM((2, SHARDS, tok, tok), F32),
            pltpu.VMEM((2, tok, HD), F32),
            pltpu.VMEM((tok, HD), F32),
            pltpu.VMEM((tok, HD), F32),
        ],
        compiler_params=pltpu.CompilerParams(vmem_limit_bytes=52 * 2**20),
        cost_estimate=pl.CostEstimate(
            flops=4 * tok * heads * SHARDS * tok * HD,
            bytes_accessed=8 * 2**20,
            transcendentals=tok * heads * SHARDS * tok,
        ),
        name="attention",
    )(info, *q_parts, *own_parts, *far_parts, img_all)


def on_device(
    text_rows, visual_rows, image_counts, image_starts, norm_gain, w_query, w_key, w_value
):
    ctx = lax.axis_index("ctx")
    sample = lax.axis_index("dp")
    mp = lax.axis_index("mp")
    tok = text_rows.shape[0]
    half = tok // 2
    heads = w_query.shape[1] // HD

    before = jnp.sum(jnp.where(jnp.arange(SHARDS) < sample, image_counts, 0))
    count = lax.dynamic_index_in_dim(image_counts, sample, 0, keepdims=False)
    starts = lax.dynamic_index_in_dim(image_starts, sample, 0, keepdims=False)
    residue = jnp.arange(SHARDS, dtype=jnp.int32)
    slot = (residue - before) & (MAX_IMG - 1)
    start_of = jnp.where(slot < count, jnp.take(starts, slot), -1)
    my_slot = (ctx - before) & (MAX_IMG - 1)
    source = jnp.minimum((before + my_slot) // SHARDS, SHARDS - 1)
    my_start = lax.dynamic_index_in_dim(start_of, ctx, 0, keepdims=False)

    gathered = lax.all_gather(visual_rows, "dp", axis=0)
    low, high = text_rows[:half], text_rows[half:]
    a_low, b_low = first_hop(low)
    a_high, b_high = first_hop(high)
    c_low, d_low = second_hop(a_low, b_low)
    c_high, d_high = second_hop(a_high, b_high)
    image = lax.dynamic_index_in_dim(gathered, source, 0, keepdims=False)
    a_img, b_img = first_hop(image)
    c_img, d_img = second_hop(a_img, b_img)

    w_kv = jnp.concatenate([w_key, w_value], axis=1)
    gain = norm_gain[None, :]
    cos_text, sin_text = rotary_tables(ctx * tok + jnp.arange(tok, dtype=jnp.int32))
    cos_img, sin_img = rotary_tables(my_start + jnp.arange(IMG_TOK, dtype=jnp.int32))
    mp_arr = mp.astype(jnp.int32)[None]

    def project(groups, cosine, sine):
        normed, kv = key_value(mp_arr, groups, gain, w_kv, cosine, sine)
        return query(normed, w_query, cosine, sine), kv

    q_low, kv_low = project([(low, a_low, b_low, c_low, d_low)], cos_text[:half], sin_text[:half])
    q_high, kv_high = project(
        [(high, a_high, b_high, c_high, d_high)], cos_text[half:], sin_text[half:]
    )
    q_img, kv_img = project([(image, a_img, b_img, c_img, d_img)], cos_img, sin_img)

    kv = jnp.concatenate([kv_low, kv_high], axis=0)
    far = [
        lax.ppermute(kv, "ctx", [(i, i + d) for i in range(SHARDS) if i + d < SHARDS])
        for d in range(1, SHARDS)
    ]
    img_all = lax.all_gather(jnp.concatenate([q_img, kv_img], axis=1), "ctx", axis=0)
    info = jnp.concatenate([ctx.astype(jnp.int32)[None], start_of.astype(jnp.int32)])
    return attention(info, [q_low, q_high], [kv_low, kv_high], far, img_all, tok, heads)


def solution(mesh):
    in_specs = (
        P(("dp", "ctx"), "mp"),
        P(("dp", "ctx"), "mp"),
        P(),
        P(),
        P(),
        P(None, "mp"),
        P(None, "mp"),
        P(None, "mp"),
    )
    out_specs = P(("dp", "ctx"), "mp")
    return jax.shard_map(
        on_device, mesh=mesh, in_specs=in_specs, out_specs=out_specs, check_vma=False
    )
```

```python
import functools
import math

import jax
import jax.numpy as jnp
from jax import lax
from jax.experimental import pallas as pl
from jax.experimental.pallas import tpu as pltpu
from jax.sharding import PartitionSpec as P

HD = 128
IMG_TOK = 64
MAX_IMG = 8
D = 4096
SHARDS = 8
rope_base = 500000.0
eps = 1e-05
BF16 = jnp.bfloat16
F32 = jnp.float32
VMEM = pltpu.VMEM
SMEM = pltpu.SMEM


def rotary_tables(positions):
    half_size = HD // 2
    exponent = jnp.arange(half_size, dtype=F32) * (2.0 / HD)
    frequency = jnp.exp(-exponent * math.log(rope_base))
    angles = positions.astype(F32)[:, None] * frequency[None, :]
    return jnp.cos(angles), jnp.sin(angles)


def rotate(u, cosine, sine):
    cosine = jnp.concatenate([cosine, cosine], axis=1)
    sine = jnp.concatenate([-sine, sine], axis=1)
    return u * cosine + pltpu.roll(u, HD // 2, 1) * sine


def shift(x, axis, d, wrap):
    pairs = [(i, (i + d) % SHARDS) for i in range(SHARDS) if wrap or 0 <= i + d < SHARDS]
    return lax.ppermute(x, axis, pairs)


def exchange(x, mask):
    return lax.ppermute(x, "mp", [(i, i ^ mask) for i in range(4)])


def first_hop(x):
    return exchange(x, 1), exchange(x, 3)


def second_hop(a, b):
    half = a.shape[0] // 2
    return exchange(a[:half], 3), exchange(b[half:], 1)


def key_value_kernel(row_counts, mp_ref, *refs):
    groups = len(row_counts)
    refs = refs[: 5 * groups + 4] + refs[-2:]
    gain_ref, w_ref, cos_ref, sin_ref = refs[5 * groups : 5 * groups + 4]
    normed_ref, kv_ref = refs[5 * groups + 4 :]
    mp = mp_ref[0]
    base = 0
    for g, rows in enumerate(row_counts):
        own, one, three, two_lo, two_hi = refs[5 * g : 5 * g + 5]
        half = rows // 2
        for part, two in ((0, two_lo), (1, two_hi)):
            span = pl.ds(part * half, half)
            pieces = [(0, own[span, :]), (1, one[span, :]), (3, three[span, :]), (2, two[...])]
            total = jnp.zeros((half, 1), F32)
            for _, piece in pieces:
                wide = piece.astype(F32)
                total = total + jnp.sum(wide * wide, axis=1, keepdims=True)
            scale = lax.rsqrt(total * (1.0 / D) + eps)
            for mask, piece in pieces:
                columns = pl.ds(pl.multiple_of((mp ^ mask) * 1024, 1024), 1024)
                value = piece.astype(F32) * scale * gain_ref[:, columns]
                normed_ref[pl.ds(base + part * half, half), columns] = value.astype(BF16)
        base += rows
    product = jnp.dot(normed_ref[...], w_ref[...], preferred_element_type=F32)
    kv_ref[:, :HD] = rotate(product[:, :HD], cos_ref[...], sin_ref[...]).astype(BF16)
    kv_ref[:, HD:] = product[:, HD:].astype(BF16)


def key_value(mp, groups, gain, w_kv, cosine, sine, after=()):
    row_counts = tuple(g[0].shape[0] for g in groups)
    rows = sum(row_counts)
    arrays = [a for g in groups for a in g]
    return pl.pallas_call(
        functools.partial(key_value_kernel, row_counts),
        out_shape=(
            jax.ShapeDtypeStruct((rows, D), BF16),
            jax.ShapeDtypeStruct((rows, 2 * HD), BF16),
        ),
        in_specs=[pl.BlockSpec(memory_space=SMEM)]
        + [pl.BlockSpec(memory_space=VMEM)] * (len(arrays) + 4)
        + [pl.BlockSpec(memory_space=pl.ANY)] * len(after),
        out_specs=[pl.BlockSpec(memory_space=VMEM)] * 2,
        compiler_params=pltpu.CompilerParams(vmem_limit_bytes=40 * 2**20),
        cost_estimate=pl.CostEstimate(
            flops=0, bytes_accessed=0, transcendentals=0
        ),
        name="key_value",
    )(mp, *arrays, gain, w_kv, cosine, sine, *after)


def images_before(counts_ref, sample):
    total = jnp.int32(0)
    for i in range(SHARDS):
        total = total + jnp.where(i < sample, counts_ref[i], 0)
    return total


def pick_kernel(other, ids_ref, counts_ref, *refs):
    out_ref, sem = refs[-2:]
    ctx, me = ids_ref[1], ids_ref[2]
    sample = me ^ 1 if other else me
    before = images_before(counts_ref, sample)
    owner = jnp.minimum((before + ((ctx - before) & (MAX_IMG - 1))) >> 3, SHARDS - 1)
    distance = jnp.clip((me >> 1) - (owner >> 1), 0, 3)
    which = distance if other else jnp.where(((owner ^ me) & 1) == 0, distance, 4)
    for d in range(4 if other else 5):
        @pl.when(which == d)
        def _():
            copy = pltpu.make_async_copy(refs[d], out_ref, sem)
            copy.start()
            copy.wait()


def pick(other, ids, counts, sources):
    return pl.pallas_call(
        functools.partial(pick_kernel, other),
        out_shape=jax.ShapeDtypeStruct(sources[0].shape, sources[0].dtype),
        in_specs=[pl.BlockSpec(memory_space=SMEM)] * 2
        + [pl.BlockSpec(memory_space=pl.ANY)] * len(sources),
        out_specs=pl.BlockSpec(memory_space=pl.ANY),
        scratch_shapes=[pltpu.SemaphoreType.DMA],
        name="pick",
    )(ids, counts, *sources)


def query_kernel(text, x_ref, w_ref, cos_ref, sin_ref, q_ref, *img_ref):
    product = jnp.dot(x_ref[...], w_ref[...], preferred_element_type=F32)
    for h in range(2):
        span = slice(h * HD, (h + 1) * HD)
        turned = rotate(product[:, span], cos_ref[...], sin_ref[...]).astype(BF16)
        q_ref[:, span] = turned[:text]
        if img_ref:
            img_ref[0][:, span] = turned[text:]


def query(normed, w_query, cosine, sine, text):
    rows, columns = normed.shape[0], w_query.shape[1]
    tile = 2 * HD
    img = rows - text
    out_shape = [jax.ShapeDtypeStruct((text, columns), BF16)]
    out_specs = [pl.BlockSpec((text, tile), lambda n: (0, n))]
    if img:
        out_shape.append(jax.ShapeDtypeStruct((img * (columns // tile), tile), BF16))
        out_specs.append(pl.BlockSpec((img, tile), lambda n: (n, 0)))
    return pl.pallas_call(
        functools.partial(query_kernel, text),
        out_shape=out_shape,
        grid=(columns // tile,),
        in_specs=[
            pl.BlockSpec((rows, D), lambda n: (0, 0)),
            pl.BlockSpec((D, tile), lambda n: (0, n)),
            pl.BlockSpec((rows, HD // 2), lambda n: (0, 0)),
            pl.BlockSpec((rows, HD // 2), lambda n: (0, 0)),
        ],
        out_specs=out_specs,
        compiler_params=pltpu.CompilerParams(vmem_limit_bytes=40 * 2**20),
        cost_estimate=pl.CostEstimate(flops=0, bytes_accessed=0, transcendentals=0),
        name="query",
    )(normed, w_query, cosine, sine)


def image_start(counts_ref, starts_ref, sample, residue):
    slot = (residue - images_before(counts_ref, sample)) & (MAX_IMG - 1)
    return jnp.where(slot < counts_ref[sample], starts_ref[sample, slot], -1)


def attention_kernel(part, half, heads, ids_ref, counts_ref, starts_ref, *refs):
    tok = 2 * half
    img_rows = IMG_TOK * (1 + heads // 2)
    step = pl.program_id(0)
    ctx, sample = ids_ref[1], ids_ref[2]
    factor = math.log2(math.e) / math.sqrt(HD)
    if part == 0:
        q_low, q_high, own, f1, f2, f3, b1, b2, b3, f4, b4 = refs[:11]
        q_ref, img_kv_ref, max_out, sum_out, acc_out = refs[-11:-6]
        kv_buf, img_buf, s_buf, max_buf, alpha_buf, sems = refs[-6:]
    else:
        q_ref, img_kv_ref, gathered, max_in, sum_in, acc_in = refs[:6]
        out_ref, kv_buf, s_buf, max_buf, alpha_buf, sems = refs[6:]

    def overlay(d):
        start = image_start(counts_ref, starts_ref, sample, (ctx - d) & (SHARDS - 1))
        shard, row = start >> (tok.bit_length() - 1), start & (tok - 1)

        @pl.when((start >= 0) & ((row >= half) if part else (row < half)))
        def _():
            place = shard * half + row - part * half
            kv_buf[pl.ds(pl.multiple_of(place, IMG_TOK), IMG_TOK), :] = img_kv_ref[d]

        if part == 0:
            @pl.when((start >= 0) & (shard == ctx))
            def _():
                rows = pl.ds(pl.multiple_of(row, IMG_TOK), IMG_TOK)
                for n in range(heads // 2):
                    q_ref[rows, n * 2 * HD : (n + 1) * 2 * HD] = img_buf[
                        d, IMG_TOK * (n + 1) : IMG_TOK * (n + 2), :
                    ]

    @pl.when(step == 0)
    def _():
        if part == 0:
            payloads = [own, f1, f2, f3, f4, b3, b2, b1]
            split = f4.shape[0] - half
            copies = [
                pltpu.make_async_copy(q_low, q_ref.at[pl.ds(0, half), :], sems.at[0]),
                pltpu.make_async_copy(q_high, q_ref.at[pl.ds(half, half), :], sems.at[1]),
                pltpu.make_async_copy(
                    b4, img_buf.at[4, pl.ds(split, img_rows - split), :], sems.at[2]
                ),
            ]
            for d, payload in enumerate(payloads):
                shard = (ctx - d) & (SHARDS - 1)
                rows = pl.ds(pl.multiple_of(shard * half, half), half)
                size = split if d == 4 else img_rows
                copies.append(
                    pltpu.make_async_copy(
                        payload.at[pl.ds(0, half), :], kv_buf.at[rows, :], sems.at[3 + 2 * d]
                    )
                )
                copies.append(
                    pltpu.make_async_copy(
                        payload.at[pl.ds(half, size), :],
                        img_buf.at[d, pl.ds(0, size), :],
                        sems.at[4 + 2 * d],
                    )
                )
        else:
            copies = [pltpu.make_async_copy(gathered, kv_buf, sems.at[0])]
        for copy in copies:
            copy.start()
        for copy in copies:
            copy.wait()
        for d in range(SHARDS):
            if part == 0:
                img_kv_ref[d] = img_buf[d, :IMG_TOK, :]
            overlay(d)

    def phase(shards, do_score, do_mix):
        slot = lax.rem(step, 2)
        other = 1 - slot
        width = shards * half
        if do_score:
            columns = pl.ds(pl.multiple_of(step * HD, HD), HD)
            s = lax.dot_general(
                q_ref[:, columns],
                kv_buf[:width, :HD],
                (((1,), (1,)), ((), ())),
                preferred_element_type=F32,
            )
            row = lax.broadcasted_iota(jnp.int32, (tok, half), 0)
            column = part * half + lax.broadcasted_iota(jnp.int32, (tok, half), 1)
            last = jnp.where(column <= row, s[:, width - half :], -1e30)
            s_buf[slot, :, width - half : width] = last
            top = last[:, :HD]
            for g in range(1, half // HD):
                top = jnp.maximum(top, last[:, g * HD : (g + 1) * HD])
            if shards > 1:
                s_buf[slot, :, : width - half] = s[:, : width - half]
                for g in range((width - half) // HD):
                    top = jnp.maximum(top, s[:, g * HD : (g + 1) * HD])
        if do_mix:
            shared = max_buf[other]
            total = sum_in[...] * alpha_buf[other] if part else None
            weights = []
            for g in range(width // HD):
                w = jnp.exp2(s_buf[other, :, g * HD : (g + 1) * HD] * factor - shared)
                total = w if total is None else total + w
                weights.append(w.astype(BF16))
            mixed = jnp.dot(
                jnp.concatenate(weights, axis=1), kv_buf[:width, HD:], preferred_element_type=F32
            )
            if part == 0:
                max_out[...] = shared
                sum_out[...] = total
                acc_out[...] = mixed
            else:
                mixed = mixed + acc_in[...] * alpha_buf[other]
                out_ref[...] = (mixed / jnp.sum(total, axis=1, keepdims=True)).astype(BF16)
        if do_score:
            top = jnp.broadcast_to(jnp.max(top, axis=1, keepdims=True) * factor, (tok, HD))
            if part:
                top = jnp.maximum(top, max_in[...])
                alpha_buf[slot] = jnp.exp2(max_in[...] - top)
            max_buf[slot] = top

    for v in range(SHARDS):
        @pl.when(ctx == v)
        def _():
            pl.when(step == 0)(lambda: phase(v + 1, True, False))
            pl.when((step > 0) & (step < heads))(lambda: phase(v + 1, True, True))
            pl.when(step == heads)(lambda: phase(v + 1, False, True))


def attention(part, half, heads, scalars, arrays, after=()):
    tok = 2 * half
    width = heads * HD
    img_rows = IMG_TOK * (1 + heads // 2)
    smem = pl.BlockSpec(memory_space=SMEM)
    far = pl.BlockSpec(memory_space=pl.ANY)
    here = pl.BlockSpec(memory_space=VMEM)
    this = pl.BlockSpec((tok, HD), lambda t: (0, jnp.minimum(t, heads - 1)))
    last = pl.BlockSpec((tok, HD), lambda t: (0, jnp.maximum(t - 1, 0)))
    queries = jax.ShapeDtypeStruct((tok, width), BF16)
    state = jax.ShapeDtypeStruct((tok, width), F32)
    if part == 0:
        in_specs = [far] * (len(arrays) + len(after))
        out_shape = [queries, jax.ShapeDtypeStruct((SHARDS, IMG_TOK, 2 * HD), BF16)] + [state] * 3
        out_specs = [
            pl.BlockSpec((tok, width), lambda t: (0, 0)),
            pl.BlockSpec((SHARDS, IMG_TOK, 2 * HD), lambda t: (0, 0, 0)),
        ] + [last] * 3
        images = [pltpu.VMEM((SHARDS, img_rows, 2 * HD), BF16)]
    else:
        in_specs = [here, here, far, this, last, last]
        out_shape, out_specs, images = queries, last, []
    return pl.pallas_call(
        functools.partial(attention_kernel, part, half, heads),
        out_shape=out_shape,
        grid=(heads + 1,),
        in_specs=[smem] * 3 + in_specs,
        out_specs=out_specs,
        scratch_shapes=[pltpu.VMEM((SHARDS * half, 2 * HD), BF16)]
        + images
        + [
            pltpu.VMEM((2, tok, SHARDS * half), F32),
            pltpu.VMEM((2, tok, HD), F32),
            pltpu.VMEM((2, tok, HD), F32),
            pltpu.SemaphoreType.DMA((3 + 2 * SHARDS,)),
        ],
        compiler_params=pltpu.CompilerParams(vmem_limit_bytes=48 * 2**20),
        cost_estimate=pl.CostEstimate(
            flops=2 * tok * heads * SHARDS * tok * HD,
            bytes_accessed=8 * 2**20,
            transcendentals=tok * heads * SHARDS * half,
        ),
        name="attention",
    )(*scalars, *arrays, *after)


def on_device(
    text_rows, visual_rows, image_counts, image_starts, norm_gain, w_query, w_key, w_value
):
    ctx = lax.axis_index("ctx").astype(jnp.int32)
    sample = lax.axis_index("dp").astype(jnp.int32)
    mp = lax.axis_index("mp").astype(jnp.int32)
    tok = text_rows.shape[0]
    half = tok // 2
    heads = w_query.shape[1] // HD
    ids = jnp.stack([mp, ctx, sample])

    low, high = text_rows[:half], text_rows[half:]
    a_low, b_low = first_hop(low)
    routed = [visual_rows] + [shift(visual_rows, "dp", 2 * d, False) for d in (1, 2, 3)]
    for_other = pick(True, ids, image_counts, routed)
    from_other = lax.ppermute(for_other, "dp", [(i, i ^ 1) for i in range(SHARDS)])
    image = pick(False, ids, image_counts, routed + [from_other])
    a_img, b_img = first_hop(image)
    a_high, b_high = first_hop(high)
    c_low, d_low = second_hop(a_low, b_low)
    c_img, d_img = second_hop(a_img, b_img)
    c_high, d_high = second_hop(a_high, b_high)

    w_kv = jnp.concatenate([w_key, w_value], axis=1)
    gain = norm_gain[None, :]
    every = jnp.arange(SHARDS, dtype=jnp.int32)
    before = jnp.sum(jnp.where(every < sample, image_counts, 0))
    my_slot = (ctx - before) & (MAX_IMG - 1)
    mine = (every[:, None] == sample) & (every[None, :] == my_slot)
    my_start = jnp.sum(jnp.where(mine, image_starts, 0))
    rows = jnp.arange(tok + IMG_TOK, dtype=jnp.int32)
    positions = jnp.where(
        rows < half,
        ctx * tok + rows,
        jnp.where(rows < half + IMG_TOK, my_start + rows - half, ctx * tok + rows - IMG_TOK),
    )
    cosine, sine = rotary_tables(positions)
    first = half + IMG_TOK
    mp_arr = ids[:1]

    normed, kv = key_value(
        mp_arr,
        [(low, a_low, b_low, c_low, d_low), (image, a_img, b_img, c_img, d_img)],
        gain, w_kv, cosine[:first], sine[:first],
    )
    q_low, q_img = query(normed, w_query, cosine[:first], sine[:first], half)
    own = jnp.concatenate([kv, q_img], axis=0)
    cut = own.shape[0] // 2
    f1, b1 = shift(own, "ctx", 1, True), shift(own, "ctx", -1, True)
    f2, b2 = shift(f1, "ctx", 1, True), shift(b1, "ctx", -1, True)
    f3, b3 = shift(f2, "ctx", 1, True), shift(b2, "ctx", -1, True)
    f4, b4 = shift(f3[:cut], "ctx", 1, True), shift(b3[cut:], "ctx", -1, True)

    normed_high, kv_high = key_value(
        mp_arr, [(high, a_high, b_high, c_high, d_high)], gain, w_kv, cosine[first:], sine[first:],
        (f1, b1),
    )
    gathered = lax.all_gather(kv_high, "ctx", axis=0, tiled=True)
    (q_high,) = query(normed_high, w_query, cosine[first:], sine[first:], half)
    scalars = (ids, image_counts, image_starts)
    q_all, img_kv, *state = attention(
        0, half, heads, scalars, [q_low, q_high, own, f1, f2, f3, b1, b2, b3, f4, b4], (kv_high,)
    )
    return attention(1, half, heads, scalars, [q_all, img_kv, gathered, *state])


def solution(mesh):
    in_specs = (
        P(("dp", "ctx"), "mp"),
        P(("dp", "ctx"), "mp"),
        P(),
        P(),
        P(),
        P(None, "mp"),
        P(None, "mp"),
        P(None, "mp"),
    )
    out_specs = P(("dp", "ctx"), "mp")
    return jax.shard_map(
        on_device, mesh=mesh, in_specs=in_specs, out_specs=out_specs, check_vma=False
    )
```

```python
import functools
import math

import jax
import jax.numpy as jnp
from jax import lax
from jax.experimental import pallas as pl
from jax.experimental.pallas import tpu as pltpu
from jax.sharding import PartitionSpec as P

HD = 128
IMG_TOK = 64
MAX_IMG = 8
D = 4096
SHARDS = 8
BLOCK = 2048
rope_base = 500000.0
eps = 1e-05
BF16 = jnp.bfloat16
F32 = jnp.float32
VMEM = pltpu.VMEM
SMEM = pltpu.SMEM


def rotary_tables(positions):
    half_size = HD // 2
    exponent = jnp.arange(half_size, dtype=F32) * (2.0 / HD)
    frequency = jnp.exp(-exponent * math.log(rope_base))
    angles = positions.astype(F32)[:, None] * frequency[None, :]
    return jnp.cos(angles), jnp.sin(angles)


def rotate(u, cosine, sine):
    cosine = jnp.concatenate([cosine, cosine], axis=1)
    sine = jnp.concatenate([-sine, sine], axis=1)
    return u * cosine + pltpu.roll(u, HD // 2, 1) * sine


def shift(x, axis, d, wrap):
    pairs = [(i, (i + d) % SHARDS) for i in range(SHARDS) if wrap or 0 <= i + d < SHARDS]
    return lax.ppermute(x, axis, pairs)


def exchange(x, mask):
    return lax.ppermute(x, "mp", [(i, i ^ mask) for i in range(4)])


def first_hop(x):
    return exchange(x, 1), exchange(x, 3)


def second_hop(a, b):
    half = a.shape[0] // 2
    return exchange(a[:half], 3), exchange(b[half:], 1)


def key_value_kernel(shapes, mp_ref, *refs):
    arrays = sum(count for _, count in shapes)
    gain_ref, w_ref, cos_ref, sin_ref = refs[arrays : arrays + 4]
    normed_ref, kv_ref = refs[-2:]
    mp = mp_ref[0]
    base = taken = 0
    for rows, count in shapes:
        own, one, three, *two = refs[taken : taken + count]
        part = rows // len(two)
        for n, two_part in enumerate(two):
            span = pl.ds(n * part, part)
            pieces = [(0, own[span, :]), (1, one[span, :]), (3, three[span, :]), (2, two_part[...])]
            total = jnp.zeros((part, 1), F32)
            for _, piece in pieces:
                wide = piece.astype(F32)
                total = total + jnp.sum(wide * wide, axis=1, keepdims=True)
            scale = lax.rsqrt(total * (1.0 / D) + eps)
            for mask, piece in pieces:
                columns = pl.ds(pl.multiple_of((mp ^ mask) * 1024, 1024), 1024)
                value = piece.astype(F32) * scale * gain_ref[:, columns]
                normed_ref[pl.ds(base + n * part, part), columns] = value.astype(BF16)
        base += rows
        taken += count
    product = jnp.dot(normed_ref[...], w_ref[...], preferred_element_type=F32)
    kv_ref[:, :HD] = rotate(product[:, :HD], cos_ref[...], sin_ref[...]).astype(BF16)
    kv_ref[:, HD:] = product[:, HD:].astype(BF16)


def key_value(mp, groups, gain, w_kv, cosine, sine, after=()):
    shapes = tuple((g[0].shape[0], len(g)) for g in groups)
    rows = sum(size for size, _ in shapes)
    arrays = [a for g in groups for a in g]
    return pl.pallas_call(
        functools.partial(key_value_kernel, shapes),
        out_shape=(
            jax.ShapeDtypeStruct((rows, D), BF16),
            jax.ShapeDtypeStruct((rows, 2 * HD), BF16),
        ),
        in_specs=[pl.BlockSpec(memory_space=SMEM)]
        + [pl.BlockSpec(memory_space=VMEM)] * (len(arrays) + 4)
        + [pl.BlockSpec(memory_space=pl.ANY)] * len(after),
        out_specs=[pl.BlockSpec(memory_space=VMEM)] * 2,
        compiler_params=pltpu.CompilerParams(vmem_limit_bytes=58 * 2**20),
        cost_estimate=pl.CostEstimate(
            flops=0, bytes_accessed=0, transcendentals=0
        ),
        name="key_value",
    )(mp, *arrays, gain, w_kv, cosine, sine, *after)


def images_before(counts_ref, sample):
    total = jnp.int32(0)
    for i in range(SHARDS):
        total = total + jnp.where(i < sample, counts_ref[i], 0)
    return total


def query_kernel(text, x_ref, w_ref, cos_ref, sin_ref, q_ref, *img_ref):
    product = jnp.dot(x_ref[...], w_ref[...], preferred_element_type=F32)
    for h in range(2):
        span = slice(h * HD, (h + 1) * HD)
        turned = rotate(product[:, span], cos_ref[...], sin_ref[...]).astype(BF16)
        q_ref[:, span] = turned[:text]
        if img_ref:
            img_ref[0][:, span] = turned[text:]


def query(normed, w_query, cosine, sine, text):
    rows, columns = normed.shape[0], w_query.shape[1]
    tile = 2 * HD
    img = rows - text
    out_shape = [jax.ShapeDtypeStruct((text, columns), BF16)]
    out_specs = [pl.BlockSpec((text, tile), lambda n: (0, n))]
    if img:
        out_shape.append(jax.ShapeDtypeStruct((img * (columns // tile), tile), BF16))
        out_specs.append(pl.BlockSpec((img, tile), lambda n: (n, 0)))
    return pl.pallas_call(
        functools.partial(query_kernel, text),
        out_shape=out_shape,
        grid=(columns // tile,),
        in_specs=[
            pl.BlockSpec((rows, D), lambda n: (0, 0)),
            pl.BlockSpec((D, tile), lambda n: (0, n)),
            pl.BlockSpec((rows, HD // 2), lambda n: (0, 0)),
            pl.BlockSpec((rows, HD // 2), lambda n: (0, 0)),
        ],
        out_specs=out_specs,
        compiler_params=pltpu.CompilerParams(vmem_limit_bytes=58 * 2**20),
        cost_estimate=pl.CostEstimate(flops=0, bytes_accessed=0, transcendentals=0),
        name="query",
    )(normed, w_query, cosine, sine)


def image_start(counts_ref, starts_ref, sample, residue):
    slot = (residue - images_before(counts_ref, sample)) & (MAX_IMG - 1)
    return jnp.where(slot < counts_ref[sample], starts_ref[sample, slot], -1)


def attention_kernel(tok, heads, ids_ref, counts_ref, starts_ref, *refs):
    half = tok // 2
    img_rows = IMG_TOK * (1 + heads // 2)
    q_low, q_high, early, own, f1, f2, f3, b1, b2, b3, f4, b4, out_ref = refs[:13]
    q_buf, kv_buf, img_buf, s_buf, max_buf, sum_buf, acc_buf, sems = refs[13:]
    step = pl.program_id(0)
    ctx, sample = ids_ref[1], ids_ref[2]
    factor = math.log2(math.e) / math.sqrt(HD)

    @pl.when(step == 0)
    def _():
        copies = [
            pltpu.make_async_copy(q_low, q_buf.at[pl.ds(0, half), :], sems.at[0]),
            pltpu.make_async_copy(q_high, q_buf.at[pl.ds(half, half), :], sems.at[1]),
        ]
        for c in range(SHARDS):
            copies.append(
                pltpu.make_async_copy(
                    early.at[c, pl.ds(0, half), :],
                    kv_buf.at[pl.ds(c * tok, half), :],
                    sems.at[2 + 2 * c],
                )
            )
            copies.append(
                pltpu.make_async_copy(
                    early.at[c, pl.ds(half, img_rows), :], img_buf.at[c], sems.at[3 + 2 * c]
                )
            )
        used = 2 + 2 * SHARDS
        cut = f4.shape[0]
        pieces = [(0, own, 0), (1, f1, 0), (2, f2, 0), (3, f3, 0), (5, b3, 0), (6, b2, 0), (7, b1, 0)]
        for n, (d, piece, offset) in enumerate(pieces + [(4, f4, 0), (4, b4, cut)]):
            shard = (ctx - d) & (SHARDS - 1)
            place = pl.multiple_of(shard * tok + half + offset, cut)
            copies.append(
                pltpu.make_async_copy(
                    piece, kv_buf.at[pl.ds(place, piece.shape[0]), :], sems.at[used + n]
                )
            )
        for copy in copies:
            copy.start()
        for copy in copies:
            copy.wait()
        before = images_before(counts_ref, sample)
        for c in range(SHARDS):
            slot = (c - before) & (MAX_IMG - 1)
            start = jnp.where(slot < counts_ref[sample], starts_ref[sample, slot], -1)

            @pl.when(start >= 0)
            def _():
                rows = pl.ds(pl.multiple_of(start, IMG_TOK), IMG_TOK)
                kv_buf[rows, :] = img_buf[c, :IMG_TOK, :]

            @pl.when((start >= ctx * tok) & (start < ctx * tok + tok))
            def _():
                rows = pl.ds(pl.multiple_of(start - ctx * tok, IMG_TOK), IMG_TOK)
                for n in range(heads // 2):
                    q_buf[rows, n * 2 * HD : (n + 1) * 2 * HD] = img_buf[
                        c, IMG_TOK * (n + 1) : IMG_TOK * (n + 2), :
                    ]

    def phase(do_score, do_mix):
        slot = lax.rem(step, 2)
        other = 1 - slot

        def block(j):
            keys = pl.ds(pl.multiple_of(j * BLOCK, BLOCK), BLOCK)
            if do_score:
                columns = pl.ds(pl.multiple_of(step * HD, HD), HD)
                s = lax.dot_general(
                    q_buf[:, columns],
                    kv_buf[keys, :HD],
                    (((1,), (1,)), ((), ())),
                    preferred_element_type=F32,
                )
                row = lax.broadcasted_iota(jnp.int32, (tok, HD), 0) + (ctx * tok - j * BLOCK)
                column = lax.broadcasted_iota(jnp.int32, (tok, HD), 1)
                top = max_buf[slot]
                for g in range(BLOCK // HD):
                    seen = s[:, g * HD : (g + 1) * HD]
                    seen = jnp.where(column + g * HD <= row, seen, -1e30)
                    s_buf[slot, j, :, g * HD : (g + 1) * HD] = seen
                    top = jnp.maximum(top, seen)
                max_buf[slot] = top
            if do_mix:
                shared = max_buf[other]
                total = sum_buf[...]
                weights = []
                for g in range(BLOCK // HD):
                    w = jnp.exp2(s_buf[other, j, :, g * HD : (g + 1) * HD] * factor - shared)
                    total = total + w
                    weights.append(w.astype(BF16))
                sum_buf[...] = total
                acc_buf[...] += jnp.dot(
                    jnp.concatenate(weights, axis=1), kv_buf[keys, HD:], preferred_element_type=F32
                )

        if do_score:
            max_buf[slot] = jnp.full((tok, HD), -1e30, F32)
        if do_mix:
            sum_buf[...] = jnp.zeros((tok, HD), F32)
            acc_buf[...] = jnp.zeros((tok, HD), F32)
        pl.loop(0, (ctx * tok + tok + BLOCK - 1) // BLOCK)(block)
        if do_score:
            top = jnp.max(max_buf[slot], axis=1, keepdims=True) * factor
            max_buf[slot] = jnp.broadcast_to(top, (tok, HD))
        if do_mix:
            total = jnp.sum(sum_buf[...], axis=1, keepdims=True)
            out_ref[...] = (acc_buf[...] / total).astype(BF16)

    pl.when(step == 0)(lambda: phase(True, False))
    pl.when((step > 0) & (step < heads))(lambda: phase(True, True))
    pl.when(step == heads)(lambda: phase(False, True))


def attention(tok, heads, scalars, arrays):
    img_rows = IMG_TOK * (1 + heads // 2)
    return pl.pallas_call(
        functools.partial(attention_kernel, tok, heads),
        out_shape=jax.ShapeDtypeStruct((tok, heads * HD), BF16),
        grid=(heads + 1,),
        in_specs=[pl.BlockSpec(memory_space=SMEM)] * 3
        + [pl.BlockSpec(memory_space=pl.ANY)] * len(arrays),
        out_specs=pl.BlockSpec((tok, HD), lambda t: (0, jnp.maximum(t - 1, 0))),
        scratch_shapes=[
            pltpu.VMEM((tok, heads * HD), BF16),
            pltpu.VMEM((SHARDS * tok, 2 * HD), BF16),
            pltpu.VMEM((SHARDS, img_rows, 2 * HD), BF16),
            pltpu.VMEM((2, SHARDS * tok // BLOCK, tok, BLOCK), F32),
            pltpu.VMEM((2, tok, HD), F32),
            pltpu.VMEM((tok, HD), F32),
            pltpu.VMEM((tok, HD), F32),
            pltpu.SemaphoreType.DMA((2 + 2 * SHARDS + 9,)),
        ],
        compiler_params=pltpu.CompilerParams(vmem_limit_bytes=52 * 2**20),
        cost_estimate=pl.CostEstimate(
            flops=4 * tok * heads * SHARDS * tok * HD,
            bytes_accessed=8 * 2**20,
            transcendentals=tok * heads * SHARDS * tok,
        ),
        name="attention",
    )(*scalars, *arrays)


def on_device(
    text_rows, visual_rows, image_counts, image_starts, norm_gain, w_query, w_key, w_value
):
    ctx = lax.axis_index("ctx").astype(jnp.int32)
    sample = lax.axis_index("dp").astype(jnp.int32)
    mp = lax.axis_index("mp").astype(jnp.int32)
    tok = text_rows.shape[0]
    half = tok // 2
    heads = w_query.shape[1] // HD
    ids = jnp.stack([mp, ctx, sample])

    w_kv = jnp.concatenate([w_key, w_value], axis=1)
    gain = norm_gain[None, :]
    every = jnp.arange(SHARDS, dtype=jnp.int32)

    def source(who):
        before = jnp.sum(jnp.where(every < who, image_counts, 0))
        slot = (ctx - before) & (MAX_IMG - 1)
        owner = jnp.minimum((before + slot) >> 3, SHARDS - 1)
        return slot, (owner ^ who) & 1, jnp.clip((who >> 1) - (owner >> 1), 0, 3)

    def choose(which, choices):
        chosen = choices[0]
        for n, choice in enumerate(choices[1:], 1):
            chosen = jnp.where(which == n, choice, chosen)
        return chosen

    my_slot, my_across, my_distance = source(sample)
    _, _, its_distance = source(sample ^ 1)
    low, high = text_rows[:half], text_rows[half:]
    routed = [visual_rows] + [shift(visual_rows, "dp", 2 * d, False) for d in (1, 2, 3)]
    a_low, b_low = first_hop(low)
    for_other = choose(its_distance, routed)
    from_other = lax.ppermute(for_other, "dp", [(i, i ^ 1) for i in range(SHARDS)])
    image = choose(jnp.where(my_across == 1, 4, my_distance), routed + [from_other])
    a_img, b_img, c_img = (exchange(image, mask) for mask in (1, 3, 2))
    a_high, b_high = first_hop(high)
    c_low, d_low = second_hop(a_low, b_low)
    c_high, d_high = second_hop(a_high, b_high)

    mine = (every[:, None] == sample) & (every[None, :] == my_slot)
    my_start = jnp.sum(jnp.where(mine, image_starts, 0))
    rows = jnp.arange(tok + IMG_TOK, dtype=jnp.int32)
    positions = jnp.where(
        rows < half,
        ctx * tok + rows,
        jnp.where(rows < half + IMG_TOK, my_start + rows - half, ctx * tok + rows - IMG_TOK),
    )
    cosine, sine = rotary_tables(positions)
    first = half + IMG_TOK
    mp_arr = ids[:1]

    normed, kv = key_value(
        mp_arr,
        [(low, a_low, b_low, c_low, d_low), (image, a_img, b_img, c_img)],
        gain, w_kv, cosine[:first], sine[:first], (a_high, b_high),
    )
    q_low, q_img = query(normed, w_query, cosine[:first], sine[:first], half)
    early = lax.all_gather(jnp.concatenate([kv, q_img], axis=0), "ctx", axis=0)
    normed_high, own = key_value(
        mp_arr, [(high, a_high, b_high, c_high, d_high)], gain, w_kv, cosine[first:], sine[first:],
        (q_img,),
    )
    cut = half // 2
    f1, b1 = shift(own, "ctx", 1, True), shift(own, "ctx", -1, True)
    f2, b2 = shift(f1, "ctx", 1, True), shift(b1, "ctx", -1, True)
    f3, b3 = shift(f2, "ctx", 1, True), shift(b2, "ctx", -1, True)
    f4, b4 = shift(f3[:cut], "ctx", 1, True), shift(b3[cut:], "ctx", -1, True)
    (q_high,) = query(normed_high, w_query, cosine[first:], sine[first:], half)
    return attention(
        tok, heads, (ids, image_counts, image_starts),
        [q_low, q_high, early, own, f1, f2, f3, b1, b2, b3, f4, b4],
    )


def solution(mesh):
    in_specs = (
        P(("dp", "ctx"), "mp"),
        P(("dp", "ctx"), "mp"),
        P(),
        P(),
        P(),
        P(None, "mp"),
        P(None, "mp"),
        P(None, "mp"),
    )
    out_specs = P(("dp", "ctx"), "mp")
    return jax.shard_map(
        on_device, mesh=mesh, in_specs=in_specs, out_specs=out_specs, check_vma=False
    )
```

```python
import functools
import math

import jax
import jax.numpy as jnp
from jax import lax
from jax.experimental import pallas as pl
from jax.experimental.pallas import tpu as pltpu
from jax.sharding import PartitionSpec as P

HD = 128
IMG_TOK = 64
MAX_IMG = 8
D = 4096
SHARDS = 8
BLOCK = 2048
rope_base = 500000.0
eps = 1e-05
BF16 = jnp.bfloat16
F32 = jnp.float32
VMEM = pltpu.VMEM
SMEM = pltpu.SMEM


def rotary_tables(positions):
    half_size = HD // 2
    exponent = jnp.arange(half_size, dtype=F32) * (2.0 / HD)
    frequency = jnp.exp(-exponent * math.log(rope_base))
    angles = positions.astype(F32)[:, None] * frequency[None, :]
    return jnp.cos(angles), jnp.sin(angles)


def rotate(u, cosine, sine):
    cosine = jnp.concatenate([cosine, cosine], axis=1)
    sine = jnp.concatenate([-sine, sine], axis=1)
    return u * cosine + pltpu.roll(u, HD // 2, 1) * sine


def shift(x, axis, d, wrap):
    pairs = [(i, (i + d) % SHARDS) for i in range(SHARDS) if wrap or 0 <= i + d < SHARDS]
    return lax.ppermute(x, axis, pairs)


def exchange(x, mask):
    return lax.ppermute(x, "mp", [(i, i ^ mask) for i in range(4)])


def first_hop(x):
    return exchange(x, 1), exchange(x, 3)


def second_hop(a, b):
    half = a.shape[0] // 2
    return exchange(a[:half], 3), exchange(b[half:], 1)


def normalise(mp, gain_ref, pieces, out_ref, rows):
    total = 0.0
    for piece in pieces:
        wide = piece.astype(F32)
        total = total + jnp.sum(wide * wide, axis=1, keepdims=True)
    scale = lax.rsqrt(total * (1.0 / D) + eps)
    for mask, piece in zip((0, 1, 3, 2), pieces):
        columns = pl.ds(pl.multiple_of((mp ^ mask) * 1024, 1024), 1024)
        value = piece.astype(F32) * scale * gain_ref[:, columns]
        out_ref[rows, columns] = value.astype(BF16)


def write_key_value(x, w_ref, cos, sin, out_ref, rows):
    product = jnp.dot(x, w_ref[...], preferred_element_type=F32)
    out_ref[rows, :HD] = rotate(product[:, :HD], cos, sin).astype(BF16)
    out_ref[rows, HD:] = product[:, HD:].astype(BF16)


def early_kernel(ids_ref, own, one, three, x3, x1, img, img_two, gain, w_kv, w_q, cos, sin, *refs):
    normed_ref, out_ref, img_normed = refs[-3:]
    text, img_rows = own.shape[0], img.shape[0]
    part = text // 2
    step = pl.program_id(0)
    mp = ids_ref[0]

    @pl.when(step == 0)
    def _():
        for n, two in enumerate((x3, x1)):
            span = pl.ds(n * part, part)
            pieces = [own[span, :], one[span, :], three[span, :], two[:part, :]]
            normalise(mp, gain, pieces, normed_ref, span)
        pieces = [img[...], x1[part:, :], x3[part:, :], img_two[...]]
        normalise(mp, gain, pieces, img_normed, slice(0, img_rows))
        rows = slice(0, text)
        write_key_value(normed_ref[...], w_kv, cos[rows, :], sin[rows, :], out_ref, rows)
        rows = slice(text, text + img_rows)
        write_key_value(img_normed[...], w_kv, cos[rows, :], sin[rows, :], out_ref, rows)

    product = jnp.dot(img_normed[...], w_q[...], preferred_element_type=F32)
    start = text + img_rows + step * img_rows
    rows = pl.ds(pl.multiple_of(start, IMG_TOK), img_rows)
    for h in range(2):
        span = slice(h * HD, (h + 1) * HD)
        turned = rotate(product[:, span], cos[text:, :], sin[text:, :])
        out_ref[rows, span] = turned.astype(BF16)


def early(ids, arrays, gain, w_kv, w_query, cosine, sine, after):
    text, img_rows, tile = arrays[0].shape[0], arrays[5].shape[0], 2 * HD
    steps = w_query.shape[1] // tile
    whole = pl.BlockSpec(memory_space=VMEM)
    return pl.pallas_call(
        early_kernel,
        out_shape=[
            jax.ShapeDtypeStruct((text, D), BF16),
            jax.ShapeDtypeStruct((text + (1 + steps) * img_rows, tile), BF16),
        ],
        grid=(steps,),
        in_specs=[pl.BlockSpec(memory_space=SMEM)]
        + [whole] * (len(arrays) + 2)
        + [pl.BlockSpec((D, tile), lambda n: (0, n))]
        + [whole] * 2
        + [pl.BlockSpec(memory_space=pl.ANY)] * len(after),
        out_specs=[
            pl.BlockSpec((text, D), lambda n: (0, 0)),
            pl.BlockSpec((text + (1 + steps) * img_rows, tile), lambda n: (0, 0)),
        ],
        scratch_shapes=[pltpu.VMEM((img_rows, D), BF16)],
        compiler_params=pltpu.CompilerParams(vmem_limit_bytes=58 * 2**20),
        cost_estimate=pl.CostEstimate(flops=0, bytes_accessed=0, transcendentals=0),
        name="early",
    )(ids, *arrays, gain, w_kv, w_query, cosine, sine, *after)


def late_kernel(ids_ref, own, one, three, two_lo, two_hi, gain, w_kv, cos, sin, normed_ref, out_ref):
    part = own.shape[0] // 2
    for n, two in enumerate((two_lo, two_hi)):
        span = pl.ds(n * part, part)
        pieces = [own[span, :], one[span, :], three[span, :], two[...]]
        normalise(ids_ref[0], gain, pieces, normed_ref, span)
    write_key_value(
        normed_ref[...], w_kv, cos[...], sin[...], out_ref, slice(0, own.shape[0])
    )


def late(ids, arrays, gain, w_kv, cosine, sine):
    rows = arrays[0].shape[0]
    return pl.pallas_call(
        late_kernel,
        out_shape=[
            jax.ShapeDtypeStruct((rows, D), BF16),
            jax.ShapeDtypeStruct((rows, 2 * HD), BF16),
        ],
        in_specs=[pl.BlockSpec(memory_space=SMEM)]
        + [pl.BlockSpec(memory_space=VMEM)] * (len(arrays) + 4),
        out_specs=[pl.BlockSpec(memory_space=VMEM)] * 2,
        compiler_params=pltpu.CompilerParams(vmem_limit_bytes=58 * 2**20),
        cost_estimate=pl.CostEstimate(flops=0, bytes_accessed=0, transcendentals=0),
        name="late",
    )(ids, *arrays, gain, w_kv, cosine, sine)


def query_kernel(low_ref, high_ref, w_ref, cos_low, sin_low, cos_high, sin_high, q_ref):
    half = low_ref.shape[0]
    parts = ((low_ref, cos_low, sin_low), (high_ref, cos_high, sin_high))
    for n, (x_ref, cos, sin) in enumerate(parts):
        product = jnp.dot(x_ref[...], w_ref[...], preferred_element_type=F32)
        for h in range(2):
            span = slice(h * HD, (h + 1) * HD)
            turned = rotate(product[:, span], cos[:half, :], sin[:half, :])
            q_ref[n * half : (n + 1) * half, span] = turned.astype(BF16)


def query(low, high, w_query, tables):
    half, columns, tile = low.shape[0], w_query.shape[1], 2 * HD
    whole = pl.BlockSpec(memory_space=VMEM)
    return pl.pallas_call(
        query_kernel,
        out_shape=jax.ShapeDtypeStruct((2 * half, columns), BF16),
        grid=(columns // tile,),
        in_specs=[whole] * 2 + [pl.BlockSpec((D, tile), lambda n: (0, n))] + [whole] * 4,
        out_specs=pl.BlockSpec((2 * half, tile), lambda n: (0, n)),
        compiler_params=pltpu.CompilerParams(vmem_limit_bytes=58 * 2**20),
        cost_estimate=pl.CostEstimate(flops=0, bytes_accessed=0, transcendentals=0),
        name="query",
    )(low, high, w_query, *tables)


def images_before(counts_ref, sample):
    total = jnp.int32(0)
    for i in range(SHARDS):
        total = total + jnp.where(i < sample, counts_ref[i], 0)
    return total


def attention_kernel(tok, heads, ids_ref, counts_ref, starts_ref, *refs):
    half = tok // 2
    img_rows = IMG_TOK * (1 + heads // 2)
    q_ref, own_e, own_l, f1, f2, f3, f4, f5, b1, b2, b3, b4, b5, out_ref = refs[:14]
    q_buf, kv_buf, img_buf, s_buf, max_buf, sum_buf, acc_buf, sems = refs[14:]
    step = pl.program_id(0)
    ctx, sample = ids_ref[1], ids_ref[2]
    factor = math.log2(math.e) / math.sqrt(HD)

    @pl.when(step == 0)
    def _():
        rows_e = own_e.shape[0]
        cut = rows_e // 2
        quarter = half // 2
        early_parts = [
            (0, own_e, 0, 0, rows_e),
            (1, f1, 0, 0, rows_e),
            (2, f2, 0, 0, rows_e),
            (3, f3, 0, 0, rows_e),
            (4, b4, half, 0, cut),
            (4, f4, 0, cut, cut),
            (5, b3, half, 0, rows_e),
            (6, b2, half, 0, rows_e),
            (7, b1, 0, 0, rows_e),
        ]
        late_parts = [
            (0, own_l, 0, 0, half),
            (1, f2, rows_e, 0, half),
            (2, f3, rows_e, 0, half),
            (3, f4, cut, 0, half),
            (4, f5, 0, 0, quarter),
            (4, b5, 0, quarter, quarter),
            (5, b4, 0, 0, half),
            (6, b3, 0, 0, half),
            (7, b2, 0, 0, half),
        ]
        moves = [(q_ref, q_buf)]
        for d, array, base, first, count in early_parts:
            shard = (ctx - d) & (SHARDS - 1)
            if first < half:
                place = pl.ds(pl.multiple_of(shard * tok, tok), half)
                moves.append((array.at[pl.ds(base, half), :], kv_buf.at[place, :]))
            skip = max(half - first, 0)
            place = pl.ds(first + skip - half, count - skip)
            moves.append(
                (array.at[pl.ds(base + skip, count - skip), :], img_buf.at[shard, place, :])
            )
        for d, array, base, first, count in late_parts:
            shard = (ctx - d) & (SHARDS - 1)
            place = pl.ds(pl.multiple_of(shard * tok + half + first, quarter), count)
            moves.append((array.at[pl.ds(base, count), :], kv_buf.at[place, :]))
        copies = [
            pltpu.make_async_copy(source, target, sems.at[n])
            for n, (source, target) in enumerate(moves)
        ]
        for copy in copies:
            copy.start()
        for copy in copies:
            copy.wait()
        before = images_before(counts_ref, sample)
        for c in range(SHARDS):
            slot = (c - before) & (MAX_IMG - 1)
            start = jnp.where(slot < counts_ref[sample], starts_ref[sample, slot], -1)

            @pl.when(start >= 0)
            def _():
                rows = pl.ds(pl.multiple_of(start, IMG_TOK), IMG_TOK)
                kv_buf[rows, :] = img_buf[c, :IMG_TOK, :]

            @pl.when((start >= ctx * tok) & (start < ctx * tok + tok))
            def _():
                rows = pl.ds(pl.multiple_of(start - ctx * tok, IMG_TOK), IMG_TOK)
                for n in range(heads // 2):
                    q_buf[rows, n * 2 * HD : (n + 1) * 2 * HD] = img_buf[
                        c, IMG_TOK * (n + 1) : IMG_TOK * (n + 2), :
                    ]

    def phase(do_score, do_mix):
        slot = lax.rem(step, 2)
        other = 1 - slot

        def block(j):
            keys = pl.ds(pl.multiple_of(j * BLOCK, BLOCK), BLOCK)
            if do_score:
                columns = pl.ds(pl.multiple_of(step * HD, HD), HD)
                s = lax.dot_general(
                    q_buf[:, columns],
                    kv_buf[keys, :HD],
                    (((1,), (1,)), ((), ())),
                    preferred_element_type=F32,
                )
                row = lax.broadcasted_iota(jnp.int32, (tok, HD), 0) + (ctx * tok - j * BLOCK)
                column = lax.broadcasted_iota(jnp.int32, (tok, HD), 1)
                top = max_buf[slot]
                for g in range(BLOCK // HD):
                    seen = s[:, g * HD : (g + 1) * HD]
                    seen = jnp.where(column + g * HD <= row, seen, -1e30)
                    s_buf[slot, j, :, g * HD : (g + 1) * HD] = seen
                    top = jnp.maximum(top, seen)
                max_buf[slot] = top
            if do_mix:
                shared = max_buf[other]
                total = sum_buf[...]
                weights = []
                for g in range(BLOCK // HD):
                    w = jnp.exp2(s_buf[other, j, :, g * HD : (g + 1) * HD] * factor - shared)
                    total = total + w
                    weights.append(w.astype(BF16))
                sum_buf[...] = total
                acc_buf[...] += jnp.dot(
                    jnp.concatenate(weights, axis=1), kv_buf[keys, HD:], preferred_element_type=F32
                )

        if do_score:
            max_buf[slot] = jnp.full((tok, HD), -1e30, F32)
        if do_mix:
            sum_buf[...] = jnp.zeros((tok, HD), F32)
            acc_buf[...] = jnp.zeros((tok, HD), F32)
        pl.loop(0, (ctx * tok + tok + BLOCK - 1) // BLOCK)(block)
        if do_score:
            top = jnp.max(max_buf[slot], axis=1, keepdims=True) * factor
            max_buf[slot] = jnp.broadcast_to(top, (tok, HD))
        if do_mix:
            total = jnp.sum(sum_buf[...], axis=1, keepdims=True)
            out_ref[...] = (acc_buf[...] / total).astype(BF16)

    pl.when(step == 0)(lambda: phase(True, False))
    pl.when((step > 0) & (step < heads))(lambda: phase(True, True))
    pl.when(step == heads)(lambda: phase(False, True))


def attention(tok, heads, scalars, arrays):
    img_rows = IMG_TOK * (1 + heads // 2)
    return pl.pallas_call(
        functools.partial(attention_kernel, tok, heads),
        out_shape=jax.ShapeDtypeStruct((tok, heads * HD), BF16),
        grid=(heads + 1,),
        in_specs=[pl.BlockSpec(memory_space=SMEM)] * 3
        + [pl.BlockSpec(memory_space=pl.ANY)] * len(arrays),
        out_specs=pl.BlockSpec((tok, HD), lambda t: (0, jnp.maximum(t - 1, 0))),
        scratch_shapes=[
            pltpu.VMEM((tok, heads * HD), BF16),
            pltpu.VMEM((SHARDS * tok, 2 * HD), BF16),
            pltpu.VMEM((SHARDS, img_rows, 2 * HD), BF16),
            pltpu.VMEM((2, SHARDS * tok // BLOCK, tok, BLOCK), F32),
            pltpu.VMEM((2, tok, HD), F32),
            pltpu.VMEM((tok, HD), F32),
            pltpu.VMEM((tok, HD), F32),
            pltpu.SemaphoreType.DMA((32,)),
        ],
        compiler_params=pltpu.CompilerParams(vmem_limit_bytes=52 * 2**20),
        cost_estimate=pl.CostEstimate(
            flops=4 * tok * heads * SHARDS * tok * HD,
            bytes_accessed=8 * 2**20,
            transcendentals=tok * heads * SHARDS * tok,
        ),
        name="attention",
    )(*scalars, *arrays)


def on_device(
    text_rows, visual_rows, image_counts, image_starts, norm_gain, w_query, w_key, w_value
):
    ctx = lax.axis_index("ctx").astype(jnp.int32)
    sample = lax.axis_index("dp").astype(jnp.int32)
    mp = lax.axis_index("mp").astype(jnp.int32)
    tok = text_rows.shape[0]
    half = tok // 2
    heads = w_query.shape[1] // HD
    ids = jnp.stack([mp, ctx, sample])

    w_kv = jnp.concatenate([w_key, w_value], axis=1)
    gain = norm_gain[None, :]
    every = jnp.arange(SHARDS, dtype=jnp.int32)

    def source(who):
        before = jnp.sum(jnp.where(every < who, image_counts, 0))
        slot = (ctx - before) & (MAX_IMG - 1)
        owner = jnp.minimum((before + slot) >> 3, SHARDS - 1)
        return slot, (owner ^ who) & 1, jnp.clip((who >> 1) - (owner >> 1), 0, 3)

    def choose(which, choices):
        chosen = choices[0]
        for n, choice in enumerate(choices[1:], 1):
            chosen = jnp.where(which == n, choice, chosen)
        return chosen

    my_slot, my_across, my_distance = source(sample)
    _, _, its_distance = source(sample ^ 1)
    low, high = text_rows[:half], text_rows[half:]
    routed = [visual_rows] + [shift(visual_rows, "dp", 2 * d, False) for d in (1, 2, 3)]
    a_low, b_low = first_hop(low)
    a_high, b_high = first_hop(high)
    for_other = choose(its_distance, routed)
    from_other = lax.ppermute(for_other, "dp", [(i, i ^ 1) for i in range(SHARDS)])
    image = choose(jnp.where(my_across == 1, 4, my_distance), routed + [from_other])
    x3 = exchange(jnp.concatenate([a_low[: half // 2], image], axis=0), 3)
    x1 = exchange(jnp.concatenate([b_low[half // 2 :], image], axis=0), 1)
    img_two = exchange(image, 2)
    c_high, d_high = second_hop(a_high, b_high)

    mine = (every[:, None] == sample) & (every[None, :] == my_slot)
    my_start = jnp.sum(jnp.where(mine, image_starts, 0))
    rows = jnp.arange(tok + IMG_TOK, dtype=jnp.int32)
    positions = jnp.where(
        rows < half,
        ctx * tok + rows,
        jnp.where(rows < half + IMG_TOK, my_start + rows - half, ctx * tok + rows - IMG_TOK),
    )
    cosine, sine = rotary_tables(positions)
    first = half + IMG_TOK
    tables_e = (cosine[:first], sine[:first])
    tables_l = (cosine[first:], sine[first:])
    normed_low, own_e = early(
        ids, [low, a_low, b_low, x3, x1, image, img_two], gain, w_kv, w_query, *tables_e,
        (a_high, b_high),
    )
    normed_high, own_l = late(
        ids, [high, a_high, b_high, c_high, d_high], gain, w_kv, *tables_l
    )
    q_all = query(normed_low, normed_high, w_query, tables_e + tables_l)

    cut = own_e.shape[0] // 2
    quarter = half // 2
    f1, b1 = shift(own_e, "ctx", 1, True), shift(own_e, "ctx", -1, True)
    f2 = shift(jnp.concatenate([f1, own_l], axis=0), "ctx", 1, True)
    b2 = shift(jnp.concatenate([own_l, b1], axis=0), "ctx", -1, True)
    f3, b3 = shift(f2, "ctx", 1, True), shift(b2, "ctx", -1, True)
    f4, b4 = shift(f3[cut:], "ctx", 1, True), shift(b3[: half + cut], "ctx", -1, True)
    f5 = shift(f4[cut : cut + quarter], "ctx", 1, True)
    b5 = shift(b4[quarter:half], "ctx", -1, True)
    return attention(
        tok, heads, (ids, image_counts, image_starts),
        [q_all, own_e, own_l, f1, f2, f3, f4, f5, b1, b2, b3, b4, b5],
    )


def solution(mesh):
    in_specs = (
        P(("dp", "ctx"), "mp"),
        P(("dp", "ctx"), "mp"),
        P(),
        P(),
        P(),
        P(None, "mp"),
        P(None, "mp"),
        P(None, "mp"),
    )
    out_specs = P(("dp", "ctx"), "mp")
    return jax.shard_map(
        on_device, mesh=mesh, in_specs=in_specs, out_specs=out_specs, check_vma=False
    )
```

```python
import functools
import math

import jax
import jax.numpy as jnp
from jax import lax
from jax.experimental import pallas as pl
from jax.experimental.pallas import tpu as pltpu
from jax.sharding import PartitionSpec as P

HD = 128
IMG_TOK = 64
MAX_IMG = 8
D = 4096
SHARDS = 8
BLOCK = 2048
rope_base = 500000.0
eps = 1e-05
BF16 = jnp.bfloat16
F32 = jnp.float32
VMEM = pltpu.VMEM
SMEM = pltpu.SMEM


def rotary_tables(positions):
    half_size = HD // 2
    exponent = jnp.arange(half_size, dtype=F32) * (2.0 / HD)
    frequency = jnp.exp(-exponent * math.log(rope_base))
    angles = positions.astype(F32)[:, None] * frequency[None, :]
    return jnp.cos(angles), jnp.sin(angles)


def rotate(u, cosine, sine):
    cosine = jnp.concatenate([cosine, cosine], axis=1)
    sine = jnp.concatenate([-sine, sine], axis=1)
    return u * cosine + pltpu.roll(u, HD // 2, 1) * sine


def shift(x, axis, d, wrap):
    pairs = [(i, (i + d) % SHARDS) for i in range(SHARDS) if wrap or 0 <= i + d < SHARDS]
    return lax.ppermute(x, axis, pairs)


def exchange(x, mask):
    return lax.ppermute(x, "mp", [(i, i ^ mask) for i in range(4)])


def first_hop(x):
    return exchange(x, 1), exchange(x, 3)


def second_hop(a, b):
    half = a.shape[0] // 2
    return exchange(a[:half], 3), exchange(b[half:], 1)


def normalise(mp, gain_ref, pieces, out_ref, rows):
    total = 0.0
    for piece in pieces:
        wide = piece.astype(F32)
        total = total + jnp.sum(wide * wide, axis=1, keepdims=True)
    scale = lax.rsqrt(total * (1.0 / D) + eps)
    for mask, piece in zip((0, 1, 3, 2), pieces):
        columns = pl.ds(pl.multiple_of((mp ^ mask) * 1024, 1024), 1024)
        value = piece.astype(F32) * scale * gain_ref[:, columns]
        out_ref[rows, columns] = value.astype(BF16)


def write_key_value(x, w_ref, cos, sin, out_ref, rows):
    product = jnp.dot(x, w_ref[...], preferred_element_type=F32)
    out_ref[rows, :HD] = rotate(product[:, :HD], cos, sin).astype(BF16)
    out_ref[rows, HD:] = product[:, HD:].astype(BF16)


def image_kernel(ids_ref, own, one, three, two, gain, w_kv, w_q, cos, sin, *refs):
    out_ref, normed = refs[-2:]
    rows = own.shape[0]
    step = pl.program_id(0)

    @pl.when(step == 0)
    def _():
        pieces = [own[...], one[...], three[...], two[...]]
        normalise(ids_ref[0], gain, pieces, normed, slice(0, rows))
        write_key_value(normed[...], w_kv, cos[...], sin[...], out_ref, slice(0, rows))

    product = jnp.dot(normed[...], w_q[...], preferred_element_type=F32)
    span = pl.ds(pl.multiple_of((step + 1) * rows, IMG_TOK), rows)
    for h in range(2):
        columns = slice(h * HD, (h + 1) * HD)
        out_ref[span, columns] = rotate(product[:, columns], cos[...], sin[...]).astype(BF16)


def project_image(ids, arrays, gain, w_kv, w_query, tables, after):
    rows, tile = arrays[0].shape[0], 2 * HD
    steps = w_query.shape[1] // tile
    whole = pl.BlockSpec(memory_space=VMEM)
    return pl.pallas_call(
        image_kernel,
        out_shape=jax.ShapeDtypeStruct(((1 + steps) * rows, tile), BF16),
        grid=(steps,),
        in_specs=[pl.BlockSpec(memory_space=SMEM)]
        + [whole] * (len(arrays) + 2)
        + [pl.BlockSpec((D, tile), lambda n: (0, n))]
        + [whole] * 2
        + [pl.BlockSpec(memory_space=pl.ANY)] * len(after),
        out_specs=pl.BlockSpec(((1 + steps) * rows, tile), lambda n: (0, 0)),
        scratch_shapes=[pltpu.VMEM((rows, D), BF16)],
        compiler_params=pltpu.CompilerParams(vmem_limit_bytes=58 * 2**20),
        cost_estimate=pl.CostEstimate(flops=8 * 10**9, bytes_accessed=10 * 2**20, transcendentals=0),
        name="project_image",
    )(ids, *arrays, gain, w_kv, w_query, *tables, *after)


def text_kernel(ids_ref, own, one, three, two_lo, two_hi, gain, w_kv, cos, sin, *refs):
    normed_ref, out_ref = refs[-2:]
    rows = own.shape[0]
    low = pl.program_id(0) < pl.num_programs(0) // 2
    two = jnp.where(low, two_lo[...], two_hi[...])
    pieces = [own[...], one[...], three[...], two]
    normalise(ids_ref[0], gain, pieces, normed_ref, slice(0, rows))
    write_key_value(normed_ref[...], w_kv, cos[...], sin[...], out_ref, slice(0, rows))


def project_text(ids, arrays, gain, w_kv, tables, after):
    rows, tile = arrays[0].shape[0], 128
    steps = rows // tile
    whole = pl.BlockSpec(memory_space=VMEM)
    block = pl.BlockSpec((tile, D // 4), lambda r: (r, 0))
    table = pl.BlockSpec((tile, HD // 2), lambda r: (r, 0))
    return pl.pallas_call(
        text_kernel,
        out_shape=[
            jax.ShapeDtypeStruct((rows, D), BF16),
            jax.ShapeDtypeStruct((rows, 2 * HD), BF16),
        ],
        grid=(steps,),
        in_specs=[pl.BlockSpec(memory_space=SMEM)]
        + [block] * 3
        + [
            pl.BlockSpec((tile, D // 4), lambda r: (jnp.minimum(r, steps // 2 - 1), 0)),
            pl.BlockSpec((tile, D // 4), lambda r: (jnp.maximum(r - steps // 2, 0), 0)),
        ]
        + [whole] * 2
        + [table] * 2
        + [pl.BlockSpec(memory_space=pl.ANY)] * len(after),
        out_specs=[
            pl.BlockSpec((tile, D), lambda r: (r, 0)),
            pl.BlockSpec((tile, 2 * HD), lambda r: (r, 0)),
        ],
        compiler_params=pltpu.CompilerParams(vmem_limit_bytes=58 * 2**20),
        cost_estimate=pl.CostEstimate(flops=0, bytes_accessed=0, transcendentals=0),
        name="project_text",
    )(ids, *arrays, gain, w_kv, *tables, *after)


def query_kernel(x_ref, w_ref, cos, sin, q_ref):
    product = jnp.dot(x_ref[...], w_ref[...], preferred_element_type=F32)
    for h in range(w_ref.shape[1] // HD):
        span = slice(h * HD, (h + 1) * HD)
        q_ref[:, span] = rotate(product[:, span], cos[...], sin[...]).astype(BF16)


def query(normed, w_query, tables):
    rows, columns, tile = normed.shape[0], w_query.shape[1], 2 * HD
    whole = pl.BlockSpec(memory_space=VMEM)
    return pl.pallas_call(
        query_kernel,
        out_shape=jax.ShapeDtypeStruct((rows, columns), BF16),
        grid=(columns // tile,),
        in_specs=[whole, pl.BlockSpec((D, tile), lambda n: (0, n))] + [whole] * 2,
        out_specs=pl.BlockSpec((rows, tile), lambda n: (0, n)),
        compiler_params=pltpu.CompilerParams(vmem_limit_bytes=58 * 2**20),
        cost_estimate=pl.CostEstimate(flops=8 * 10**9, bytes_accessed=10 * 2**20, transcendentals=0),
        name="query",
    )(normed, w_query, *tables)


def images_before(counts_ref, sample):
    total = jnp.int32(0)
    for i in range(SHARDS):
        total = total + jnp.where(i < sample, counts_ref[i], 0)
    return total


def attention_kernel(tok, heads, ids_ref, counts_ref, starts_ref, *refs):
    q_ref, own_e, own_l, f1, f2, f3, f4, f5, b1, b2, b3, b4, b5, out_ref = refs[:14]
    q_buf, kv_buf, img_buf, s_buf, max_buf, sum_buf, acc_buf, sems = refs[14:]
    step = pl.program_id(0)
    ctx, sample = ids_ref[1], ids_ref[2]
    factor = math.log2(math.e) / math.sqrt(HD)

    @pl.when(step == 0)
    def _():
        rows_e, rows_l = own_e.shape[0], own_l.shape[0]
        cut, part = rows_e // 2, rows_l // 2
        moves = [(q_ref, q_buf)]
        for d, array, base, first, count in (
            (0, own_e, 0, 0, rows_e),
            (1, f1, 0, 0, rows_e),
            (2, f2, 0, 0, rows_e),
            (3, f3, 0, 0, rows_e),
            (4, f4, 0, cut, cut),
            (4, b4, rows_l, 0, cut),
            (5, b3, rows_l, 0, rows_e),
            (6, b2, rows_l, 0, rows_e),
            (7, b1, 0, 0, rows_e),
        ):
            shard = (ctx - d) & (SHARDS - 1)
            moves.append(
                (array.at[pl.ds(base, count), :], img_buf.at[shard, pl.ds(first, count), :])
            )
        for d, array, base, first, count in (
            (0, own_l, 0, 0, rows_l),
            (1, f2, rows_e, 0, rows_l),
            (2, f3, rows_e, 0, rows_l),
            (3, f4, cut, 0, rows_l),
            (4, f5, 0, 0, part),
            (4, b5, 0, part, part),
            (5, b4, 0, 0, rows_l),
            (6, b3, 0, 0, rows_l),
            (7, b2, 0, 0, rows_l),
        ):
            shard = (ctx - d) & (SHARDS - 1)
            place = pl.ds(pl.multiple_of(shard * tok + first, part), count)
            moves.append((array.at[pl.ds(base, count), :], kv_buf.at[place, :]))
        copies = [
            pltpu.make_async_copy(source, target, sems.at[n])
            for n, (source, target) in enumerate(moves)
        ]
        for copy in copies:
            copy.start()
        for copy in copies:
            copy.wait()
        before = images_before(counts_ref, sample)
        for c in range(SHARDS):
            slot = (c - before) & (MAX_IMG - 1)
            start = jnp.where(slot < counts_ref[sample], starts_ref[sample, slot], -1)

            @pl.when(start >= 0)
            def _():
                rows = pl.ds(pl.multiple_of(start, IMG_TOK), IMG_TOK)
                kv_buf[rows, :] = img_buf[c, :IMG_TOK, :]

            @pl.when((start >= ctx * tok) & (start < ctx * tok + tok))
            def _():
                rows = pl.ds(pl.multiple_of(start - ctx * tok, IMG_TOK), IMG_TOK)
                for n in range(heads // 2):
                    q_buf[rows, n * 2 * HD : (n + 1) * 2 * HD] = img_buf[
                        c, IMG_TOK * (n + 1) : IMG_TOK * (n + 2), :
                    ]

    def phase(do_score, do_mix):
        slot = lax.rem(step, 2)
        other = 1 - slot

        def block(j):
            keys = pl.ds(pl.multiple_of(j * BLOCK, BLOCK), BLOCK)
            if do_score:
                columns = pl.ds(pl.multiple_of(step * HD, HD), HD)
                s = lax.dot_general(
                    q_buf[:, columns],
                    kv_buf[keys, :HD],
                    (((1,), (1,)), ((), ())),
                    preferred_element_type=F32,
                )
                row = lax.broadcasted_iota(jnp.int32, (tok, HD), 0) + (ctx * tok - j * BLOCK)
                column = lax.broadcasted_iota(jnp.int32, (tok, HD), 1)
                top = max_buf[slot]
                for g in range(BLOCK // HD):
                    seen = s[:, g * HD : (g + 1) * HD]
                    seen = jnp.where(column + g * HD <= row, seen, -1e30)
                    s_buf[slot, j, :, g * HD : (g + 1) * HD] = seen
                    top = jnp.maximum(top, seen)
                max_buf[slot] = top
            if do_mix:
                shared = max_buf[other]
                total = sum_buf[...]
                weights = []
                for g in range(BLOCK // HD):
                    w = jnp.exp2(s_buf[other, j, :, g * HD : (g + 1) * HD] * factor - shared)
                    total = total + w
                    weights.append(w.astype(BF16))
                sum_buf[...] = total
                acc_buf[...] += jnp.dot(
                    jnp.concatenate(weights, axis=1), kv_buf[keys, HD:], preferred_element_type=F32
                )

        if do_score:
            max_buf[slot] = jnp.full((tok, HD), -1e30, F32)
        if do_mix:
            sum_buf[...] = jnp.zeros((tok, HD), F32)
            acc_buf[...] = jnp.zeros((tok, HD), F32)
        pl.loop(0, (ctx * tok + tok + BLOCK - 1) // BLOCK)(block)
        if do_score:
            top = jnp.max(max_buf[slot], axis=1, keepdims=True) * factor
            max_buf[slot] = jnp.broadcast_to(top, (tok, HD))
        if do_mix:
            total = jnp.sum(sum_buf[...], axis=1, keepdims=True)
            out_ref[...] = (acc_buf[...] / total).astype(BF16)

    pl.when(step == 0)(lambda: phase(True, False))
    pl.when((step > 0) & (step < heads))(lambda: phase(True, True))
    pl.when(step == heads)(lambda: phase(False, True))


def attention(tok, heads, scalars, arrays):
    img_rows = IMG_TOK * (1 + heads // 2)
    return pl.pallas_call(
        functools.partial(attention_kernel, tok, heads),
        out_shape=jax.ShapeDtypeStruct((tok, heads * HD), BF16),
        grid=(heads + 1,),
        in_specs=[pl.BlockSpec(memory_space=SMEM)] * 3
        + [pl.BlockSpec(memory_space=pl.ANY)] * len(arrays),
        out_specs=pl.BlockSpec((tok, HD), lambda t: (0, jnp.maximum(t - 1, 0))),
        scratch_shapes=[
            pltpu.VMEM((tok, heads * HD), BF16),
            pltpu.VMEM((SHARDS * tok, 2 * HD), BF16),
            pltpu.VMEM((SHARDS, img_rows, 2 * HD), BF16),
            pltpu.VMEM((2, SHARDS * tok // BLOCK, tok, BLOCK), F32),
            pltpu.VMEM((2, tok, HD), F32),
            pltpu.VMEM((tok, HD), F32),
            pltpu.VMEM((tok, HD), F32),
            pltpu.SemaphoreType.DMA((32,)),
        ],
        compiler_params=pltpu.CompilerParams(vmem_limit_bytes=52 * 2**20),
        cost_estimate=pl.CostEstimate(
            flops=4 * tok * heads * SHARDS * tok * HD,
            bytes_accessed=8 * 2**20,
            transcendentals=tok * heads * SHARDS * tok,
        ),
        name="attention",
    )(*scalars, *arrays)


def on_device(
    text_rows, visual_rows, image_counts, image_starts, norm_gain, w_query, w_key, w_value
):
    ctx = lax.axis_index("ctx").astype(jnp.int32)
    sample = lax.axis_index("dp").astype(jnp.int32)
    mp = lax.axis_index("mp").astype(jnp.int32)
    tok = text_rows.shape[0]
    heads = w_query.shape[1] // HD
    ids = jnp.stack([mp, ctx, sample])

    w_kv = jnp.concatenate([w_key, w_value], axis=1)
    gain = norm_gain[None, :]
    every = jnp.arange(SHARDS, dtype=jnp.int32)

    def source(who):
        before = jnp.sum(jnp.where(every < who, image_counts, 0))
        slot = (ctx - before) & (MAX_IMG - 1)
        owner = jnp.minimum((before + slot) >> 3, SHARDS - 1)
        return slot, (owner ^ who) & 1, jnp.clip((who >> 1) - (owner >> 1), 0, 3)

    def choose(which, choices):
        chosen = choices[0]
        for n, choice in enumerate(choices[1:], 1):
            chosen = jnp.where(which == n, choice, chosen)
        return chosen

    my_slot, my_across, my_distance = source(sample)
    _, _, its_distance = source(sample ^ 1)
    one, three = first_hop(text_rows)
    routed = [visual_rows] + [shift(visual_rows, "dp", 2 * d, False) for d in (1, 2, 3)]
    for_other = choose(its_distance, routed)
    from_other = lax.ppermute(for_other, "dp", [(i, i ^ 1) for i in range(SHARDS)])
    image = choose(jnp.where(my_across == 1, 4, my_distance), routed + [from_other])
    image_parts = [image] + [exchange(image, mask) for mask in (1, 3, 2)]
    two_lo, two_hi = second_hop(one, three)

    mine = (every[:, None] == sample) & (every[None, :] == my_slot)
    my_start = jnp.sum(jnp.where(mine, image_starts, 0))
    text_tables = rotary_tables(ctx * tok + jnp.arange(tok, dtype=jnp.int32))
    image_tables = rotary_tables(my_start + jnp.arange(IMG_TOK, dtype=jnp.int32))
    own_e = project_image(ids, image_parts, gain, w_kv, w_query, image_tables, (one, three))
    normed, own_l = project_text(
        ids, [text_rows, one, three, two_lo, two_hi], gain, w_kv, text_tables, (own_e,)
    )
    q_all = query(normed, w_query, text_tables)

    cut, part = own_e.shape[0] // 2, tok // 2
    f1, b1 = shift(own_e, "ctx", 1, True), shift(own_e, "ctx", -1, True)
    f2 = shift(jnp.concatenate([f1, own_l], axis=0), "ctx", 1, True)
    b2 = shift(jnp.concatenate([own_l, b1], axis=0), "ctx", -1, True)
    f3, b3 = shift(f2, "ctx", 1, True), shift(b2, "ctx", -1, True)
    f4, b4 = shift(f3[cut:], "ctx", 1, True), shift(b3[: tok + cut], "ctx", -1, True)
    f5 = shift(f4[cut : cut + part], "ctx", 1, True)
    b5 = shift(b4[part:tok], "ctx", -1, True)
    return attention(
        tok, heads, (ids, image_counts, image_starts),
        [q_all, own_e, own_l, f1, f2, f3, f4, f5, b1, b2, b3, b4, b5],
    )


def solution(mesh):
    in_specs = (
        P(("dp", "ctx"), "mp"),
        P(("dp", "ctx"), "mp"),
        P(),
        P(),
        P(),
        P(None, "mp"),
        P(None, "mp"),
        P(None, "mp"),
    )
    out_specs = P(("dp", "ctx"), "mp")
    return jax.shard_map(
        on_device, mesh=mesh, in_specs=in_specs, out_specs=out_specs, check_vma=False
    )
```

```python
import functools
import math

import jax
import jax.numpy as jnp
from jax import lax
from jax.experimental import pallas as pl
from jax.experimental.pallas import tpu as pltpu
from jax.sharding import PartitionSpec as P

HD = 128
IMG_TOK = 64
MAX_IMG = 8
D = 4096
SHARDS = 8
BLOCK = 2048
rope_base = 500000.0
eps = 1e-05
BF16 = jnp.bfloat16
F32 = jnp.float32
VMEM = pltpu.VMEM
SMEM = pltpu.SMEM


def rotary_tables(positions):
    half_size = HD // 2
    exponent = jnp.arange(half_size, dtype=F32) * (2.0 / HD)
    frequency = jnp.exp(-exponent * math.log(rope_base))
    angles = positions.astype(F32)[:, None] * frequency[None, :]
    return jnp.cos(angles), jnp.sin(angles)


def rotate(u, cosine, sine):
    cosine = jnp.concatenate([cosine, cosine], axis=1)
    sine = jnp.concatenate([-sine, sine], axis=1)
    return u * cosine + pltpu.roll(u, HD // 2, 1) * sine


def shift(x, axis, d, wrap):
    pairs = [(i, (i + d) % SHARDS) for i in range(SHARDS) if wrap or 0 <= i + d < SHARDS]
    return lax.ppermute(x, axis, pairs)


def exchange(x, mask):
    return lax.ppermute(x, "mp", [(i, i ^ mask) for i in range(4)])


def first_hop(x):
    return exchange(x, 1), exchange(x, 3)


def second_hop(a, b):
    half = a.shape[0] // 2
    return exchange(a[:half], 3), exchange(b[half:], 1)


def normalise(mp, gain_ref, pieces, out_ref, rows):
    total = 0.0
    for piece in pieces:
        wide = piece.astype(F32)
        total = total + jnp.sum(wide * wide, axis=1, keepdims=True)
    scale = lax.rsqrt(total * (1.0 / D) + eps)
    for mask, piece in zip((0, 1, 3, 2), pieces):
        columns = pl.ds(pl.multiple_of((mp ^ mask) * 1024, 1024), 1024)
        value = piece.astype(F32) * scale * gain_ref[:, columns]
        out_ref[rows, columns] = value.astype(BF16)


def write_key_value(x, w_ref, cos, sin, out_ref, rows):
    product = jnp.dot(x, w_ref[...], preferred_element_type=F32)
    out_ref[rows, :HD] = rotate(product[:, :HD], cos, sin).astype(BF16)
    out_ref[rows, HD:] = product[:, HD:].astype(BF16)


def image_kernel(ids_ref, own, one, three, two, gain, w_kv, w_q, cos, sin, *refs):
    out_ref, normed = refs[-2:]
    rows = own.shape[0]
    step = pl.program_id(0)

    @pl.when(step == 0)
    def _():
        pieces = [own[...], one[...], three[...], two[...]]
        normalise(ids_ref[0], gain, pieces, normed, slice(0, rows))
        write_key_value(normed[...], w_kv, cos[...], sin[...], out_ref, slice(0, rows))

    product = jnp.dot(normed[...], w_q[...], preferred_element_type=F32)
    span = pl.ds(pl.multiple_of((step + 1) * rows, IMG_TOK), rows)
    for h in range(2):
        columns = slice(h * HD, (h + 1) * HD)
        out_ref[span, columns] = rotate(product[:, columns], cos[...], sin[...]).astype(BF16)


def project_image(ids, arrays, gain, w_kv, w_query, tables, after):
    rows, tile = arrays[0].shape[0], 2 * HD
    steps = w_query.shape[1] // tile
    whole = pl.BlockSpec(memory_space=VMEM)
    return pl.pallas_call(
        image_kernel,
        out_shape=jax.ShapeDtypeStruct(((1 + steps) * rows, tile), BF16),
        grid=(steps,),
        in_specs=[pl.BlockSpec(memory_space=SMEM)]
        + [whole] * (len(arrays) + 2)
        + [pl.BlockSpec((D, tile), lambda n: (0, n))]
        + [whole] * 2
        + [pl.BlockSpec(memory_space=pl.ANY)] * len(after),
        out_specs=pl.BlockSpec(((1 + steps) * rows, tile), lambda n: (0, 0)),
        scratch_shapes=[pltpu.VMEM((rows, D), BF16)],
        compiler_params=pltpu.CompilerParams(vmem_limit_bytes=58 * 2**20),
        cost_estimate=pl.CostEstimate(flops=8 * 10**9, bytes_accessed=10 * 2**20, transcendentals=0),
        name="project_image",
    )(ids, *arrays, gain, w_kv, w_query, *tables, *after)


def text_kernel(ids_ref, own, one_lo, one_hi, three_lo, three_hi, *refs):
    twos = refs[:4]
    gain, w_kv, cos, sin = refs[4:8]
    normed_ref, out_ref = refs[-2:]
    rows = own.shape[0]
    for n in range(4):
        @pl.when(pl.program_id(0) == n)
        def _():
            one, three = ((one_lo, three_lo), (one_hi, three_hi))[n // 2]
            pieces = [own[...], one[...], three[...], twos[n][...]]
            normalise(ids_ref[0], gain, pieces, normed_ref, slice(0, rows))

    write_key_value(normed_ref[...], w_kv, cos[...], sin[...], out_ref, slice(0, rows))


def project_text(ids, arrays, gain, w_kv, tables, after):
    rows = arrays[0].shape[0]
    steps = 4
    tile = rows // steps
    whole = pl.BlockSpec(memory_space=VMEM)
    low = pl.BlockSpec((tile, D // 4), lambda r: (jnp.minimum(r, 1), 0))
    high = pl.BlockSpec((tile, D // 4), lambda r: (jnp.maximum(r - 2, 0), 0))
    table = pl.BlockSpec((tile, HD // 2), lambda r: (r, 0))
    return pl.pallas_call(
        text_kernel,
        out_shape=[
            jax.ShapeDtypeStruct((rows, D), BF16),
            jax.ShapeDtypeStruct((rows, 2 * HD), BF16),
        ],
        grid=(steps,),
        in_specs=[pl.BlockSpec(memory_space=SMEM)]
        + [pl.BlockSpec((tile, D // 4), lambda r: (r, 0)), low, high, low, high]
        + [whole] * 6
        + [table] * 2
        + [pl.BlockSpec(memory_space=pl.ANY)] * len(after),
        out_specs=[
            pl.BlockSpec((tile, D), lambda r: (r, 0)),
            pl.BlockSpec((tile, 2 * HD), lambda r: (r, 0)),
        ],
        compiler_params=pltpu.CompilerParams(vmem_limit_bytes=58 * 2**20),
        cost_estimate=pl.CostEstimate(flops=0, bytes_accessed=0, transcendentals=0),
        name="project_text",
    )(ids, *arrays, gain, w_kv, *tables, *after)


def cut_kernel(starts, a_ref, b_ref, _, a_out, b_out):
    for start, ref, out in zip(starts, (a_ref, b_ref), (a_out, b_out)):
        out[...] = ref[start : start + out.shape[0], :]


def cut_payloads(a, b, starts, rows, after):
    whole = pl.BlockSpec(memory_space=VMEM)
    return pl.pallas_call(
        functools.partial(cut_kernel, starts),
        out_shape=[jax.ShapeDtypeStruct((rows, a.shape[1]), a.dtype)] * 2,
        in_specs=[whole] * 2 + [pl.BlockSpec(memory_space=pl.ANY)],
        out_specs=[whole] * 2,
        cost_estimate=pl.CostEstimate(flops=0, bytes_accessed=0, transcendentals=0),
        name="cut_payloads",
    )(a, b, after)


def query_kernel(x_ref, w_ref, cos, sin, q_ref):
    product = jnp.dot(x_ref[...], w_ref[...], preferred_element_type=F32)
    for h in range(w_ref.shape[1] // HD):
        span = slice(h * HD, (h + 1) * HD)
        q_ref[:, span] = rotate(product[:, span], cos[...], sin[...]).astype(BF16)


def query(normed, w_query, tables):
    rows, columns, tile = normed.shape[0], w_query.shape[1], 2 * HD
    whole = pl.BlockSpec(memory_space=VMEM)
    return pl.pallas_call(
        query_kernel,
        out_shape=jax.ShapeDtypeStruct((rows, columns), BF16),
        grid=(columns // tile,),
        in_specs=[whole, pl.BlockSpec((D, tile), lambda n: (0, n))] + [whole] * 2,
        out_specs=pl.BlockSpec((rows, tile), lambda n: (0, n)),
        compiler_params=pltpu.CompilerParams(vmem_limit_bytes=58 * 2**20),
        cost_estimate=pl.CostEstimate(flops=8 * 10**9, bytes_accessed=10 * 2**20, transcendentals=0),
        name="query",
    )(normed, w_query, *tables)


def images_before(counts_ref, sample):
    total = jnp.int32(0)
    for i in range(SHARDS):
        total = total + jnp.where(i < sample, counts_ref[i], 0)
    return total


def attention_kernel(tok, heads, ids_ref, counts_ref, starts_ref, *refs):
    q_ref, own_e, own_l, f1, f2, f3, f4, f5, b1, b2, b3, b4, b5, out_ref = refs[:14]
    q_buf, kv_buf, img_buf, s_buf, max_buf, sum_buf, acc_buf, sems = refs[14:]
    ctx, sample = ids_ref[1], ids_ref[2]
    factor = math.log2(math.e) / math.sqrt(HD)

    rows_e, rows_l = own_e.shape[0], own_l.shape[0]
    cut, part = rows_e // 2, rows_l // 2
    moves = [(q_ref, q_buf)]
    for d, array, base, first, count in (
        (0, own_e, 0, 0, rows_e),
        (1, f1, 0, 0, rows_e),
        (2, f2, 0, 0, rows_e),
        (3, f3, 0, 0, rows_e),
        (4, f4, 0, cut, cut),
        (4, b4, rows_l, 0, cut),
        (5, b3, rows_l, 0, rows_e),
        (6, b2, rows_l, 0, rows_e),
        (7, b1, 0, 0, rows_e),
    ):
        shard = (ctx - d) & (SHARDS - 1)
        moves.append(
            (array.at[pl.ds(base, count), :], img_buf.at[shard, pl.ds(first, count), :])
        )
    for d, array, base, first, count in (
        (0, own_l, 0, 0, rows_l),
        (1, f2, rows_e, 0, rows_l),
        (2, f3, rows_e, 0, rows_l),
        (3, f4, cut, 0, rows_l),
        (4, f5, 0, 0, part),
        (4, b5, 0, part, part),
        (5, b4, 0, 0, rows_l),
        (6, b3, 0, 0, rows_l),
        (7, b2, 0, 0, rows_l),
    ):
        shard = (ctx - d) & (SHARDS - 1)
        place = pl.ds(pl.multiple_of(shard * tok + first, part), count)
        moves.append((array.at[pl.ds(base, count), :], kv_buf.at[place, :]))
    copies = [
        pltpu.make_async_copy(source, target, sems.at[n])
        for n, (source, target) in enumerate(moves)
    ]
    for copy in copies:
        copy.start()
    for copy in copies:
        copy.wait()
    before = images_before(counts_ref, sample)
    for c in range(SHARDS):
        slot = (c - before) & (MAX_IMG - 1)
        start = jnp.where(slot < counts_ref[sample], starts_ref[sample, slot], -1)

        @pl.when(start >= 0)
        def _():
            rows = pl.ds(pl.multiple_of(start, IMG_TOK), IMG_TOK)
            kv_buf[rows, :] = img_buf[c, :IMG_TOK, :]

        @pl.when((start >= ctx * tok) & (start < ctx * tok + tok))
        def _():
            rows = pl.ds(pl.multiple_of(start - ctx * tok, IMG_TOK), IMG_TOK)
            for n in range(heads // 2):
                q_buf[rows, n * 2 * HD : (n + 1) * 2 * HD] = img_buf[
                    c, IMG_TOK * (n + 1) : IMG_TOK * (n + 2), :
                ]

    def phase(step, do_score, do_mix):
        slot = lax.rem(step, 2)
        other = 1 - slot

        def block(j):
            keys = pl.ds(pl.multiple_of(j * BLOCK, BLOCK), BLOCK)
            if do_score:
                columns = pl.ds(pl.multiple_of(step * HD, HD), HD)
                s = lax.dot_general(
                    q_buf[:, columns],
                    kv_buf[keys, :HD],
                    (((1,), (1,)), ((), ())),
                    preferred_element_type=F32,
                )
                row = lax.broadcasted_iota(jnp.int32, (tok, HD), 0) + (ctx * tok - j * BLOCK)
                column = lax.broadcasted_iota(jnp.int32, (tok, HD), 1)
                top = max_buf[slot]
                for g in range(BLOCK // HD):
                    seen = s[:, g * HD : (g + 1) * HD]
                    seen = jnp.where(column + g * HD <= row, seen, -1e30)
                    s_buf[slot, j, :, g * HD : (g + 1) * HD] = seen
                    top = jnp.maximum(top, seen)
                max_buf[slot] = top
            if do_mix:
                shared = max_buf[other]
                total = sum_buf[...]
                weights = []
                for g in range(BLOCK // HD):
                    w = jnp.exp2(s_buf[other, j, :, g * HD : (g + 1) * HD] * factor - shared)
                    total = total + w
                    weights.append(w.astype(BF16))
                sum_buf[...] = total
                acc_buf[...] += jnp.dot(
                    jnp.concatenate(weights, axis=1), kv_buf[keys, HD:], preferred_element_type=F32
                )

        if do_score:
            max_buf[slot] = jnp.full((tok, HD), -1e30, F32)
        if do_mix:
            sum_buf[...] = jnp.zeros((tok, HD), F32)
            acc_buf[...] = jnp.zeros((tok, HD), F32)
        pl.loop(0, (ctx * tok + tok + BLOCK - 1) // BLOCK)(block)
        if do_score:
            top = jnp.max(max_buf[slot], axis=1, keepdims=True) * factor
            max_buf[slot] = jnp.broadcast_to(top, (tok, HD))
        if do_mix:
            total = jnp.sum(sum_buf[...], axis=1, keepdims=True)
            columns = pl.ds(pl.multiple_of((step - 1) * HD, HD), HD)
            out_ref[:, columns] = (acc_buf[...] / total).astype(BF16)

    phase(jnp.int32(0), True, False)
    pl.loop(1, heads)(lambda step: phase(step, True, True))
    phase(jnp.int32(heads), False, True)


def attention(tok, heads, scalars, arrays):
    img_rows = IMG_TOK * (1 + heads // 2)
    return pl.pallas_call(
        functools.partial(attention_kernel, tok, heads),
        out_shape=jax.ShapeDtypeStruct((tok, heads * HD), BF16),
        in_specs=[pl.BlockSpec(memory_space=SMEM)] * 3
        + [pl.BlockSpec(memory_space=pl.ANY)] * len(arrays),
        out_specs=pl.BlockSpec(memory_space=VMEM),
        scratch_shapes=[
            pltpu.VMEM((tok, heads * HD), BF16),
            pltpu.VMEM((SHARDS * tok, 2 * HD), BF16),
            pltpu.VMEM((SHARDS, img_rows, 2 * HD), BF16),
            pltpu.VMEM((2, SHARDS * tok // BLOCK, tok, BLOCK), F32),
            pltpu.VMEM((2, tok, HD), F32),
            pltpu.VMEM((tok, HD), F32),
            pltpu.VMEM((tok, HD), F32),
            pltpu.SemaphoreType.DMA((32,)),
        ],
        compiler_params=pltpu.CompilerParams(vmem_limit_bytes=52 * 2**20),
        cost_estimate=pl.CostEstimate(
            flops=4 * tok * heads * SHARDS * tok * HD,
            bytes_accessed=8 * 2**20,
            transcendentals=tok * heads * SHARDS * tok,
        ),
        name="attention",
    )(*scalars, *arrays)


def on_device(
    text_rows, visual_rows, image_counts, image_starts, norm_gain, w_query, w_key, w_value
):
    ctx = lax.axis_index("ctx").astype(jnp.int32)
    sample = lax.axis_index("dp").astype(jnp.int32)
    mp = lax.axis_index("mp").astype(jnp.int32)
    tok = text_rows.shape[0]
    heads = w_query.shape[1] // HD
    ids = jnp.stack([mp, ctx, sample])

    w_kv = jnp.concatenate([w_key, w_value], axis=1)
    gain = norm_gain[None, :]
    every = jnp.arange(SHARDS, dtype=jnp.int32)

    def source(who):
        before = jnp.sum(jnp.where(every < who, image_counts, 0))
        slot = (ctx - before) & (MAX_IMG - 1)
        owner = jnp.minimum((before + slot) >> 3, SHARDS - 1)
        return slot, (owner ^ who) & 1, jnp.clip((who >> 1) - (owner >> 1), 0, 3)

    def choose(which, choices):
        chosen = choices[0]
        for n, choice in enumerate(choices[1:], 1):
            chosen = jnp.where(which == n, choice, chosen)
        return chosen

    my_slot, my_across, my_distance = source(sample)
    _, _, its_distance = source(sample ^ 1)
    half = tok // 2
    low, high = text_rows[:half], text_rows[half:]
    one_lo, three_lo = first_hop(low)
    routed = [visual_rows] + [shift(visual_rows, "dp", 2 * d, False) for d in (1, 2, 3)]
    one_hi, three_hi = first_hop(high)
    for_other = choose(its_distance, routed)
    from_other = lax.ppermute(for_other, "dp", [(i, i ^ 1) for i in range(SHARDS)])
    image = choose(jnp.where(my_across == 1, 4, my_distance), routed + [from_other])
    twos_lo = second_hop(one_lo, three_lo)
    image_parts = [image] + [exchange(image, mask) for mask in (1, 3, 2)]
    twos_hi = second_hop(one_hi, three_hi)

    mine = (every[:, None] == sample) & (every[None, :] == my_slot)
    my_start = jnp.sum(jnp.where(mine, image_starts, 0))
    text_tables = rotary_tables(ctx * tok + jnp.arange(tok, dtype=jnp.int32))
    image_tables = rotary_tables(my_start + jnp.arange(IMG_TOK, dtype=jnp.int32))
    own_e = project_image(
        ids, image_parts, gain, w_kv, w_query, image_tables, (one_hi, three_hi)
    )
    normed, own_l = project_text(
        ids, [text_rows, one_lo, one_hi, three_lo, three_hi, *twos_lo, *twos_hi],
        gain, w_kv, text_tables, (own_e,)
    )
    q_all = query(normed, w_query, text_tables)

    cut, part = own_e.shape[0] // 2, tok // 2
    f1, b1 = shift(own_e, "ctx", 1, True), shift(own_e, "ctx", -1, True)
    f2 = shift(jnp.concatenate([f1, own_l], axis=0), "ctx", 1, True)
    b2 = shift(jnp.concatenate([own_l, b1], axis=0), "ctx", -1, True)
    f3, b3 = shift(f2, "ctx", 1, True), shift(b2, "ctx", -1, True)
    onward = cut_payloads(f3, b3, (cut, 0), tok + cut, q_all)
    f4, b4 = shift(onward[0], "ctx", 1, True), shift(onward[1], "ctx", -1, True)
    f5 = shift(f4[cut : cut + part], "ctx", 1, True)
    b5 = shift(b4[part:tok], "ctx", -1, True)
    return attention(
        tok, heads, (ids, image_counts, image_starts),
        [q_all, own_e, own_l, f1, f2, f3, f4, f5, b1, b2, b3, b4, b5],
    )


def solution(mesh):
    in_specs = (
        P(("dp", "ctx"), "mp"),
        P(("dp", "ctx"), "mp"),
        P(),
        P(),
        P(),
        P(None, "mp"),
        P(None, "mp"),
        P(None, "mp"),
    )
    out_specs = P(("dp", "ctx"), "mp")
    return jax.shard_map(
        on_device, mesh=mesh, in_specs=in_specs, out_specs=out_specs, check_vma=False
    )
```

```python
import functools
import math

import jax
import jax.numpy as jnp
from jax import lax
from jax.experimental import pallas as pl
from jax.experimental.pallas import tpu as pltpu
from jax.sharding import PartitionSpec as P

HD = 128
IMG_TOK = 64
MAX_IMG = 8
D = 4096
SHARDS = 8
BLOCK = 2048
rope_base = 500000.0
eps = 1e-05
BF16 = jnp.bfloat16
F32 = jnp.float32
VMEM = pltpu.VMEM
SMEM = pltpu.SMEM


def rotary_tables(positions):
    half_size = HD // 2
    exponent = jnp.arange(half_size, dtype=F32) * (2.0 / HD)
    frequency = jnp.exp(-exponent * math.log(rope_base))
    angles = positions.astype(F32)[:, None] * frequency[None, :]
    return jnp.cos(angles), jnp.sin(angles)


def rotate(u, cosine, sine):
    cosine = jnp.concatenate([cosine, cosine], axis=1)
    sine = jnp.concatenate([-sine, sine], axis=1)
    return u * cosine + pltpu.roll(u, HD // 2, 1) * sine


def shift(x, axis, d, wrap):
    pairs = [(i, (i + d) % SHARDS) for i in range(SHARDS) if wrap or 0 <= i + d < SHARDS]
    return lax.ppermute(x, axis, pairs)


def exchange(x, mask):
    return lax.ppermute(x, "mp", [(i, i ^ mask) for i in range(4)])


def first_hop(x):
    return exchange(x, 1), exchange(x, 3)


def normalise(mp, gain_ref, pieces, out_ref, rows):
    total = 0.0
    for piece in pieces:
        wide = piece.astype(F32)
        total = total + jnp.sum(wide * wide, axis=1, keepdims=True)
    scale = lax.rsqrt(total * (1.0 / D) + eps)
    for mask, piece in zip((0, 1, 3, 2), pieces):
        columns = pl.ds(pl.multiple_of((mp ^ mask) * 1024, 1024), 1024)
        value = piece.astype(F32) * scale * gain_ref[:, columns]
        out_ref[rows, columns] = value.astype(BF16)


def write_key_value(x, w_ref, cos, sin, out_ref, rows):
    product = jnp.dot(x, w_ref[...], preferred_element_type=F32)
    out_ref[rows, :HD] = rotate(product[:, :HD], cos, sin).astype(BF16)
    out_ref[rows, HD:] = product[:, HD:].astype(BF16)


def image_kernel(ids_ref, own, one, three, two, gain, w_kv, w_q, cos, sin, *refs):
    out_ref, normed = refs[-2:]
    rows = own.shape[0]
    step = pl.program_id(0)

    @pl.when(step == 0)
    def _():
        pieces = [own[...], one[...], three[...], two[...]]
        normalise(ids_ref[0], gain, pieces, normed, slice(0, rows))
        write_key_value(normed[...], w_kv, cos[...], sin[...], out_ref, slice(0, rows))

    product = jnp.dot(normed[...], w_q[...], preferred_element_type=F32)
    span = pl.ds(pl.multiple_of((step + 1) * rows, IMG_TOK), rows)
    for h in range(2):
        columns = slice(h * HD, (h + 1) * HD)
        out_ref[span, columns] = rotate(product[:, columns], cos[...], sin[...]).astype(BF16)


def project_image(ids, arrays, gain, w_kv, w_query, tables, after):
    rows, tile = arrays[0].shape[0], 2 * HD
    steps = w_query.shape[1] // tile
    whole = pl.BlockSpec(memory_space=VMEM)
    return pl.pallas_call(
        image_kernel,
        out_shape=jax.ShapeDtypeStruct(((1 + steps) * rows, tile), BF16),
        grid=(steps,),
        in_specs=[pl.BlockSpec(memory_space=SMEM)]
        + [whole] * (len(arrays) + 2)
        + [pl.BlockSpec((D, tile), lambda n: (0, n))]
        + [whole] * 2
        + [pl.BlockSpec(memory_space=pl.ANY)] * len(after),
        out_specs=pl.BlockSpec(((1 + steps) * rows, tile), lambda n: (0, 0)),
        scratch_shapes=[pltpu.VMEM((rows, D), BF16)],
        compiler_params=pltpu.CompilerParams(vmem_limit_bytes=58 * 2**20),
        cost_estimate=pl.CostEstimate(flops=8 * 10**9, bytes_accessed=10 * 2**20, transcendentals=0),
        name="project_image",
    )(ids, *arrays, gain, w_kv, w_query, *tables, *after)


def text_kernel(ids_ref, own, one_a, one_b, three_a, three_b, two_a, two_b, two_c, *refs):
    gain, w_kv, cos, sin = refs[:4]
    normed_ref, out_ref = refs[-2:]
    rows = own.shape[0]
    for n, others in enumerate(
        ((one_a, three_a, two_a), (one_b, three_b, two_b), (one_b, three_b, two_c))
    ):
        @pl.when(jnp.minimum(pl.program_id(0), 2) == n)
        def _():
            pieces = [own[...]] + [other[...] for other in others]
            normalise(ids_ref[0], gain, pieces, normed_ref, slice(0, rows))

    write_key_value(normed_ref[...], w_kv, cos[...], sin[...], out_ref, slice(0, rows))


def project_text(ids, arrays, gain, w_kv, tables, after):
    rows = arrays[0].shape[0]
    steps = 4
    tile = rows // steps

    def block(skipped):
        return pl.BlockSpec((tile, D // 4), lambda r: (jnp.maximum(r - skipped, 0), 0))

    whole = pl.BlockSpec(memory_space=VMEM)
    only = pl.BlockSpec((tile, D // 4), lambda r: (0, 0))
    table = pl.BlockSpec((tile, HD // 2), lambda r: (r, 0))
    return pl.pallas_call(
        text_kernel,
        out_shape=[
            jax.ShapeDtypeStruct((rows, D), BF16),
            jax.ShapeDtypeStruct((rows, 2 * HD), BF16),
        ],
        grid=(steps,),
        in_specs=[pl.BlockSpec(memory_space=SMEM)]
        + [block(0), only, block(1), only, block(1), only, only, block(2)]
        + [whole] * 2
        + [table] * 2
        + [pl.BlockSpec(memory_space=pl.ANY)] * len(after),
        out_specs=[
            pl.BlockSpec((tile, D), lambda r: (r, 0)),
            pl.BlockSpec((tile, 2 * HD), lambda r: (r, 0)),
        ],
        compiler_params=pltpu.CompilerParams(vmem_limit_bytes=58 * 2**20),
        cost_estimate=pl.CostEstimate(flops=0, bytes_accessed=0, transcendentals=0),
        name="project_text",
    )(ids, *arrays, gain, w_kv, *tables, *after)


def query_kernel(x_ref, w_ref, cos, sin, q_ref):
    product = jnp.dot(x_ref[...], w_ref[...], preferred_element_type=F32)
    for h in range(w_ref.shape[1] // HD):
        span = slice(h * HD, (h + 1) * HD)
        q_ref[:, span] = rotate(product[:, span], cos[...], sin[...]).astype(BF16)


def query(normed, w_query, tables, part, parts):
    rows, tile = normed.shape[0], 2 * HD
    columns = w_query.shape[1] // parts
    first = part * (columns // tile)
    whole = pl.BlockSpec(memory_space=VMEM)
    return pl.pallas_call(
        query_kernel,
        out_shape=jax.ShapeDtypeStruct((rows, columns), BF16),
        grid=(columns // tile,),
        in_specs=[whole, pl.BlockSpec((D, tile), lambda n: (0, first + n))] + [whole] * 2,
        out_specs=pl.BlockSpec((rows, tile), lambda n: (0, n)),
        compiler_params=pltpu.CompilerParams(vmem_limit_bytes=58 * 2**20),
        cost_estimate=pl.CostEstimate(flops=3 * 10**9, bytes_accessed=2**20, transcendentals=0),
        name="query",
    )(normed, w_query, *tables)


def images_before(counts_ref, sample):
    total = jnp.int32(0)
    for i in range(SHARDS):
        total = total + jnp.where(i < sample, counts_ref[i], 0)
    return total


def attention_kernel(tok, heads, ids_ref, counts_ref, starts_ref, *refs):
    q_one, q_two, own_e, own_l, f1, f2, f3, f4, f5, b1, b2, b3, b4, b5, out_ref = refs[:15]
    q_buf, kv_buf, img_buf, s_buf, max_buf, sum_buf, acc_buf, sems = refs[15:]
    ctx, sample = ids_ref[1], ids_ref[2]
    factor = math.log2(math.e) / math.sqrt(HD)

    rows_e, rows_l = own_e.shape[0], own_l.shape[0]
    cut, part = rows_e // 2, rows_l // 2
    middle = heads * HD // 2
    moves = [(q_one, q_buf.at[:, :middle]), (q_two, q_buf.at[:, middle:])]
    for d, array, base, first, count in (
        (0, own_e, 0, 0, rows_e),
        (1, f1, 0, 0, rows_e),
        (2, f2, 0, 0, rows_e),
        (3, f3, 0, 0, rows_e),
        (4, f4, 0, cut, cut),
        (4, b4, rows_l, 0, cut),
        (5, b3, rows_l, 0, rows_e),
        (6, b2, rows_l, 0, rows_e),
        (7, b1, 0, 0, rows_e),
    ):
        shard = (ctx - d) & (SHARDS - 1)
        moves.append(
            (array.at[pl.ds(base, count), :], img_buf.at[shard, pl.ds(first, count), :])
        )
    for d, array, base, first, count in (
        (0, own_l, 0, 0, rows_l),
        (1, f2, rows_e, 0, rows_l),
        (2, f3, rows_e, 0, rows_l),
        (3, f4, cut, 0, rows_l),
        (4, f5, 0, 0, part),
        (4, b5, 0, part, part),
        (5, b4, 0, 0, rows_l),
        (6, b3, 0, 0, rows_l),
        (7, b2, 0, 0, rows_l),
    ):
        shard = (ctx - d) & (SHARDS - 1)
        place = pl.ds(pl.multiple_of(shard * tok + first, part), count)
        moves.append((array.at[pl.ds(base, count), :], kv_buf.at[place, :]))
    copies = [
        pltpu.make_async_copy(source, target, sems.at[n])
        for n, (source, target) in enumerate(moves)
    ]
    for copy in copies:
        copy.start()
    for copy in copies:
        copy.wait()
    before = images_before(counts_ref, sample)
    for c in range(SHARDS):
        slot = (c - before) & (MAX_IMG - 1)
        start = jnp.where(slot < counts_ref[sample], starts_ref[sample, slot], -1)

        @pl.when(start >= 0)
        def _():
            rows = pl.ds(pl.multiple_of(start, IMG_TOK), IMG_TOK)
            kv_buf[rows, :] = img_buf[c, :IMG_TOK, :]

        @pl.when((start >= ctx * tok) & (start < ctx * tok + tok))
        def _():
            rows = pl.ds(pl.multiple_of(start - ctx * tok, IMG_TOK), IMG_TOK)
            for n in range(heads // 2):
                q_buf[rows, n * 2 * HD : (n + 1) * 2 * HD] = img_buf[
                    c, IMG_TOK * (n + 1) : IMG_TOK * (n + 2), :
                ]

    def phase(step, do_score, do_mix):
        slot = lax.rem(step, 2)
        other = 1 - slot

        def block(j):
            keys = pl.ds(pl.multiple_of(j * BLOCK, BLOCK), BLOCK)
            if do_score:
                columns = pl.ds(pl.multiple_of(step * HD, HD), HD)
                s = lax.dot_general(
                    q_buf[:, columns],
                    kv_buf[keys, :HD],
                    (((1,), (1,)), ((), ())),
                    preferred_element_type=F32,
                )
                row = lax.broadcasted_iota(jnp.int32, (tok, HD), 0) + (ctx * tok - j * BLOCK)
                column = lax.broadcasted_iota(jnp.int32, (tok, HD), 1)
                top = max_buf[slot]
                for g in range(BLOCK // HD):
                    seen = s[:, g * HD : (g + 1) * HD]
                    seen = jnp.where(column + g * HD <= row, seen, -1e30)
                    s_buf[slot, j, :, g * HD : (g + 1) * HD] = seen
                    top = jnp.maximum(top, seen)
                max_buf[slot] = top
            if do_mix:
                shared = max_buf[other]
                total = sum_buf[...]
                weights = []
                for g in range(BLOCK // HD):
                    w = jnp.exp2(s_buf[other, j, :, g * HD : (g + 1) * HD] * factor - shared)
                    total = total + w
                    weights.append(w.astype(BF16))
                sum_buf[...] = total
                acc_buf[...] += jnp.dot(
                    jnp.concatenate(weights, axis=1), kv_buf[keys, HD:], preferred_element_type=F32
                )

        if do_score:
            max_buf[slot] = jnp.full((tok, HD), -1e30, F32)
        if do_mix:
            sum_buf[...] = jnp.zeros((tok, HD), F32)
            acc_buf[...] = jnp.zeros((tok, HD), F32)
        pl.loop(0, (ctx * tok + tok + BLOCK - 1) // BLOCK)(block)
        if do_score:
            top = jnp.max(max_buf[slot], axis=1, keepdims=True) * factor
            max_buf[slot] = jnp.broadcast_to(top, (tok, HD))
        if do_mix:
            total = jnp.sum(sum_buf[...], axis=1, keepdims=True)
            columns = pl.ds(pl.multiple_of((step - 1) * HD, HD), HD)
            out_ref[:, columns] = (acc_buf[...] / total).astype(BF16)

    phase(jnp.int32(0), True, False)
    pl.loop(1, heads)(lambda step: phase(step, True, True))
    phase(jnp.int32(heads), False, True)


def attention(tok, heads, scalars, arrays):
    img_rows = IMG_TOK * (1 + heads // 2)
    return pl.pallas_call(
        functools.partial(attention_kernel, tok, heads),
        out_shape=jax.ShapeDtypeStruct((tok, heads * HD), BF16),
        in_specs=[pl.BlockSpec(memory_space=SMEM)] * 3
        + [pl.BlockSpec(memory_space=pl.ANY)] * len(arrays),
        out_specs=pl.BlockSpec(memory_space=VMEM),
        scratch_shapes=[
            pltpu.VMEM((tok, heads * HD), BF16),
            pltpu.VMEM((SHARDS * tok, 2 * HD), BF16),
            pltpu.VMEM((SHARDS, img_rows, 2 * HD), BF16),
            pltpu.VMEM((2, SHARDS * tok // BLOCK, tok, BLOCK), F32),
            pltpu.VMEM((2, tok, HD), F32),
            pltpu.VMEM((tok, HD), F32),
            pltpu.VMEM((tok, HD), F32),
            pltpu.SemaphoreType.DMA((32,)),
        ],
        compiler_params=pltpu.CompilerParams(vmem_limit_bytes=52 * 2**20),
        cost_estimate=pl.CostEstimate(
            flops=4 * tok * heads * SHARDS * tok * HD,
            bytes_accessed=8 * 2**20,
            transcendentals=tok * heads * SHARDS * tok,
        ),
        name="attention",
    )(*scalars, *arrays)


def on_device(
    text_rows, visual_rows, image_counts, image_starts, norm_gain, w_query, w_key, w_value
):
    ctx = lax.axis_index("ctx").astype(jnp.int32)
    sample = lax.axis_index("dp").astype(jnp.int32)
    mp = lax.axis_index("mp").astype(jnp.int32)
    tok = text_rows.shape[0]
    heads = w_query.shape[1] // HD
    ids = jnp.stack([mp, ctx, sample])

    w_kv = jnp.concatenate([w_key, w_value], axis=1)
    gain = norm_gain[None, :]
    every = jnp.arange(SHARDS, dtype=jnp.int32)

    def source(who):
        before = jnp.sum(jnp.where(every < who, image_counts, 0))
        slot = (ctx - before) & (MAX_IMG - 1)
        owner = jnp.minimum((before + slot) >> 3, SHARDS - 1)
        return slot, (owner ^ who) & 1, jnp.clip((who >> 1) - (owner >> 1), 0, 3)

    def choose(which, choices):
        chosen = choices[0]
        for n, choice in enumerate(choices[1:], 1):
            chosen = jnp.where(which == n, choice, chosen)
        return chosen

    my_slot, my_across, my_distance = source(sample)
    _, _, its_distance = source(sample ^ 1)
    quarter = tok // 4
    one_a, three_a = first_hop(text_rows[:quarter])
    one_b, three_b = first_hop(text_rows[quarter:])
    values = jnp.stack([one_a[0, 0], three_a[0, 0]]).astype(jnp.int32)
    zero = jnp.minimum(jnp.sum(jnp.abs(values)), 0)
    leaving = jnp.where(zero == 0, visual_rows, 0)
    routed = [visual_rows] + [shift(leaving, "dp", 2 * d, False) for d in (1, 2, 3)]
    for_other = choose(its_distance, routed)
    from_other = lax.ppermute(for_other, "dp", [(i, i ^ 1) for i in range(SHARDS)])
    image = choose(jnp.where(my_across == 1, 4, my_distance), routed + [from_other])
    image_parts = [image] + [exchange(image, mask) for mask in (1, 3, 2)]
    two_a = exchange(one_a, 3)
    two_b = exchange(one_b[:quarter], 3)
    two_c = exchange(three_b[quarter:], 1)

    mine = (every[:, None] == sample) & (every[None, :] == my_slot)
    my_start = jnp.sum(jnp.where(mine, image_starts, 0))
    text_tables = rotary_tables(ctx * tok + jnp.arange(tok, dtype=jnp.int32))
    image_tables = rotary_tables(my_start + jnp.arange(IMG_TOK, dtype=jnp.int32))
    own_e = project_image(
        ids, image_parts, gain, w_kv, w_query, image_tables,
        (one_a, three_a, *text_tables),
    )
    normed, own_l = project_text(
        ids, [text_rows, one_a, one_b, three_a, three_b, two_a, two_b, two_c],
        gain, w_kv, text_tables, (own_e,)
    )
    queries = [query(normed, w_query, text_tables, n, 2) for n in range(2)]

    cut, part = own_e.shape[0] // 2, tok // 2
    f1, b1 = shift(own_e, "ctx", 1, True), shift(own_e, "ctx", -1, True)
    f2 = shift(jnp.concatenate([f1, own_l], axis=0), "ctx", 1, True)
    b2 = shift(jnp.concatenate([own_l, b1], axis=0), "ctx", -1, True)
    f3, b3 = shift(f2, "ctx", 1, True), shift(b2, "ctx", -1, True)
    f4, b4 = shift(f3[cut:], "ctx", 1, True), shift(b3[: tok + cut], "ctx", -1, True)
    f5 = shift(f4[cut : cut + part], "ctx", 1, True)
    b5 = shift(b4[part:tok], "ctx", -1, True)
    return attention(
        tok, heads, (ids, image_counts, image_starts),
        [*queries, own_e, own_l, f1, f2, f3, f4, f5, b1, b2, b3, b4, b5],
    )


def solution(mesh):
    in_specs = (
        P(("dp", "ctx"), "mp"),
        P(("dp", "ctx"), "mp"),
        P(),
        P(),
        P(),
        P(None, "mp"),
        P(None, "mp"),
        P(None, "mp"),
    )
    out_specs = P(("dp", "ctx"), "mp")
    return jax.shard_map(
        on_device, mesh=mesh, in_specs=in_specs, out_specs=out_specs, check_vma=False
    )
```

```python
import functools
import math

import jax
import jax.numpy as jnp
from jax import lax
from jax.experimental import pallas as pl
from jax.experimental.pallas import tpu as pltpu
from jax.sharding import PartitionSpec as P

HD = 128
IMG_TOK = 64
MAX_IMG = 8
D = 4096
SHARDS = 8
BLOCK = 2048
rope_base = 500000.0
eps = 1e-05
BF16 = jnp.bfloat16
F32 = jnp.float32
VMEM = pltpu.VMEM
SMEM = pltpu.SMEM


def rotary_tables(positions):
    half_size = HD // 2
    exponent = jnp.arange(half_size, dtype=F32) * (2.0 / HD)
    frequency = jnp.exp(-exponent * math.log(rope_base))
    angles = positions.astype(F32)[:, None] * frequency[None, :]
    return jnp.cos(angles), jnp.sin(angles)


def rotate(u, cosine, sine):
    cosine = jnp.concatenate([cosine, cosine], axis=1)
    sine = jnp.concatenate([-sine, sine], axis=1)
    return u * cosine + pltpu.roll(u, HD // 2, 1) * sine


def shift(x, axis, d, wrap):
    pairs = [(i, (i + d) % SHARDS) for i in range(SHARDS) if wrap or 0 <= i + d < SHARDS]
    return lax.ppermute(x, axis, pairs)


def exchange(x, mask):
    return lax.ppermute(x, "mp", [(i, i ^ mask) for i in range(4)])


def first_hop(x):
    return exchange(x, 1), exchange(x, 3)


def normalise(mp, gain_ref, pieces, out_ref, rows):
    total = 0.0
    for piece in pieces:
        wide = piece.astype(F32)
        total = total + jnp.sum(wide * wide, axis=1, keepdims=True)
    scale = lax.rsqrt(total * (1.0 / D) + eps)
    for mask, piece in zip((0, 1, 3, 2), pieces):
        columns = pl.ds(pl.multiple_of((mp ^ mask) * 1024, 1024), 1024)
        value = piece.astype(F32) * scale * gain_ref[:, columns]
        out_ref[rows, columns] = value.astype(BF16)


def write_key_value(x, w_ref, cos, sin, out_ref, rows):
    product = jnp.dot(x, w_ref[...], preferred_element_type=F32)
    out_ref[rows, :HD] = rotate(product[:, :HD], cos, sin).astype(BF16)
    out_ref[rows, HD:] = product[:, HD:].astype(BF16)


def image_kernel(ids_ref, own, one, three, two, gain, w_kv, w_q, cos, sin, *refs):
    out_ref, normed = refs[-2:]
    rows = own.shape[0]
    step = pl.program_id(0)

    @pl.when(step == 0)
    def _():
        pieces = [own[...], one[...], three[...], two[...]]
        normalise(ids_ref[0], gain, pieces, normed, slice(0, rows))
        write_key_value(normed[...], w_kv, cos[...], sin[...], out_ref, slice(0, rows))

    product = jnp.dot(normed[...], w_q[...], preferred_element_type=F32)
    span = pl.ds(pl.multiple_of((step + 1) * rows, IMG_TOK), rows)
    for h in range(2):
        columns = slice(h * HD, (h + 1) * HD)
        out_ref[span, columns] = rotate(product[:, columns], cos[...], sin[...]).astype(BF16)


def project_image(ids, arrays, gain, w_kv, w_query, tables, after):
    rows, tile = arrays[0].shape[0], 2 * HD
    steps = w_query.shape[1] // tile
    whole = pl.BlockSpec(memory_space=VMEM)
    return pl.pallas_call(
        image_kernel,
        out_shape=jax.ShapeDtypeStruct(((1 + steps) * rows, tile), BF16),
        grid=(steps,),
        in_specs=[pl.BlockSpec(memory_space=SMEM)]
        + [whole] * (len(arrays) + 2)
        + [pl.BlockSpec((D, tile), lambda n: (0, n))]
        + [whole] * 2
        + [pl.BlockSpec(memory_space=pl.ANY)] * len(after),
        out_specs=pl.BlockSpec(((1 + steps) * rows, tile), lambda n: (0, 0)),
        scratch_shapes=[pltpu.VMEM((rows, D), BF16)],
        compiler_params=pltpu.CompilerParams(vmem_limit_bytes=58 * 2**20),
        cost_estimate=pl.CostEstimate(flops=8 * 10**9, bytes_accessed=10 * 2**20, transcendentals=0),
        name="project_image",
    )(ids, *arrays, gain, w_kv, w_query, *tables, *after)


def text_kernel(ids_ref, own, one_a, one_b, three_a, three_b, two_a, two_b, two_c, *refs):
    gain, w_kv, cos, sin = refs[:4]
    normed_ref, out_ref = refs[-2:]
    rows = own.shape[0]
    for n, others in enumerate(
        ((one_a, three_a, two_a), (one_b, three_b, two_b), (one_b, three_b, two_c))
    ):
        @pl.when(jnp.minimum(pl.program_id(0), 2) == n)
        def _():
            pieces = [own[...]] + [other[...] for other in others]
            normalise(ids_ref[0], gain, pieces, normed_ref, slice(0, rows))

    write_key_value(normed_ref[...], w_kv, cos[...], sin[...], out_ref, slice(0, rows))


def project_text(ids, arrays, gain, w_kv, tables, after):
    rows = arrays[0].shape[0]
    steps = 4
    tile = rows // steps

    def block(skipped):
        return pl.BlockSpec((tile, D // 4), lambda r: (jnp.maximum(r - skipped, 0), 0))

    whole = pl.BlockSpec(memory_space=VMEM)
    only = pl.BlockSpec((tile, D // 4), lambda r: (0, 0))
    table = pl.BlockSpec((tile, HD // 2), lambda r: (r, 0))
    return pl.pallas_call(
        text_kernel,
        out_shape=[
            jax.ShapeDtypeStruct((rows, D), BF16),
            jax.ShapeDtypeStruct((rows, 2 * HD), BF16),
        ],
        grid=(steps,),
        in_specs=[pl.BlockSpec(memory_space=SMEM)]
        + [block(0), only, block(1), only, block(1), only, only, block(2)]
        + [whole] * 2
        + [table] * 2
        + [pl.BlockSpec(memory_space=pl.ANY)] * len(after),
        out_specs=[
            pl.BlockSpec((tile, D), lambda r: (r, 0)),
            pl.BlockSpec((tile, 2 * HD), lambda r: (r, 0)),
        ],
        compiler_params=pltpu.CompilerParams(vmem_limit_bytes=58 * 2**20),
        cost_estimate=pl.CostEstimate(flops=0, bytes_accessed=0, transcendentals=0),
        name="project_text",
    )(ids, *arrays, gain, w_kv, *tables, *after)


def query_kernel(x_ref, w_ref, cos, sin, q_ref):
    product = jnp.dot(x_ref[...], w_ref[...], preferred_element_type=F32)
    for h in range(w_ref.shape[1] // HD):
        span = slice(h * HD, (h + 1) * HD)
        q_ref[:, span] = rotate(product[:, span], cos[...], sin[...]).astype(BF16)


def query(normed, w_query, tables, part, parts):
    rows, tile = normed.shape[0], 2 * HD
    columns = w_query.shape[1] // parts
    first = part * (columns // tile)
    whole = pl.BlockSpec(memory_space=VMEM)
    return pl.pallas_call(
        query_kernel,
        out_shape=jax.ShapeDtypeStruct((rows, columns), BF16),
        grid=(columns // tile,),
        in_specs=[whole, pl.BlockSpec((D, tile), lambda n: (0, first + n))] + [whole] * 2,
        out_specs=pl.BlockSpec((rows, tile), lambda n: (0, n)),
        compiler_params=pltpu.CompilerParams(vmem_limit_bytes=58 * 2**20),
        cost_estimate=pl.CostEstimate(flops=3 * 10**9, bytes_accessed=2**20, transcendentals=0),
        name="query",
    )(normed, w_query, *tables)


def images_before(counts_ref, sample):
    total = jnp.int32(0)
    for i in range(SHARDS):
        total = total + jnp.where(i < sample, counts_ref[i], 0)
    return total


def attention_kernel(tok, heads, ids_ref, counts_ref, starts_ref, *refs):
    q_one, q_two = refs[:2]
    images, texts = refs[2 : 3 + SHARDS], refs[3 + SHARDS : 4 + 2 * SHARDS]
    out_ref = refs[4 + 2 * SHARDS]
    q_buf, kv_buf, img_buf, s_buf, max_buf, sum_buf, acc_buf, sems = refs[5 + 2 * SHARDS :]
    ctx, sample = ids_ref[1], ids_ref[2]
    factor = math.log2(math.e) / math.sqrt(HD)

    middle = heads * HD // 2
    moves = [(q_one, q_buf.at[:, :middle]), (q_two, q_buf.at[:, middle:])]
    for n, d in enumerate((0, 1, 2, 3, 4, 4, 5, 6, 7)):
        shard = (ctx - d) & (SHARDS - 1)
        first = images[4].shape[0] if n == 5 else 0
        rows = pl.ds(first, images[n].shape[0])
        moves.append((images[n], img_buf.at[shard, rows, :]))
        first = texts[4].shape[0] if n == 5 else 0
        place = pl.multiple_of(shard * tok + first, texts[4].shape[0])
        moves.append((texts[n], kv_buf.at[pl.ds(place, texts[n].shape[0]), :]))
    copies = [
        pltpu.make_async_copy(source, target, sems.at[n])
        for n, (source, target) in enumerate(moves)
    ]
    for copy in copies:
        copy.start()
    for copy in copies:
        copy.wait()
    before = images_before(counts_ref, sample)
    for c in range(SHARDS):
        slot = (c - before) & (MAX_IMG - 1)
        start = jnp.where(slot < counts_ref[sample], starts_ref[sample, slot], -1)

        @pl.when(start >= 0)
        def _():
            rows = pl.ds(pl.multiple_of(start, IMG_TOK), IMG_TOK)
            kv_buf[rows, :] = img_buf[c, :IMG_TOK, :]

        @pl.when((start >= ctx * tok) & (start < ctx * tok + tok))
        def _():
            rows = pl.ds(pl.multiple_of(start - ctx * tok, IMG_TOK), IMG_TOK)
            for n in range(heads // 2):
                q_buf[rows, n * 2 * HD : (n + 1) * 2 * HD] = img_buf[
                    c, IMG_TOK * (n + 1) : IMG_TOK * (n + 2), :
                ]

    def phase(step, do_score, do_mix):
        slot = lax.rem(step, 2)
        other = 1 - slot

        def block(j):
            keys = pl.ds(pl.multiple_of(j * BLOCK, BLOCK), BLOCK)
            if do_score:
                columns = pl.ds(pl.multiple_of(step * HD, HD), HD)
                s = lax.dot_general(
                    q_buf[:, columns],
                    kv_buf[keys, :HD],
                    (((1,), (1,)), ((), ())),
                    preferred_element_type=F32,
                )
                row = lax.broadcasted_iota(jnp.int32, (tok, HD), 0) + (ctx * tok - j * BLOCK)
                column = lax.broadcasted_iota(jnp.int32, (tok, HD), 1)
                top = max_buf[slot]
                for g in range(BLOCK // HD):
                    seen = s[:, g * HD : (g + 1) * HD]
                    seen = jnp.where(column + g * HD <= row, seen, -1e30)
                    s_buf[slot, j, :, g * HD : (g + 1) * HD] = seen
                    top = jnp.maximum(top, seen)
                max_buf[slot] = top
            if do_mix:
                shared = max_buf[other]
                total = sum_buf[...]
                weights = []
                for g in range(BLOCK // HD):
                    w = jnp.exp2(s_buf[other, j, :, g * HD : (g + 1) * HD] * factor - shared)
                    total = total + w
                    weights.append(w.astype(BF16))
                sum_buf[...] = total
                acc_buf[...] += jnp.dot(
                    jnp.concatenate(weights, axis=1), kv_buf[keys, HD:], preferred_element_type=F32
                )

        if do_score:
            max_buf[slot] = jnp.full((tok, HD), -1e30, F32)
        if do_mix:
            sum_buf[...] = jnp.zeros((tok, HD), F32)
            acc_buf[...] = jnp.zeros((tok, HD), F32)
        pl.loop(0, (ctx * tok + tok + BLOCK - 1) // BLOCK)(block)
        if do_score:
            top = jnp.max(max_buf[slot], axis=1, keepdims=True) * factor
            max_buf[slot] = jnp.broadcast_to(top, (tok, HD))
        if do_mix:
            total = jnp.sum(sum_buf[...], axis=1, keepdims=True)
            columns = pl.ds(pl.multiple_of((step - 1) * HD, HD), HD)
            out_ref[:, columns] = (acc_buf[...] / total).astype(BF16)

    phase(jnp.int32(0), True, False)
    pl.loop(1, heads)(lambda step: phase(step, True, True))
    phase(jnp.int32(heads), False, True)


def attention(tok, heads, scalars, arrays):
    img_rows = IMG_TOK * (1 + heads // 2)
    return pl.pallas_call(
        functools.partial(attention_kernel, tok, heads),
        out_shape=jax.ShapeDtypeStruct((tok, heads * HD), BF16),
        in_specs=[pl.BlockSpec(memory_space=SMEM)] * 3
        + [pl.BlockSpec(memory_space=pl.ANY)] * len(arrays),
        out_specs=pl.BlockSpec(memory_space=VMEM),
        scratch_shapes=[
            pltpu.VMEM((tok, heads * HD), BF16),
            pltpu.VMEM((SHARDS * tok, 2 * HD), BF16),
            pltpu.VMEM((SHARDS, img_rows, 2 * HD), BF16),
            pltpu.VMEM((2, SHARDS * tok // BLOCK, tok, BLOCK), F32),
            pltpu.VMEM((2, tok, HD), F32),
            pltpu.VMEM((tok, HD), F32),
            pltpu.VMEM((tok, HD), F32),
            pltpu.SemaphoreType.DMA((32,)),
        ],
        compiler_params=pltpu.CompilerParams(vmem_limit_bytes=52 * 2**20),
        cost_estimate=pl.CostEstimate(
            flops=4 * tok * heads * SHARDS * tok * HD,
            bytes_accessed=8 * 2**20,
            transcendentals=tok * heads * SHARDS * tok,
        ),
        name="attention",
    )(*scalars, *arrays)


def on_device(
    text_rows, visual_rows, image_counts, image_starts, norm_gain, w_query, w_key, w_value
):
    ctx = lax.axis_index("ctx").astype(jnp.int32)
    sample = lax.axis_index("dp").astype(jnp.int32)
    mp = lax.axis_index("mp").astype(jnp.int32)
    tok = text_rows.shape[0]
    heads = w_query.shape[1] // HD
    ids = jnp.stack([mp, ctx, sample])

    w_kv = jnp.concatenate([w_key, w_value], axis=1)
    gain = norm_gain[None, :]
    every = jnp.arange(SHARDS, dtype=jnp.int32)

    def source(who):
        before = jnp.sum(jnp.where(every < who, image_counts, 0))
        slot = (ctx - before) & (MAX_IMG - 1)
        owner = jnp.minimum((before + slot) >> 3, SHARDS - 1)
        return slot, (owner ^ who) & 1, jnp.clip((who >> 1) - (owner >> 1), 0, 3)

    def choose(which, choices):
        chosen = choices[0]
        for n, choice in enumerate(choices[1:], 1):
            chosen = jnp.where(which == n, choice, chosen)
        return chosen

    my_slot, my_across, my_distance = source(sample)
    _, _, its_distance = source(sample ^ 1)
    quarter = tok // 4
    one_a, three_a = first_hop(text_rows[:quarter])
    one_b, three_b = first_hop(text_rows[quarter:])
    values = jnp.stack([one_a[0, 0], three_a[0, 0]]).astype(jnp.int32)
    zero = jnp.minimum(jnp.sum(jnp.abs(values)), 0)
    leaving = jnp.where(zero == 0, visual_rows, 0)
    routed = [visual_rows] + [shift(leaving, "dp", 2 * d, False) for d in (1, 2, 3)]
    for_other = choose(its_distance, routed)
    from_other = lax.ppermute(for_other, "dp", [(i, i ^ 1) for i in range(SHARDS)])
    image = choose(jnp.where(my_across == 1, 4, my_distance), routed + [from_other])
    image_parts = [image] + [exchange(image, mask) for mask in (1, 3, 2)]
    two_a = exchange(one_a, 3)
    two_b = exchange(one_b[:quarter], 3)
    two_c = exchange(three_b[quarter:], 1)

    mine = (every[:, None] == sample) & (every[None, :] == my_slot)
    my_start = jnp.sum(jnp.where(mine, image_starts, 0))
    text_tables = rotary_tables(ctx * tok + jnp.arange(tok, dtype=jnp.int32))
    image_tables = rotary_tables(my_start + jnp.arange(IMG_TOK, dtype=jnp.int32))
    own_e = project_image(
        ids, image_parts, gain, w_kv, w_query, image_tables,
        (one_a, three_a, *text_tables),
    )
    normed, own_l = project_text(
        ids, [text_rows, one_a, one_b, three_a, three_b, two_a, two_b, two_c],
        gain, w_kv, text_tables, (own_e,)
    )
    queries = [query(normed, w_query, text_tables, n, 2) for n in range(2)]

    def ring(own):
        cut = own.shape[0] // 2
        ups, downs = [own], [own]
        for _ in range(3):
            ups.append(shift(ups[-1], "ctx", 1, True))
            downs.append(shift(downs[-1], "ctx", -1, True))
        last = [shift(ups[3][:cut], "ctx", 1, True), shift(downs[3][cut:], "ctx", -1, True)]
        return [own, *ups[1:], *last, *downs[:0:-1]]

    return attention(
        tok, heads, (ids, image_counts, image_starts), [*queries, *ring(own_e), *ring(own_l)]
    )


def solution(mesh):
    in_specs = (
        P(("dp", "ctx"), "mp"),
        P(("dp", "ctx"), "mp"),
        P(),
        P(),
        P(),
        P(None, "mp"),
        P(None, "mp"),
        P(None, "mp"),
    )
    out_specs = P(("dp", "ctx"), "mp")
    return jax.shard_map(
        on_device, mesh=mesh, in_specs=in_specs, out_specs=out_specs, check_vma=False
    )
```

```python
import functools
import math

import jax
import jax.numpy as jnp
from jax import lax
from jax.experimental import pallas as pl
from jax.experimental.pallas import tpu as pltpu
from jax.sharding import PartitionSpec as P

HD = 128
IMG_TOK = 64
MAX_IMG = 8
D = 4096
SHARDS = 8
BLOCK = 2048
rope_base = 500000.0
eps = 1e-05
BF16 = jnp.bfloat16
F32 = jnp.float32
VMEM = pltpu.VMEM
SMEM = pltpu.SMEM


def rotary_tables(positions):
    half_size = HD // 2
    exponent = jnp.arange(half_size, dtype=F32) * (2.0 / HD)
    frequency = jnp.exp(-exponent * math.log(rope_base))
    angles = positions.astype(F32)[:, None] * frequency[None, :]
    return jnp.cos(angles), jnp.sin(angles)


def rotate(u, cosine, sine):
    cosine = jnp.concatenate([cosine, cosine], axis=1)
    sine = jnp.concatenate([-sine, sine], axis=1)
    return u * cosine + pltpu.roll(u, HD // 2, 1) * sine


def shift(x, axis, d, wrap):
    pairs = [(i, (i + d) % SHARDS) for i in range(SHARDS) if wrap or 0 <= i + d < SHARDS]
    return lax.ppermute(x, axis, pairs)


def exchange(x, mask):
    return lax.ppermute(x, "mp", [(i, i ^ mask) for i in range(4)])


def first_hop(x):
    return exchange(x, 1), exchange(x, 3)


def normalise(mp, gain_ref, pieces, out_ref, rows):
    total = 0.0
    for piece in pieces:
        wide = piece.astype(F32)
        total = total + jnp.sum(wide * wide, axis=1, keepdims=True)
    scale = lax.rsqrt(total * (1.0 / D) + eps)
    for mask, piece in zip((0, 1, 3, 2), pieces):
        columns = pl.ds(pl.multiple_of((mp ^ mask) * 1024, 1024), 1024)
        value = piece.astype(F32) * scale * gain_ref[:, columns]
        out_ref[rows, columns] = value.astype(BF16)


def write_key_value(x, w_ref, cos, sin, out_ref, rows):
    product = jnp.dot(x, w_ref[...], preferred_element_type=F32)
    out_ref[rows, :HD] = rotate(product[:, :HD], cos, sin).astype(BF16)
    out_ref[rows, HD:] = product[:, HD:].astype(BF16)


def image_kernel(ids_ref, own, one, three, two, gain, w_kv, w_q, cos, sin, *refs):
    out_ref, normed = refs[-2:]
    rows = own.shape[0]
    step = pl.program_id(0)

    @pl.when(step == 0)
    def _():
        pieces = [own[...], one[...], three[...], two[...]]
        normalise(ids_ref[0], gain, pieces, normed, slice(0, rows))
        write_key_value(normed[...], w_kv, cos[...], sin[...], out_ref, slice(0, rows))

    product = jnp.dot(normed[...], w_q[...], preferred_element_type=F32)
    span = pl.ds(pl.multiple_of((step + 1) * rows, IMG_TOK), rows)
    for h in range(2):
        columns = slice(h * HD, (h + 1) * HD)
        out_ref[span, columns] = rotate(product[:, columns], cos[...], sin[...]).astype(BF16)


def project_image(ids, arrays, gain, w_kv, w_query, tables, after):
    rows, tile = arrays[0].shape[0], 2 * HD
    steps = w_query.shape[1] // tile
    whole = pl.BlockSpec(memory_space=VMEM)
    return pl.pallas_call(
        image_kernel,
        out_shape=jax.ShapeDtypeStruct(((1 + steps) * rows, tile), BF16),
        grid=(steps,),
        in_specs=[pl.BlockSpec(memory_space=SMEM)]
        + [whole] * (len(arrays) + 2)
        + [pl.BlockSpec((D, tile), lambda n: (0, n))]
        + [whole] * 2
        + [pl.BlockSpec(memory_space=pl.ANY)] * len(after),
        out_specs=pl.BlockSpec(((1 + steps) * rows, tile), lambda n: (0, 0)),
        scratch_shapes=[pltpu.VMEM((rows, D), BF16)],
        compiler_params=pltpu.CompilerParams(vmem_limit_bytes=58 * 2**20),
        cost_estimate=pl.CostEstimate(flops=8 * 10**9, bytes_accessed=10 * 2**20, transcendentals=0),
        name="project_image",
    )(ids, *arrays, gain, w_kv, w_query, *tables, *after)


def hold_kernel(x_ref, *refs):
    refs[-1][...] = x_ref[...]


def hold(x, after):
    whole = pl.BlockSpec(memory_space=VMEM)
    return pl.pallas_call(
        hold_kernel,
        out_shape=jax.ShapeDtypeStruct(x.shape, x.dtype),
        in_specs=[whole] + [pl.BlockSpec(memory_space=pl.ANY)] * len(after),
        out_specs=whole,
        cost_estimate=pl.CostEstimate(flops=0, bytes_accessed=0, transcendentals=0),
        name="hold",
    )(x, *after)


def text_kernel(ids_ref, own, one_a, one_b, three_a, three_b, two_a, two_b, two_c, *refs):
    gain, w_kv, cos, sin = refs[:4]
    normed_ref, out_ref = refs[-2:]
    rows = own.shape[0]
    for n, others in enumerate(
        ((one_a, three_a, two_a), (one_b, three_b, two_b), (one_b, three_b, two_c))
    ):
        @pl.when(jnp.minimum(pl.program_id(0), 2) == n)
        def _():
            pieces = [own[...]] + [other[...] for other in others]
            normalise(ids_ref[0], gain, pieces, normed_ref, slice(0, rows))

    write_key_value(normed_ref[...], w_kv, cos[...], sin[...], out_ref, slice(0, rows))


def project_text(ids, arrays, gain, w_kv, tables, after):
    rows = arrays[0].shape[0]
    steps = 4
    tile = rows // steps

    def block(skipped):
        return pl.BlockSpec((tile, D // 4), lambda r: (jnp.maximum(r - skipped, 0), 0))

    whole = pl.BlockSpec(memory_space=VMEM)
    only = pl.BlockSpec((tile, D // 4), lambda r: (0, 0))
    table = pl.BlockSpec((tile, HD // 2), lambda r: (r, 0))
    return pl.pallas_call(
        text_kernel,
        out_shape=[
            jax.ShapeDtypeStruct((rows, D), BF16),
            jax.ShapeDtypeStruct((rows, 2 * HD), BF16),
        ],
        grid=(steps,),
        in_specs=[pl.BlockSpec(memory_space=SMEM)]
        + [block(0), only, block(1), only, block(1), only, only, block(2)]
        + [whole] * 2
        + [table] * 2
        + [pl.BlockSpec(memory_space=pl.ANY)] * len(after),
        out_specs=[
            pl.BlockSpec((tile, D), lambda r: (r, 0)),
            pl.BlockSpec((tile, 2 * HD), lambda r: (r, 0)),
        ],
        compiler_params=pltpu.CompilerParams(vmem_limit_bytes=58 * 2**20),
        cost_estimate=pl.CostEstimate(flops=0, bytes_accessed=0, transcendentals=0),
        name="project_text",
    )(ids, *arrays, gain, w_kv, *tables, *after)


def query_kernel(x_ref, w_ref, cos, sin, q_ref):
    product = jnp.dot(x_ref[...], w_ref[...], preferred_element_type=F32)
    for h in range(w_ref.shape[1] // HD):
        span = slice(h * HD, (h + 1) * HD)
        q_ref[:, span] = rotate(product[:, span], cos[...], sin[...]).astype(BF16)


def query(normed, w_query, tables, part, parts):
    rows, tile = normed.shape[0], 2 * HD
    columns = w_query.shape[1] // parts
    first = part * (columns // tile)
    whole = pl.BlockSpec(memory_space=VMEM)
    return pl.pallas_call(
        query_kernel,
        out_shape=jax.ShapeDtypeStruct((rows, columns), BF16),
        grid=(columns // tile,),
        in_specs=[whole, pl.BlockSpec((D, tile), lambda n: (0, first + n))] + [whole] * 2,
        out_specs=pl.BlockSpec((rows, tile), lambda n: (0, n)),
        compiler_params=pltpu.CompilerParams(vmem_limit_bytes=58 * 2**20),
        cost_estimate=pl.CostEstimate(flops=3 * 10**9, bytes_accessed=2**20, transcendentals=0),
        name="query",
    )(normed, w_query, *tables)


def images_before(counts_ref, sample):
    total = jnp.int32(0)
    for i in range(SHARDS):
        total = total + jnp.where(i < sample, counts_ref[i], 0)
    return total


def attention_kernel(tok, heads, ids_ref, counts_ref, starts_ref, *refs):
    queries, refs = refs[:4], refs[4:]
    own_e, own_l, f1, f2, f3, f4, f5, b1, b2, b3, b4, b5, out_ref = refs[:13]
    q_buf, kv_buf, img_buf, s_buf, max_buf, sum_buf, acc_buf, sems = refs[13:]
    ctx, sample = ids_ref[1], ids_ref[2]
    factor = math.log2(math.e) / math.sqrt(HD)

    rows_e, rows_l = own_e.shape[0], own_l.shape[0]
    cut, part = rows_e // 2, rows_l // 2
    moves = []
    for n, q_ref in enumerate(queries):
        width = q_ref.shape[1]
        moves.append((q_ref, q_buf.at[:, n * width : (n + 1) * width]))
    for d, array, base, first, count in (
        (0, own_e, 0, 0, rows_e),
        (1, f1, 0, 0, rows_e),
        (2, f2, 0, 0, rows_e),
        (3, f3, 0, 0, rows_e),
        (4, f4, 0, cut, cut),
        (4, b4, rows_l, 0, cut),
        (5, b3, rows_l, 0, rows_e),
        (6, b2, rows_l, 0, rows_e),
        (7, b1, 0, 0, rows_e),
    ):
        shard = (ctx - d) & (SHARDS - 1)
        moves.append(
            (array.at[pl.ds(base, count), :], img_buf.at[shard, pl.ds(first, count), :])
        )
    for d, array, base, first, count in (
        (0, own_l, 0, 0, rows_l),
        (1, f2, rows_e, 0, rows_l),
        (2, f3, rows_e, 0, rows_l),
        (3, f4, cut, 0, rows_l),
        (4, f5, 0, 0, part),
        (4, b5, 0, part, part),
        (5, b4, 0, 0, rows_l),
        (6, b3, 0, 0, rows_l),
        (7, b2, 0, 0, rows_l),
    ):
        shard = (ctx - d) & (SHARDS - 1)
        place = pl.ds(pl.multiple_of(shard * tok + first, part), count)
        moves.append((array.at[pl.ds(base, count), :], kv_buf.at[place, :]))
    copies = [
        pltpu.make_async_copy(source, target, sems.at[n])
        for n, (source, target) in enumerate(moves)
    ]
    for copy in copies:
        copy.start()
    for copy in copies:
        copy.wait()
    before = images_before(counts_ref, sample)
    for c in range(SHARDS):
        slot = (c - before) & (MAX_IMG - 1)
        start = jnp.where(slot < counts_ref[sample], starts_ref[sample, slot], -1)

        @pl.when(start >= 0)
        def _():
            rows = pl.ds(pl.multiple_of(start, IMG_TOK), IMG_TOK)
            kv_buf[rows, :] = img_buf[c, :IMG_TOK, :]

        @pl.when((start >= ctx * tok) & (start < ctx * tok + tok))
        def _():
            rows = pl.ds(pl.multiple_of(start - ctx * tok, IMG_TOK), IMG_TOK)
            for n in range(heads // 2):
                q_buf[rows, n * 2 * HD : (n + 1) * 2 * HD] = img_buf[
                    c, IMG_TOK * (n + 1) : IMG_TOK * (n + 2), :
                ]

    def phase(step, do_score, do_mix):
        slot = lax.rem(step, 2)
        other = 1 - slot

        def block(j):
            keys = pl.ds(pl.multiple_of(j * BLOCK, BLOCK), BLOCK)
            if do_score:
                columns = pl.ds(pl.multiple_of(step * HD, HD), HD)
                s = lax.dot_general(
                    q_buf[:, columns],
                    kv_buf[keys, :HD],
                    (((1,), (1,)), ((), ())),
                    preferred_element_type=F32,
                )
                row = lax.broadcasted_iota(jnp.int32, (tok, HD), 0) + (ctx * tok - j * BLOCK)
                column = lax.broadcasted_iota(jnp.int32, (tok, HD), 1)
                top = max_buf[slot]
                for g in range(BLOCK // HD):
                    seen = s[:, g * HD : (g + 1) * HD]
                    seen = jnp.where(column + g * HD <= row, seen, -1e30)
                    s_buf[slot, j, :, g * HD : (g + 1) * HD] = seen
                    top = jnp.maximum(top, seen)
                max_buf[slot] = top
            if do_mix:
                shared = max_buf[other]
                total = sum_buf[...]
                weights = []
                for g in range(BLOCK // HD):
                    w = jnp.exp2(s_buf[other, j, :, g * HD : (g + 1) * HD] * factor - shared)
                    total = total + w
                    weights.append(w.astype(BF16))
                sum_buf[...] = total
                acc_buf[...] += jnp.dot(
                    jnp.concatenate(weights, axis=1), kv_buf[keys, HD:], preferred_element_type=F32
                )

        if do_score:
            max_buf[slot] = jnp.full((tok, HD), -1e30, F32)
        if do_mix:
            sum_buf[...] = jnp.zeros((tok, HD), F32)
            acc_buf[...] = jnp.zeros((tok, HD), F32)
        pl.loop(0, (ctx * tok + tok + BLOCK - 1) // BLOCK)(block)
        if do_score:
            top = jnp.max(max_buf[slot], axis=1, keepdims=True) * factor
            max_buf[slot] = jnp.broadcast_to(top, (tok, HD))
        if do_mix:
            total = jnp.sum(sum_buf[...], axis=1, keepdims=True)
            columns = pl.ds(pl.multiple_of((step - 1) * HD, HD), HD)
            out_ref[:, columns] = (acc_buf[...] / total).astype(BF16)

    phase(jnp.int32(0), True, False)
    pl.loop(1, heads)(lambda step: phase(step, True, True))
    phase(jnp.int32(heads), False, True)


def attention(tok, heads, scalars, arrays):
    img_rows = IMG_TOK * (1 + heads // 2)
    return pl.pallas_call(
        functools.partial(attention_kernel, tok, heads),
        out_shape=jax.ShapeDtypeStruct((tok, heads * HD), BF16),
        in_specs=[pl.BlockSpec(memory_space=SMEM)] * 3
        + [pl.BlockSpec(memory_space=pl.ANY)] * len(arrays),
        out_specs=pl.BlockSpec(memory_space=VMEM),
        scratch_shapes=[
            pltpu.VMEM((tok, heads * HD), BF16),
            pltpu.VMEM((SHARDS * tok, 2 * HD), BF16),
            pltpu.VMEM((SHARDS, img_rows, 2 * HD), BF16),
            pltpu.VMEM((2, SHARDS * tok // BLOCK, tok, BLOCK), F32),
            pltpu.VMEM((2, tok, HD), F32),
            pltpu.VMEM((tok, HD), F32),
            pltpu.VMEM((tok, HD), F32),
            pltpu.SemaphoreType.DMA((32,)),
        ],
        compiler_params=pltpu.CompilerParams(vmem_limit_bytes=52 * 2**20),
        cost_estimate=pl.CostEstimate(
            flops=4 * tok * heads * SHARDS * tok * HD,
            bytes_accessed=8 * 2**20,
            transcendentals=tok * heads * SHARDS * tok,
        ),
        name="attention",
    )(*scalars, *arrays)


def on_device(
    text_rows, visual_rows, image_counts, image_starts, norm_gain, w_query, w_key, w_value
):
    ctx = lax.axis_index("ctx").astype(jnp.int32)
    sample = lax.axis_index("dp").astype(jnp.int32)
    mp = lax.axis_index("mp").astype(jnp.int32)
    tok = text_rows.shape[0]
    heads = w_query.shape[1] // HD
    ids = jnp.stack([mp, ctx, sample])

    w_kv = jnp.concatenate([w_key, w_value], axis=1)
    gain = norm_gain[None, :]
    every = jnp.arange(SHARDS, dtype=jnp.int32)

    def source(who):
        before = jnp.sum(jnp.where(every < who, image_counts, 0))
        slot = (ctx - before) & (MAX_IMG - 1)
        owner = jnp.minimum((before + slot) >> 3, SHARDS - 1)
        return slot, (owner ^ who) & 1, jnp.clip((who >> 1) - (owner >> 1), 0, 3)

    def choose(which, choices):
        chosen = choices[0]
        for n, choice in enumerate(choices[1:], 1):
            chosen = jnp.where(which == n, choice, chosen)
        return chosen

    my_slot, my_across, my_distance = source(sample)
    _, _, its_distance = source(sample ^ 1)
    quarter = tok // 4
    group_a, group_b = text_rows[:quarter], text_rows[quarter:]
    one_a, three_a = first_hop(group_a)
    one_b, three_b = first_hop(group_b)
    leaving = hold(visual_rows, (one_a, three_a))
    routed = [visual_rows] + [shift(leaving, "dp", 2 * d, False) for d in (1, 2, 3)]
    for_other = choose(its_distance, routed)
    from_other = lax.ppermute(for_other, "dp", [(i, i ^ 1) for i in range(SHARDS)])
    image = choose(jnp.where(my_across == 1, 4, my_distance), routed + [from_other])
    image_parts = [image] + [exchange(image, mask) for mask in (1, 3, 2)]
    two_a = exchange(one_a, 3)
    two_b = exchange(one_b[:quarter], 3)
    two_c = exchange(three_b[quarter:], 1)

    mine = (every[:, None] == sample) & (every[None, :] == my_slot)
    my_start = jnp.sum(jnp.where(mine, image_starts, 0))
    text_tables = rotary_tables(ctx * tok + jnp.arange(tok, dtype=jnp.int32))
    image_tables = rotary_tables(my_start + jnp.arange(IMG_TOK, dtype=jnp.int32))
    own_e = project_image(
        ids, image_parts, gain, w_kv, w_query, image_tables,
        (one_a, three_a, *text_tables),
    )
    normed, own_l = project_text(
        ids, [text_rows, one_a, one_b, three_a, three_b, two_a, two_b, two_c],
        gain, w_kv, text_tables, (own_e,)
    )
    queries = [query(normed, w_query, text_tables, n, 4) for n in range(4)]

    cut, part = own_e.shape[0] // 2, tok // 2
    f1, b1 = shift(own_e, "ctx", 1, True), shift(own_e, "ctx", -1, True)
    f2 = shift(jnp.concatenate([f1, own_l], axis=0), "ctx", 1, True)
    b2 = shift(jnp.concatenate([own_l, b1], axis=0), "ctx", -1, True)
    f3, b3 = shift(f2, "ctx", 1, True), shift(b2, "ctx", -1, True)
    f4, b4 = shift(f3[cut:], "ctx", 1, True), shift(b3[: tok + cut], "ctx", -1, True)
    f5 = shift(f4[cut : cut + part], "ctx", 1, True)
    b5 = shift(b4[part:tok], "ctx", -1, True)
    return attention(
        tok, heads, (ids, image_counts, image_starts),
        [*queries, own_e, own_l, f1, f2, f3, f4, f5, b1, b2, b3, b4, b5],
    )


def solution(mesh):
    in_specs = (
        P(("dp", "ctx"), "mp"),
        P(("dp", "ctx"), "mp"),
        P(),
        P(),
        P(),
        P(None, "mp"),
        P(None, "mp"),
        P(None, "mp"),
    )
    out_specs = P(("dp", "ctx"), "mp")
    return jax.shard_map(
        on_device, mesh=mesh, in_specs=in_specs, out_specs=out_specs, check_vma=False
    )
```

```python
import functools
import math

import jax
import jax.numpy as jnp
from jax import lax
from jax.experimental import pallas as pl
from jax.experimental.pallas import tpu as pltpu
from jax.sharding import PartitionSpec as P

HD = 128
IMG_TOK = 64
MAX_IMG = 8
D = 4096
SHARDS = 8
BLOCK = 1792
rope_base = 500000.0
eps = 1e-05
BF16 = jnp.bfloat16
F32 = jnp.float32
VMEM = pltpu.VMEM
SMEM = pltpu.SMEM


def rotary_tables(positions):
    half_size = HD // 2
    exponent = jnp.arange(half_size, dtype=F32) * (2.0 / HD)
    frequency = jnp.exp(-exponent * math.log(rope_base))
    angles = positions.astype(F32)[:, None] * frequency[None, :]
    return jnp.cos(angles), jnp.sin(angles)


def rotate(u, cosine, sine):
    cosine = jnp.concatenate([cosine, cosine], axis=1)
    sine = jnp.concatenate([-sine, sine], axis=1)
    return u * cosine + pltpu.roll(u, HD // 2, 1) * sine


def shift(x, axis, d, wrap):
    pairs = [(i, (i + d) % SHARDS) for i in range(SHARDS) if wrap or 0 <= i + d < SHARDS]
    return lax.ppermute(x, axis, pairs)


def exchange(x, mask):
    return lax.ppermute(x, "mp", [(i, i ^ mask) for i in range(4)])


def first_hop(x):
    return exchange(x, 1), exchange(x, 3)


def normalise(mp, gain_ref, pieces, out_ref, rows):
    total = 0.0
    for piece in pieces:
        wide = piece.astype(F32)
        total = total + jnp.sum(wide * wide, axis=1, keepdims=True)
    scale = lax.rsqrt(total * (1.0 / D) + eps)
    for mask, piece in zip((0, 1, 3, 2), pieces):
        columns = pl.ds(pl.multiple_of((mp ^ mask) * 1024, 1024), 1024)
        value = piece.astype(F32) * scale * gain_ref[:, columns]
        out_ref[rows, columns] = value.astype(BF16)


def write_key_value(x, w_ref, cos, sin, out_ref, rows):
    product = jnp.dot(x, w_ref[...], preferred_element_type=F32)
    out_ref[rows, :HD] = rotate(product[:, :HD], cos, sin).astype(BF16)
    out_ref[rows, HD:] = product[:, HD:].astype(BF16)


def image_kernel(ids_ref, own, one, three, two, gain, w_kv, w_q, cos, sin, *refs):
    out_ref, normed = refs[-2:]
    rows = own.shape[0]
    step = pl.program_id(0)

    @pl.when(step == 0)
    def _():
        pieces = [own[...], one[...], three[...], two[...]]
        normalise(ids_ref[0], gain, pieces, normed, slice(0, rows))
        write_key_value(normed[...], w_kv, cos[...], sin[...], out_ref, slice(0, rows))

    product = jnp.dot(normed[...], w_q[...], preferred_element_type=F32)
    span = pl.ds(pl.multiple_of((step + 1) * rows, IMG_TOK), rows)
    for h in range(2):
        columns = slice(h * HD, (h + 1) * HD)
        out_ref[span, columns] = rotate(product[:, columns], cos[...], sin[...]).astype(BF16)


def project_image(ids, arrays, gain, w_kv, w_query, tables, after):
    rows, tile = arrays[0].shape[0], 2 * HD
    steps = w_query.shape[1] // tile
    whole = pl.BlockSpec(memory_space=VMEM)
    return pl.pallas_call(
        image_kernel,
        out_shape=jax.ShapeDtypeStruct(((1 + steps) * rows, tile), BF16),
        grid=(steps,),
        in_specs=[pl.BlockSpec(memory_space=SMEM)]
        + [whole] * (len(arrays) + 2)
        + [pl.BlockSpec((D, tile), lambda n: (0, n))]
        + [whole] * 2
        + [pl.BlockSpec(memory_space=pl.ANY)] * len(after),
        out_specs=pl.BlockSpec(((1 + steps) * rows, tile), lambda n: (0, 0)),
        scratch_shapes=[pltpu.VMEM((rows, D), BF16)],
        compiler_params=pltpu.CompilerParams(vmem_limit_bytes=58 * 2**20),
        cost_estimate=pl.CostEstimate(flops=8 * 10**9, bytes_accessed=10 * 2**20, transcendentals=0),
        name="project_image",
    )(ids, *arrays, gain, w_kv, w_query, *tables, *after)


def hold_kernel(x_ref, *refs):
    refs[-1][...] = x_ref[...]


def hold(x, after):
    whole = pl.BlockSpec(memory_space=VMEM)
    return pl.pallas_call(
        hold_kernel,
        out_shape=jax.ShapeDtypeStruct(x.shape, x.dtype),
        in_specs=[whole] + [pl.BlockSpec(memory_space=pl.ANY)] * len(after),
        out_specs=whole,
        cost_estimate=pl.CostEstimate(flops=0, bytes_accessed=0, transcendentals=0),
        name="hold",
    )(x, *after)


def text_kernel(ids_ref, own, one_a, one_b, three_a, three_b, two_a, two_b, two_c, *refs):
    gain, w_kv, cos, sin = refs[:4]
    normed_ref, out_ref = refs[-2:]
    rows = own.shape[0]
    for n, others in enumerate(
        ((one_a, three_a, two_a), (one_b, three_b, two_b), (one_b, three_b, two_c))
    ):
        @pl.when(jnp.minimum(pl.program_id(0), 2) == n)
        def _():
            pieces = [own[...]] + [other[...] for other in others]
            normalise(ids_ref[0], gain, pieces, normed_ref, slice(0, rows))

    write_key_value(normed_ref[...], w_kv, cos[...], sin[...], out_ref, slice(0, rows))


def project_text(ids, arrays, gain, w_kv, tables, after):
    rows = arrays[0].shape[0]
    steps = 4
    tile = rows // steps

    def block(skipped):
        return pl.BlockSpec((tile, D // 4), lambda r: (jnp.maximum(r - skipped, 0), 0))

    whole = pl.BlockSpec(memory_space=VMEM)
    only = pl.BlockSpec((tile, D // 4), lambda r: (0, 0))
    table = pl.BlockSpec((tile, HD // 2), lambda r: (r, 0))
    return pl.pallas_call(
        text_kernel,
        out_shape=[
            jax.ShapeDtypeStruct((rows, D), BF16),
            jax.ShapeDtypeStruct((rows, 2 * HD), BF16),
        ],
        grid=(steps,),
        in_specs=[pl.BlockSpec(memory_space=SMEM)]
        + [block(0), only, block(1), only, block(1), only, only, block(2)]
        + [whole] * 2
        + [table] * 2
        + [pl.BlockSpec(memory_space=pl.ANY)] * len(after),
        out_specs=[
            pl.BlockSpec((tile, D), lambda r: (r, 0)),
            pl.BlockSpec((tile, 2 * HD), lambda r: (r, 0)),
        ],
        compiler_params=pltpu.CompilerParams(vmem_limit_bytes=58 * 2**20),
        cost_estimate=pl.CostEstimate(flops=0, bytes_accessed=0, transcendentals=0),
        name="project_text",
    )(ids, *arrays, gain, w_kv, *tables, *after)


def query_kernel(x_ref, w_ref, cos, sin, q_ref):
    product = jnp.dot(x_ref[...], w_ref[...], preferred_element_type=F32)
    for h in range(w_ref.shape[1] // HD):
        span = slice(h * HD, (h + 1) * HD)
        q_ref[:, span] = rotate(product[:, span], cos[...], sin[...]).astype(BF16)


def query(normed, w_query, tables, part, parts):
    rows, tile = normed.shape[0], 2 * HD
    columns = w_query.shape[1] // parts
    first = part * (columns // tile)
    whole = pl.BlockSpec(memory_space=VMEM)
    return pl.pallas_call(
        query_kernel,
        out_shape=jax.ShapeDtypeStruct((rows, columns), BF16),
        grid=(columns // tile,),
        in_specs=[whole, pl.BlockSpec((D, tile), lambda n: (0, first + n))] + [whole] * 2,
        out_specs=pl.BlockSpec((rows, tile), lambda n: (0, n)),
        compiler_params=pltpu.CompilerParams(vmem_limit_bytes=58 * 2**20),
        cost_estimate=pl.CostEstimate(flops=6 * 10**9, bytes_accessed=2**20, transcendentals=0),
        name="query",
    )(normed, w_query, *tables)


def images_before(counts_ref, sample):
    total = jnp.int32(0)
    for i in range(SHARDS):
        total = total + jnp.where(i < sample, counts_ref[i], 0)
    return total


def image_starts_of(ids_ref, counts_ref, starts_ref):
    sample = ids_ref[2]
    before = images_before(counts_ref, sample)
    for c in range(SHARDS):
        slot = (c - before) & (MAX_IMG - 1)
        yield c, jnp.where(slot < counts_ref[sample], starts_ref[sample, slot], -1)


def attention_kernel(tok, heads, ids_ref, counts_ref, starts_ref, *refs):
    q_one, q_two, own_e, own_l, f1, f2, f3, f4, b1, b2, b3, b4 = refs[:12]
    q_buf, img_kv, acc_out, max_out, sum_out = refs[12:17]
    kv_buf, img_buf, s_buf, max_buf, sum_buf, acc_buf, sems = refs[17:]
    ctx = ids_ref[1]
    factor = math.log2(math.e) / math.sqrt(HD)
    shift_by = tok.bit_length() - 1
    rows_e, rows_l = own_e.shape[0], own_l.shape[0]
    cut = rows_e // 2

    middle = heads * HD // 2
    moves = [(q_one, q_buf.at[:, :middle]), (q_two, q_buf.at[:, middle:])]
    for d, array, base, first, count in (
        (0, own_e, 0, 0, rows_e),
        (1, f1, 0, 0, rows_e),
        (2, f2, 0, 0, rows_e),
        (3, f3, 0, 0, rows_e),
        (4, f4, 0, cut, cut),
        (4, b4, rows_l, 0, cut),
        (5, b3, rows_l, 0, rows_e),
        (6, b2, rows_l, 0, rows_e),
        (7, b1, 0, 0, rows_e),
    ):
        shard = (ctx - d) & (SHARDS - 1)
        moves.append((array.at[pl.ds(base, count), :], img_buf.at[shard, pl.ds(first, count), :]))
    texts = ((own_l, 0), (f2, rows_e), (f3, rows_e), (f4, cut), (b4, 0), (b3, 0), (b2, 0))
    for n, (array, base) in enumerate(texts):
        moves.append((array.at[pl.ds(base, rows_l), :], kv_buf.at[pl.ds(n * tok, tok), :]))
    copies = [
        pltpu.make_async_copy(source, target, sems.at[n])
        for n, (source, target) in enumerate(moves)
    ]
    for copy in copies:
        copy.start()
    for copy in copies:
        copy.wait()
    for c, start in image_starts_of(ids_ref, counts_ref, starts_ref):
        img_kv[c] = img_buf[c, :IMG_TOK, :]
        shard, row = start >> shift_by, start & (tok - 1)
        distance = ctx - shard

        @pl.when((start >= 0) & (distance >= 0) & (distance != 4))
        def _():
            place = jnp.where(distance > 4, distance - 1, distance) * tok + row
            kv_buf[pl.ds(pl.multiple_of(place, IMG_TOK), IMG_TOK), :] = img_buf[c, :IMG_TOK, :]

        @pl.when((start >= 0) & (distance == 0))
        def _():
            rows = pl.ds(pl.multiple_of(row, IMG_TOK), IMG_TOK)
            for n in range(heads // 2):
                q_buf[rows, n * 2 * HD : (n + 1) * 2 * HD] = img_buf[
                    c, IMG_TOK * (n + 1) : IMG_TOK * (n + 2), :
                ]

    max_out[...] = jnp.zeros((tok, HD), F32)
    sum_out[...] = jnp.zeros((tok, HD), F32)

    def phase(step, do_score, do_mix):
        slot = lax.rem(step, 2)
        other = 1 - slot

        def block(j):
            keys = pl.ds(pl.multiple_of(j * BLOCK, BLOCK), BLOCK)
            if do_score:
                columns = pl.ds(pl.multiple_of(step * HD, HD), HD)
                s = lax.dot_general(
                    q_buf[:, columns],
                    kv_buf[keys, :HD],
                    (((1,), (1,)), ((), ())),
                    preferred_element_type=F32,
                )
                row = lax.broadcasted_iota(jnp.int32, (tok, HD), 0)
                column = lax.broadcasted_iota(jnp.int32, (tok, HD), 1)
                top = max_buf[slot]
                for g in range(BLOCK // HD):
                    place = j * BLOCK + g * HD
                    nth = place >> shift_by
                    earlier = nth + jnp.where(nth > 3, 1, 0) <= ctx
                    ahead = jnp.where(nth == 0, place, jnp.where(earlier, -tok, tok))
                    seen = s[:, g * HD : (g + 1) * HD]
                    seen = jnp.where(column + ahead <= row, seen, -1e30)
                    s_buf[slot, j, :, g * HD : (g + 1) * HD] = seen
                    top = jnp.maximum(top, seen)
                max_buf[slot] = top
            if do_mix:
                shared = max_buf[other]
                total = sum_buf[...]
                weights = []
                for g in range(BLOCK // HD):
                    w = jnp.exp2(s_buf[other, j, :, g * HD : (g + 1) * HD] * factor - shared)
                    total = total + w
                    weights.append(w.astype(BF16))
                sum_buf[...] = total
                acc_buf[...] += jnp.dot(
                    jnp.concatenate(weights, axis=1), kv_buf[keys, HD:], preferred_element_type=F32
                )

        if do_score:
            max_buf[slot] = jnp.full((tok, HD), -1e30, F32)
        if do_mix:
            sum_buf[...] = jnp.zeros((tok, HD), F32)
            acc_buf[...] = jnp.zeros((tok, HD), F32)
        pl.loop(0, jnp.where(ctx * tok + tok > BLOCK, 2, 1))(block)
        if do_score:
            top = jnp.max(max_buf[slot], axis=1, keepdims=True) * factor
            max_buf[slot] = jnp.broadcast_to(top, (tok, HD))
        if do_mix:
            head = step - 1
            here = lax.broadcasted_iota(jnp.int32, (tok, HD), 1) == head
            max_out[...] = jnp.where(here, max_buf[other], max_out[...])
            total = jnp.sum(sum_buf[...], axis=1, keepdims=True)
            sum_out[...] = jnp.where(here, total, sum_out[...])
            acc_out[:, pl.ds(pl.multiple_of(head * HD, HD), HD)] = acc_buf[...]

    phase(jnp.int32(0), True, False)
    pl.loop(1, heads)(lambda step: phase(step, True, True))
    phase(jnp.int32(heads), False, True)


def attention(tok, heads, scalars, arrays):
    img_rows = IMG_TOK * (1 + heads // 2)
    keys = (SHARDS - 1) * tok
    return pl.pallas_call(
        functools.partial(attention_kernel, tok, heads),
        out_shape=[
            jax.ShapeDtypeStruct((tok, heads * HD), BF16),
            jax.ShapeDtypeStruct((SHARDS, IMG_TOK, 2 * HD), BF16),
            jax.ShapeDtypeStruct((tok, heads * HD), F32),
            jax.ShapeDtypeStruct((tok, HD), F32),
            jax.ShapeDtypeStruct((tok, HD), F32),
        ],
        in_specs=[pl.BlockSpec(memory_space=SMEM)] * 3
        + [pl.BlockSpec(memory_space=pl.ANY)] * len(arrays),
        out_specs=[pl.BlockSpec(memory_space=VMEM)] * 5,
        scratch_shapes=[
            pltpu.VMEM((keys, 2 * HD), BF16),
            pltpu.VMEM((SHARDS, img_rows, 2 * HD), BF16),
            pltpu.VMEM((2, keys // BLOCK, tok, BLOCK), F32),
            pltpu.VMEM((2, tok, HD), F32),
            pltpu.VMEM((tok, HD), F32),
            pltpu.VMEM((tok, HD), F32),
            pltpu.SemaphoreType.DMA((32,)),
        ],
        compiler_params=pltpu.CompilerParams(vmem_limit_bytes=52 * 2**20),
        cost_estimate=pl.CostEstimate(
            flops=4 * tok * heads * keys * HD,
            bytes_accessed=8 * 2**20,
            transcendentals=tok * heads * keys,
        ),
        name="attention",
    )(*scalars, *arrays)


def finish_kernel(tok, ids_ref, counts_ref, starts_ref, *refs):
    q_ref, img_kv, lower, upper, acc_ref, max_ref, sum_ref, out_ref, kv_buf = refs
    ctx = ids_ref[1]
    step = pl.program_id(0)
    factor = math.log2(math.e) / math.sqrt(HD)
    shift_by = tok.bit_length() - 1

    @pl.when(step == 0)
    def _():
        half = lower.shape[0]
        kv_buf[:half, :] = lower[...]
        kv_buf[half:, :] = upper[...]
        for c, start in image_starts_of(ids_ref, counts_ref, starts_ref):
            @pl.when((start >= 0) & (ctx - (start >> shift_by) == 4))
            def _():
                rows = pl.ds(pl.multiple_of(start & (tok - 1), IMG_TOK), IMG_TOK)
                kv_buf[rows, :] = img_kv[c]

    def of_head(ref, head):
        here = lax.broadcasted_iota(jnp.int32, (tok, HD), 1) == head
        return jnp.sum(jnp.where(here, ref[...], 0.0), axis=1, keepdims=True)

    count = out_ref.shape[1] // HD

    @pl.when(ctx >= 4)
    def _():
        for n in range(count):
            span = slice(n * HD, (n + 1) * HD)
            s = lax.dot_general(
                q_ref[:, span],
                kv_buf[:, :HD],
                (((1,), (1,)), ((), ())),
                preferred_element_type=F32,
            )
            before = of_head(max_ref, step * count + n)
            top = jnp.maximum(before, jnp.max(s, axis=1, keepdims=True) * factor)
            scale = jnp.exp2(before - top)
            w = jnp.exp2(s * factor - top)
            total = of_head(sum_ref, step * count + n) * scale + jnp.sum(w, axis=1, keepdims=True)
            mixed = jnp.dot(w.astype(BF16), kv_buf[:, HD:], preferred_element_type=F32)
            out_ref[:, span] = ((acc_ref[:, span] * scale + mixed) / total).astype(BF16)

    @pl.when(ctx < 4)
    def _():
        for n in range(count):
            span = slice(n * HD, (n + 1) * HD)
            total = of_head(sum_ref, step * count + n)
            out_ref[:, span] = (acc_ref[:, span] / total).astype(BF16)


def finish(tok, heads, scalars, q_all, img_kv, lower, upper, state):
    width = 2 * HD
    whole = pl.BlockSpec(memory_space=VMEM)
    block = pl.BlockSpec((tok, width), lambda n: (0, n))
    return pl.pallas_call(
        functools.partial(finish_kernel, tok),
        out_shape=jax.ShapeDtypeStruct((tok, heads * HD), BF16),
        grid=(heads * HD // width,),
        in_specs=[pl.BlockSpec(memory_space=SMEM)] * 3 + [block] + [whole] * 3 + [block] + [whole] * 2,
        out_specs=block,
        scratch_shapes=[pltpu.VMEM((tok, 2 * HD), BF16)],
        compiler_params=pltpu.CompilerParams(vmem_limit_bytes=40 * 2**20),
        cost_estimate=pl.CostEstimate(
            flops=4 * tok * heads * tok * HD, bytes_accessed=6 * 2**20, transcendentals=0
        ),
        name="finish",
    )(*scalars, q_all, img_kv, lower, upper, *state)


def on_device(
    text_rows, visual_rows, image_counts, image_starts, norm_gain, w_query, w_key, w_value
):
    ctx = lax.axis_index("ctx").astype(jnp.int32)
    sample = lax.axis_index("dp").astype(jnp.int32)
    mp = lax.axis_index("mp").astype(jnp.int32)
    tok = text_rows.shape[0]
    heads = w_query.shape[1] // HD
    ids = jnp.stack([mp, ctx, sample])

    w_kv = jnp.concatenate([w_key, w_value], axis=1)
    gain = norm_gain[None, :]
    every = jnp.arange(SHARDS, dtype=jnp.int32)

    def source(who):
        before = jnp.sum(jnp.where(every < who, image_counts, 0))
        slot = (ctx - before) & (MAX_IMG - 1)
        owner = jnp.minimum((before + slot) >> 3, SHARDS - 1)
        return slot, (owner ^ who) & 1, jnp.clip((who >> 1) - (owner >> 1), 0, 3)

    def choose(which, choices):
        chosen = choices[0]
        for n, choice in enumerate(choices[1:], 1):
            chosen = jnp.where(which == n, choice, chosen)
        return chosen

    my_slot, my_across, my_distance = source(sample)
    _, _, its_distance = source(sample ^ 1)
    quarter = tok // 4
    group_a, group_b = text_rows[:quarter], text_rows[quarter:]
    one_a, three_a = first_hop(group_a)
    one_b, three_b = first_hop(group_b)
    leaving = hold(visual_rows, (one_a, three_a))
    routed = [visual_rows] + [shift(leaving, "dp", 2 * d, False) for d in (1, 2, 3)]
    for_other = choose(its_distance, routed)
    from_other = lax.ppermute(for_other, "dp", [(i, i ^ 1) for i in range(SHARDS)])
    image = choose(jnp.where(my_across == 1, 4, my_distance), routed + [from_other])
    image_parts = [image] + [exchange(image, mask) for mask in (1, 3, 2)]
    two_a = exchange(one_a, 3)
    two_b = exchange(one_b[:quarter], 3)
    two_c = exchange(three_b[quarter:], 1)

    mine = (every[:, None] == sample) & (every[None, :] == my_slot)
    my_start = jnp.sum(jnp.where(mine, image_starts, 0))
    text_tables = rotary_tables(ctx * tok + jnp.arange(tok, dtype=jnp.int32))
    image_tables = rotary_tables(my_start + jnp.arange(IMG_TOK, dtype=jnp.int32))
    own_e = project_image(
        ids, image_parts, gain, w_kv, w_query, image_tables,
        (one_a, three_a, *text_tables),
    )
    normed, own_l = project_text(
        ids, [text_rows, one_a, one_b, three_a, three_b, two_a, two_b, two_c],
        gain, w_kv, text_tables, (own_e,)
    )
    queries = [query(normed, w_query, text_tables, n, 2) for n in range(2)]

    cut, part = own_e.shape[0] // 2, tok // 2
    f1, b1 = shift(own_e, "ctx", 1, True), shift(own_e, "ctx", -1, True)
    f2 = shift(jnp.concatenate([f1, own_l], axis=0), "ctx", 1, True)
    b2 = shift(jnp.concatenate([own_l, b1], axis=0), "ctx", -1, True)
    f3, b3 = shift(f2, "ctx", 1, True), shift(b2, "ctx", -1, True)
    f4, b4 = shift(f3[cut:], "ctx", 1, True), shift(b3[: tok + cut], "ctx", -1, True)
    f5 = shift(f4[cut : cut + part], "ctx", 1, True)
    b5 = shift(b4[part:tok], "ctx", -1, True)
    scalars = (ids, image_counts, image_starts)
    q_all, img_kv, *state = attention(
        tok, heads, scalars, [*queries, own_e, own_l, f1, f2, f3, f4, b1, b2, b3, b4]
    )
    return finish(tok, heads, scalars, q_all, img_kv, f5, b5, state)


def solution(mesh):
    in_specs = (
        P(("dp", "ctx"), "mp"),
        P(("dp", "ctx"), "mp"),
        P(),
        P(),
        P(),
        P(None, "mp"),
        P(None, "mp"),
        P(None, "mp"),
    )
    out_specs = P(("dp", "ctx"), "mp")
    return jax.shard_map(
        on_device, mesh=mesh, in_specs=in_specs, out_specs=out_specs, check_vma=False
    )
```

```python
import functools
import math

import jax
import jax.numpy as jnp
from jax import lax
from jax.experimental import pallas as pl
from jax.experimental.pallas import tpu as pltpu
from jax.sharding import PartitionSpec as P

HD = 128
IMG_TOK = 64
MAX_IMG = 8
D = 4096
SHARDS = 8
BLOCK = 1792
rope_base = 500000.0
eps = 1e-05
BF16 = jnp.bfloat16
F32 = jnp.float32
VMEM = pltpu.VMEM
SMEM = pltpu.SMEM


def rotary_tables(positions):
    half_size = HD // 2
    exponent = jnp.arange(half_size, dtype=F32) * (2.0 / HD)
    frequency = jnp.exp(-exponent * math.log(rope_base))
    angles = positions.astype(F32)[:, None] * frequency[None, :]
    return jnp.cos(angles), jnp.sin(angles)


def rotate(u, cosine, sine):
    cosine = jnp.concatenate([cosine, cosine], axis=1)
    sine = jnp.concatenate([-sine, sine], axis=1)
    return u * cosine + pltpu.roll(u, HD // 2, 1) * sine


def shift(x, axis, d, wrap):
    pairs = [(i, (i + d) % SHARDS) for i in range(SHARDS) if wrap or 0 <= i + d < SHARDS]
    return lax.ppermute(x, axis, pairs)


def exchange(x, mask):
    return lax.ppermute(x, "mp", [(i, i ^ mask) for i in range(4)])


def first_hop(x):
    return exchange(x, 1), exchange(x, 3)


def normalise(mp, gain_ref, pieces, out_ref, rows):
    total = 0.0
    for piece in pieces:
        wide = piece.astype(F32)
        total = total + jnp.sum(wide * wide, axis=1, keepdims=True)
    scale = lax.rsqrt(total * (1.0 / D) + eps)
    for mask, piece in zip((0, 1, 3, 2), pieces):
        columns = pl.ds(pl.multiple_of((mp ^ mask) * 1024, 1024), 1024)
        value = piece.astype(F32) * scale * gain_ref[:, columns]
        out_ref[rows, columns] = value.astype(BF16)


def write_key_value(x, w_ref, cos, sin, out_ref, rows):
    product = jnp.dot(x, w_ref[...], preferred_element_type=F32)
    out_ref[rows, :HD] = rotate(product[:, :HD], cos, sin).astype(BF16)
    out_ref[rows, HD:] = product[:, HD:].astype(BF16)


def image_kernel(ids_ref, own, one, three, two, gain, w_kv, w_q, cos, sin, *refs):
    out_ref, normed = refs[-2:]
    rows = own.shape[0]
    step = pl.program_id(0)

    @pl.when(step == 0)
    def _():
        pieces = [own[...], one[...], three[...], two[...]]
        normalise(ids_ref[0], gain, pieces, normed, slice(0, rows))
        write_key_value(normed[...], w_kv, cos[...], sin[...], out_ref, slice(0, rows))

    product = jnp.dot(normed[...], w_q[...], preferred_element_type=F32)
    span = pl.ds(pl.multiple_of((step + 1) * rows, IMG_TOK), rows)
    for h in range(2):
        columns = slice(h * HD, (h + 1) * HD)
        out_ref[span, columns] = rotate(product[:, columns], cos[...], sin[...]).astype(BF16)


def project_image(ids, arrays, gain, w_kv, w_query, tables, after):
    rows, tile = arrays[0].shape[0], 2 * HD
    steps = w_query.shape[1] // tile
    whole = pl.BlockSpec(memory_space=VMEM)
    return pl.pallas_call(
        image_kernel,
        out_shape=jax.ShapeDtypeStruct(((1 + steps) * rows, tile), BF16),
        grid=(steps,),
        in_specs=[pl.BlockSpec(memory_space=SMEM)]
        + [whole] * (len(arrays) + 2)
        + [pl.BlockSpec((D, tile), lambda n: (0, n))]
        + [whole] * 2
        + [pl.BlockSpec(memory_space=pl.ANY)] * len(after),
        out_specs=pl.BlockSpec(((1 + steps) * rows, tile), lambda n: (0, 0)),
        scratch_shapes=[pltpu.VMEM((rows, D), BF16)],
        compiler_params=pltpu.CompilerParams(vmem_limit_bytes=58 * 2**20),
        cost_estimate=pl.CostEstimate(flops=8 * 10**9, bytes_accessed=10 * 2**20, transcendentals=0),
        name="project_image",
    )(ids, *arrays, gain, w_kv, w_query, *tables, *after)


def hold_kernel(x_ref, *refs):
    refs[-1][...] = x_ref[...]


def hold(x, after):
    whole = pl.BlockSpec(memory_space=VMEM)
    return pl.pallas_call(
        hold_kernel,
        out_shape=jax.ShapeDtypeStruct(x.shape, x.dtype),
        in_specs=[whole] + [pl.BlockSpec(memory_space=pl.ANY)] * len(after),
        out_specs=whole,
        cost_estimate=pl.CostEstimate(flops=0, bytes_accessed=0, transcendentals=0),
        name="hold",
    )(x, *after)


def text_kernel(ids_ref, own, one_a, one_b, three_a, three_b, two_a, two_b, two_c, *refs):
    gain, w_kv, cos, sin = refs[:4]
    normed_ref, out_ref = refs[-2:]
    rows = own.shape[0]
    for n, others in enumerate(
        ((one_a, three_a, two_a), (one_b, three_b, two_b), (one_b, three_b, two_c))
    ):
        @pl.when(jnp.minimum(pl.program_id(0), 2) == n)
        def _():
            pieces = [own[...]] + [other[...] for other in others]
            normalise(ids_ref[0], gain, pieces, normed_ref, slice(0, rows))

    write_key_value(normed_ref[...], w_kv, cos[...], sin[...], out_ref, slice(0, rows))


def project_text(ids, arrays, gain, w_kv, tables, after):
    rows = arrays[0].shape[0]
    steps = 4
    tile = rows // steps

    def block(skipped):
        return pl.BlockSpec((tile, D // 4), lambda r: (jnp.maximum(r - skipped, 0), 0))

    whole = pl.BlockSpec(memory_space=VMEM)
    only = pl.BlockSpec((tile, D // 4), lambda r: (0, 0))
    table = pl.BlockSpec((tile, HD // 2), lambda r: (r, 0))
    return pl.pallas_call(
        text_kernel,
        out_shape=[
            jax.ShapeDtypeStruct((rows, D), BF16),
            jax.ShapeDtypeStruct((rows, 2 * HD), BF16),
        ],
        grid=(steps,),
        in_specs=[pl.BlockSpec(memory_space=SMEM)]
        + [block(0), only, block(1), only, block(1), only, only, block(2)]
        + [whole] * 2
        + [table] * 2
        + [pl.BlockSpec(memory_space=pl.ANY)] * len(after),
        out_specs=[
            pl.BlockSpec((tile, D), lambda r: (r, 0)),
            pl.BlockSpec((tile, 2 * HD), lambda r: (r, 0)),
        ],
        compiler_params=pltpu.CompilerParams(vmem_limit_bytes=58 * 2**20),
        cost_estimate=pl.CostEstimate(flops=0, bytes_accessed=0, transcendentals=0),
        name="project_text",
    )(ids, *arrays, gain, w_kv, *tables, *after)


def query_kernel(x_ref, w_ref, cos, sin, q_ref):
    product = jnp.dot(x_ref[...], w_ref[...], preferred_element_type=F32)
    for h in range(w_ref.shape[1] // HD):
        span = slice(h * HD, (h + 1) * HD)
        q_ref[:, span] = rotate(product[:, span], cos[...], sin[...]).astype(BF16)


def query(normed, w_query, tables, part, parts):
    rows, tile = normed.shape[0], 2 * HD
    columns = w_query.shape[1] // parts
    first = part * (columns // tile)
    whole = pl.BlockSpec(memory_space=VMEM)
    return pl.pallas_call(
        query_kernel,
        out_shape=jax.ShapeDtypeStruct((rows, columns), BF16),
        grid=(columns // tile,),
        in_specs=[whole, pl.BlockSpec((D, tile), lambda n: (0, first + n))] + [whole] * 2,
        out_specs=pl.BlockSpec((rows, tile), lambda n: (0, n)),
        compiler_params=pltpu.CompilerParams(vmem_limit_bytes=58 * 2**20),
        cost_estimate=pl.CostEstimate(flops=6 * 10**9, bytes_accessed=2**20, transcendentals=0),
        name="query",
    )(normed, w_query, *tables)


def images_before(counts_ref, sample):
    total = jnp.int32(0)
    for i in range(SHARDS):
        total = total + jnp.where(i < sample, counts_ref[i], 0)
    return total


def image_starts_of(ids_ref, counts_ref, starts_ref):
    sample = ids_ref[2]
    before = images_before(counts_ref, sample)
    for c in range(SHARDS):
        slot = (c - before) & (MAX_IMG - 1)
        yield c, jnp.where(slot < counts_ref[sample], starts_ref[sample, slot], -1)


def attention_kernel(tok, heads, ids_ref, counts_ref, starts_ref, *refs):
    q_one, q_two, own_e, own_l, f1, f2, f3, f4, b1, b2, b3, b4 = refs[:12]
    q_buf, img_kv, acc_out, max_out, sum_out = refs[12:17]
    kv_buf, img_buf, s_buf, max_buf, sum_buf, acc_buf, sems = refs[17:]
    ctx = ids_ref[1]
    factor = math.log2(math.e) / math.sqrt(HD)
    shift_by = tok.bit_length() - 1
    rows_e, rows_l = own_e.shape[0], own_l.shape[0]
    cut = rows_e // 2

    middle = heads * HD // 2
    moves = [(q_one, q_buf.at[:, :middle]), (q_two, q_buf.at[:, middle:])]
    for d, array, base, first, count in (
        (0, own_e, 0, 0, rows_e),
        (1, f1, 0, 0, rows_e),
        (2, f2, 0, 0, rows_e),
        (3, f3, 0, 0, rows_e),
        (4, f4, 0, cut, cut),
        (4, b4, rows_l, 0, cut),
        (5, b3, rows_l, 0, rows_e),
        (6, b2, rows_l, 0, rows_e),
        (7, b1, 0, 0, rows_e),
    ):
        shard = (ctx - d) & (SHARDS - 1)
        moves.append((array.at[pl.ds(base, count), :], img_buf.at[shard, pl.ds(first, count), :]))
    texts = ((own_l, 0), (f2, rows_e), (f3, rows_e), (f4, cut), (b4, 0), (b3, 0), (b2, 0))
    for n, (array, base) in enumerate(texts):
        moves.append((array.at[pl.ds(base, rows_l), :], kv_buf.at[pl.ds(n * tok, tok), :]))
    copies = [
        pltpu.make_async_copy(source, target, sems.at[n])
        for n, (source, target) in enumerate(moves)
    ]
    for copy in copies:
        copy.start()
    for copy in copies:
        copy.wait()
    for c, start in image_starts_of(ids_ref, counts_ref, starts_ref):
        img_kv[c] = img_buf[c, :IMG_TOK, :]
        shard, row = start >> shift_by, start & (tok - 1)
        distance = ctx - shard

        @pl.when((start >= 0) & (distance >= 0) & (distance != 4))
        def _():
            place = jnp.where(distance > 4, distance - 1, distance) * tok + row
            kv_buf[pl.ds(pl.multiple_of(place, IMG_TOK), IMG_TOK), :] = img_buf[c, :IMG_TOK, :]

        @pl.when((start >= 0) & (distance == 0))
        def _():
            rows = pl.ds(pl.multiple_of(row, IMG_TOK), IMG_TOK)
            for n in range(heads // 2):
                q_buf[rows, n * 2 * HD : (n + 1) * 2 * HD] = img_buf[
                    c, IMG_TOK * (n + 1) : IMG_TOK * (n + 2), :
                ]

    max_out[...] = jnp.zeros((tok, HD), F32)
    sum_out[...] = jnp.zeros((tok, HD), F32)

    def phase(step, do_score, do_mix):
        slot = lax.rem(step, 2)
        other = 1 - slot

        def block(j):
            keys = pl.ds(pl.multiple_of(j * BLOCK, BLOCK), BLOCK)
            if do_score:
                columns = pl.ds(pl.multiple_of(step * HD, HD), HD)
                s = lax.dot_general(
                    q_buf[:, columns],
                    kv_buf[keys, :HD],
                    (((1,), (1,)), ((), ())),
                    preferred_element_type=F32,
                )
                row = lax.broadcasted_iota(jnp.int32, (tok, HD), 0)
                column = lax.broadcasted_iota(jnp.int32, (tok, HD), 1)
                top = max_buf[slot]
                for g in range(BLOCK // HD):
                    place = j * BLOCK + g * HD
                    nth = place >> shift_by
                    earlier = nth + jnp.where(nth > 3, 1, 0) <= ctx
                    ahead = jnp.where(nth == 0, place, jnp.where(earlier, -tok, tok))
                    seen = s[:, g * HD : (g + 1) * HD]
                    seen = jnp.where(column + ahead <= row, seen, -1e30)
                    s_buf[slot, j, :, g * HD : (g + 1) * HD] = seen
                    top = jnp.maximum(top, seen)
                max_buf[slot] = top
            if do_mix:
                shared = max_buf[other]
                total = sum_buf[...]
                weights = []
                for g in range(BLOCK // HD):
                    w = jnp.exp2(s_buf[other, j, :, g * HD : (g + 1) * HD] * factor - shared)
                    total = total + w
                    weights.append(w.astype(BF16))
                sum_buf[...] = total
                acc_buf[...] += jnp.dot(
                    jnp.concatenate(weights, axis=1), kv_buf[keys, HD:], preferred_element_type=F32
                )

        if do_score:
            max_buf[slot] = jnp.full((tok, HD), -1e30, F32)
        if do_mix:
            sum_buf[...] = jnp.zeros((tok, HD), F32)
            acc_buf[...] = jnp.zeros((tok, HD), F32)
        pl.loop(0, jnp.where(ctx * tok + tok > BLOCK, 2, 1))(block)
        if do_score:
            top = jnp.max(max_buf[slot], axis=1, keepdims=True) * factor
            max_buf[slot] = jnp.broadcast_to(top, (tok, HD))
        if do_mix:
            head = step - 1
            here = lax.broadcasted_iota(jnp.int32, (tok, HD), 1) == head
            max_out[...] = jnp.where(here, max_buf[other], max_out[...])
            total = jnp.sum(sum_buf[...], axis=1, keepdims=True)
            sum_out[...] = jnp.where(here, total, sum_out[...])
            acc_out[:, pl.ds(pl.multiple_of(head * HD, HD), HD)] = acc_buf[...]

    phase(jnp.int32(0), True, False)
    pl.loop(1, heads)(lambda step: phase(step, True, True))
    phase(jnp.int32(heads), False, True)


def attention(tok, heads, scalars, arrays):
    img_rows = IMG_TOK * (1 + heads // 2)
    keys = (SHARDS - 1) * tok
    return pl.pallas_call(
        functools.partial(attention_kernel, tok, heads),
        out_shape=[
            jax.ShapeDtypeStruct((tok, heads * HD), BF16),
            jax.ShapeDtypeStruct((SHARDS, IMG_TOK, 2 * HD), BF16),
            jax.ShapeDtypeStruct((tok, heads * HD), F32),
            jax.ShapeDtypeStruct((tok, HD), F32),
            jax.ShapeDtypeStruct((tok, HD), F32),
        ],
        in_specs=[pl.BlockSpec(memory_space=SMEM)] * 3
        + [pl.BlockSpec(memory_space=pl.ANY)] * len(arrays),
        out_specs=[pl.BlockSpec(memory_space=VMEM)] * 5,
        scratch_shapes=[
            pltpu.VMEM((keys, 2 * HD), BF16),
            pltpu.VMEM((SHARDS, img_rows, 2 * HD), BF16),
            pltpu.VMEM((2, keys // BLOCK, tok, BLOCK), F32),
            pltpu.VMEM((2, tok, HD), F32),
            pltpu.VMEM((tok, HD), F32),
            pltpu.VMEM((tok, HD), F32),
            pltpu.SemaphoreType.DMA((32,)),
        ],
        compiler_params=pltpu.CompilerParams(vmem_limit_bytes=34 * 2**20),
        cost_estimate=pl.CostEstimate(
            flops=4 * tok * heads * keys * HD,
            bytes_accessed=8 * 2**20,
            transcendentals=tok * heads * keys,
        ),
        name="attention",
    )(*scalars, *arrays)


def finish_kernel(tok, ids_ref, counts_ref, starts_ref, *refs):
    q_ref, img_kv, lower, upper, acc_ref, max_ref, sum_ref, out_ref, kv_buf = refs
    ctx = ids_ref[1]
    step = pl.program_id(0)
    factor = math.log2(math.e) / math.sqrt(HD)
    shift_by = tok.bit_length() - 1

    @pl.when(step == 0)
    def _():
        half = lower.shape[0]
        kv_buf[:half, :] = lower[...]
        kv_buf[half:, :] = upper[...]
        for c, start in image_starts_of(ids_ref, counts_ref, starts_ref):
            @pl.when((start >= 0) & (ctx - (start >> shift_by) == 4))
            def _():
                rows = pl.ds(pl.multiple_of(start & (tok - 1), IMG_TOK), IMG_TOK)
                kv_buf[rows, :] = img_kv[c]

    def of_head(ref, head):
        here = lax.broadcasted_iota(jnp.int32, (tok, HD), 1) == head
        return jnp.sum(jnp.where(here, ref[...], 0.0), axis=1, keepdims=True)

    count = out_ref.shape[1] // HD

    @pl.when(ctx >= 4)
    def _():
        for n in range(count):
            span = slice(n * HD, (n + 1) * HD)
            s = lax.dot_general(
                q_ref[:, span],
                kv_buf[:, :HD],
                (((1,), (1,)), ((), ())),
                preferred_element_type=F32,
            )
            before = of_head(max_ref, step * count + n)
            top = jnp.maximum(before, jnp.max(s, axis=1, keepdims=True) * factor)
            scale = jnp.exp2(before - top)
            w = jnp.exp2(s * factor - top)
            total = of_head(sum_ref, step * count + n) * scale + jnp.sum(w, axis=1, keepdims=True)
            mixed = jnp.dot(w.astype(BF16), kv_buf[:, HD:], preferred_element_type=F32)
            out_ref[:, span] = ((acc_ref[:, span] * scale + mixed) / total).astype(BF16)

    @pl.when(ctx < 4)
    def _():
        for n in range(count):
            span = slice(n * HD, (n + 1) * HD)
            total = of_head(sum_ref, step * count + n)
            out_ref[:, span] = (acc_ref[:, span] / total).astype(BF16)


def finish(tok, heads, scalars, q_all, img_kv, lower, upper, state):
    width = 2 * HD
    whole = pl.BlockSpec(memory_space=VMEM)
    block = pl.BlockSpec((tok, width), lambda n: (0, n))
    return pl.pallas_call(
        functools.partial(finish_kernel, tok),
        out_shape=jax.ShapeDtypeStruct((tok, heads * HD), BF16),
        grid=(heads * HD // width,),
        in_specs=[pl.BlockSpec(memory_space=SMEM)] * 3 + [block] + [whole] * 3 + [block] + [whole] * 2,
        out_specs=block,
        scratch_shapes=[pltpu.VMEM((tok, 2 * HD), BF16)],
        compiler_params=pltpu.CompilerParams(vmem_limit_bytes=24 * 2**20),
        cost_estimate=pl.CostEstimate(
            flops=4 * tok * heads * tok * HD, bytes_accessed=6 * 2**20, transcendentals=0
        ),
        name="finish",
    )(*scalars, q_all, img_kv, lower, upper, *state)


def on_device(
    text_rows, visual_rows, image_counts, image_starts, norm_gain, w_query, w_key, w_value
):
    ctx = lax.axis_index("ctx").astype(jnp.int32)
    sample = lax.axis_index("dp").astype(jnp.int32)
    mp = lax.axis_index("mp").astype(jnp.int32)
    tok = text_rows.shape[0]
    heads = w_query.shape[1] // HD
    ids = jnp.stack([mp, ctx, sample])

    w_kv = jnp.concatenate([w_key, w_value], axis=1)
    gain = norm_gain[None, :]
    every = jnp.arange(SHARDS, dtype=jnp.int32)

    def source(who):
        before = jnp.sum(jnp.where(every < who, image_counts, 0))
        slot = (ctx - before) & (MAX_IMG - 1)
        owner = jnp.minimum((before + slot) >> 3, SHARDS - 1)
        return slot, (owner ^ who) & 1, jnp.clip((who >> 1) - (owner >> 1), 0, 3)

    def choose(which, choices):
        chosen = choices[0]
        for n, choice in enumerate(choices[1:], 1):
            chosen = jnp.where(which == n, choice, chosen)
        return chosen

    my_slot, my_across, my_distance = source(sample)
    _, _, its_distance = source(sample ^ 1)
    mine = (every[:, None] == sample) & (every[None, :] == my_slot)
    my_start = jnp.sum(jnp.where(mine, image_starts, 0))
    text_tables = rotary_tables(ctx * tok + jnp.arange(tok, dtype=jnp.int32))
    image_tables = rotary_tables(my_start + jnp.arange(IMG_TOK, dtype=jnp.int32))
    quarter = tok // 4
    group_a, group_b = text_rows[:quarter], text_rows[quarter:]
    one_a, three_a = first_hop(group_a)
    one_b, three_b = first_hop(group_b)
    leaving = hold(visual_rows, (one_a, three_a, ids, *image_tables))
    routed = [visual_rows] + [shift(leaving, "dp", 2 * d, False) for d in (1, 2, 3)]
    for_other = choose(its_distance, routed)
    from_other = lax.ppermute(for_other, "dp", [(i, i ^ 1) for i in range(SHARDS)])
    image = choose(jnp.where(my_across == 1, 4, my_distance), routed + [from_other])
    image_parts = [image] + [exchange(image, mask) for mask in (1, 3, 2)]
    two_a = exchange(one_a, 3)
    two_b = exchange(one_b[:quarter], 3)
    two_c = exchange(three_b[quarter:], 1)

    own_e = project_image(
        ids, image_parts, gain, w_kv, w_query, image_tables,
        (one_a, three_a, *text_tables),
    )
    normed, own_l = project_text(
        ids, [text_rows, one_a, one_b, three_a, three_b, two_a, two_b, two_c],
        gain, w_kv, text_tables, (own_e,)
    )
    queries = [query(normed, w_query, text_tables, n, 2) for n in range(2)]

    cut, part = own_e.shape[0] // 2, tok // 2
    f1, b1 = shift(own_e, "ctx", 1, True), shift(own_e, "ctx", -1, True)
    f2 = shift(jnp.concatenate([f1, own_l], axis=0), "ctx", 1, True)
    b2 = shift(jnp.concatenate([own_l, b1], axis=0), "ctx", -1, True)
    f3, b3 = shift(f2, "ctx", 1, True), shift(b2, "ctx", -1, True)
    f4, b4 = shift(f3[cut:], "ctx", 1, True), shift(b3[: tok + cut], "ctx", -1, True)
    f5 = shift(f4[cut : cut + part], "ctx", 1, True)
    b5 = shift(b4[part:tok], "ctx", -1, True)
    scalars = (ids, image_counts, image_starts)
    q_all, img_kv, *state = attention(
        tok, heads, scalars, [*queries, own_e, own_l, f1, f2, f3, f4, b1, b2, b3, b4]
    )
    return finish(tok, heads, scalars, q_all, img_kv, f5, b5, state)


def solution(mesh):
    in_specs = (
        P(("dp", "ctx"), "mp"),
        P(("dp", "ctx"), "mp"),
        P(),
        P(),
        P(),
        P(None, "mp"),
        P(None, "mp"),
        P(None, "mp"),
    )
    out_specs = P(("dp", "ctx"), "mp")
    return jax.shard_map(
        on_device, mesh=mesh, in_specs=in_specs, out_specs=out_specs, check_vma=False
    )
```

```python
import functools
import math

import jax
import jax.numpy as jnp
from jax import lax
from jax.experimental import pallas as pl
from jax.experimental.pallas import tpu as pltpu
from jax.sharding import PartitionSpec as P

HD = 128
IMG_TOK = 64
MAX_IMG = 8
D = 4096
SHARDS = 8
BLOCK = 1792
rope_base = 500000.0
eps = 1e-05
BF16 = jnp.bfloat16
F32 = jnp.float32
VMEM = pltpu.VMEM
SMEM = pltpu.SMEM


def rotary_tables(positions):
    half_size = HD // 2
    exponent = jnp.arange(half_size, dtype=F32) * (2.0 / HD)
    frequency = jnp.exp(-exponent * math.log(rope_base))
    angles = positions.astype(F32)[:, None] * frequency[None, :]
    return jnp.cos(angles), jnp.sin(angles)


def rotate(u, cosine, sine):
    cosine = jnp.concatenate([cosine, cosine], axis=1)
    sine = jnp.concatenate([-sine, sine], axis=1)
    return u * cosine + pltpu.roll(u, HD // 2, 1) * sine


def shift(x, axis, d, wrap):
    pairs = [(i, (i + d) % SHARDS) for i in range(SHARDS) if wrap or 0 <= i + d < SHARDS]
    return lax.ppermute(x, axis, pairs)


def exchange(x, mask):
    return lax.ppermute(x, "mp", [(i, i ^ mask) for i in range(4)])


def first_hop(x):
    return exchange(x, 1), exchange(x, 3)


def normalise(mp, gain_ref, pieces, out_ref, rows):
    total = 0.0
    for piece in pieces:
        wide = piece.astype(F32)
        total = total + jnp.sum(wide * wide, axis=1, keepdims=True)
    scale = lax.rsqrt(total * (1.0 / D) + eps)
    for mask, piece in zip((0, 1, 3, 2), pieces):
        columns = pl.ds(pl.multiple_of((mp ^ mask) * 1024, 1024), 1024)
        value = piece.astype(F32) * scale * gain_ref[:, columns]
        out_ref[rows, columns] = value.astype(BF16)


def write_key_value(x, w_ref, cos, sin, out_ref, rows):
    product = jnp.dot(x, w_ref[...], preferred_element_type=F32)
    out_ref[rows, :HD] = rotate(product[:, :HD], cos, sin).astype(BF16)
    out_ref[rows, HD:] = product[:, HD:].astype(BF16)


def image_kernel(ids_ref, own, one, three, two, gain, w_kv, w_q, cos, sin, *refs):
    out_ref, normed = refs[-2:]
    rows = own.shape[0]
    step = pl.program_id(0)

    @pl.when(step == 0)
    def _():
        pieces = [own[...], one[...], three[...], two[...]]
        normalise(ids_ref[0], gain, pieces, normed, slice(0, rows))
        write_key_value(normed[...], w_kv, cos[...], sin[...], out_ref, slice(0, rows))

    product = jnp.dot(normed[...], w_q[...], preferred_element_type=F32)
    span = pl.ds(pl.multiple_of((step + 1) * rows, IMG_TOK), rows)
    for h in range(2):
        columns = slice(h * HD, (h + 1) * HD)
        out_ref[span, columns] = rotate(product[:, columns], cos[...], sin[...]).astype(BF16)


def project_image(ids, arrays, gain, w_kv, w_query, tables, after):
    rows, tile = arrays[0].shape[0], 2 * HD
    steps = w_query.shape[1] // tile
    whole = pl.BlockSpec(memory_space=VMEM)
    return pl.pallas_call(
        image_kernel,
        out_shape=jax.ShapeDtypeStruct(((1 + steps) * rows, tile), BF16),
        grid=(steps,),
        in_specs=[pl.BlockSpec(memory_space=SMEM)]
        + [whole] * (len(arrays) + 2)
        + [pl.BlockSpec((D, tile), lambda n: (0, n))]
        + [whole] * 2
        + [pl.BlockSpec(memory_space=pl.ANY)] * len(after),
        out_specs=pl.BlockSpec(((1 + steps) * rows, tile), lambda n: (0, 0)),
        scratch_shapes=[pltpu.VMEM((rows, D), BF16)],
        compiler_params=pltpu.CompilerParams(vmem_limit_bytes=58 * 2**20),
        cost_estimate=pl.CostEstimate(flops=8 * 10**9, bytes_accessed=10 * 2**20, transcendentals=0),
        name="project_image",
    )(ids, *arrays, gain, w_kv, w_query, *tables, *after)


def hold_kernel(x_ref, *refs):
    refs[-1][...] = x_ref[...]


def hold(x, after):
    whole = pl.BlockSpec(memory_space=VMEM)
    return pl.pallas_call(
        hold_kernel,
        out_shape=jax.ShapeDtypeStruct(x.shape, x.dtype),
        in_specs=[whole] + [pl.BlockSpec(memory_space=pl.ANY)] * len(after),
        out_specs=whole,
        cost_estimate=pl.CostEstimate(flops=0, bytes_accessed=0, transcendentals=0),
        name="hold",
    )(x, *after)


def text_kernel(ids_ref, own, one_a, one_b, three_a, three_b, two_a, two_b, two_c, *refs):
    gain, w_kv, cos, sin = refs[:4]
    normed_ref, out_ref, held = refs[-3:]
    rows = own.shape[0]
    step = pl.program_id(0)
    last = pl.num_programs(0) - 1
    slot = lax.rem(step, 2)

    def phase(do_norm, do_product):
        if do_norm:
            pieces = [
                own[...],
                jnp.where(step == 0, one_a[...], one_b[...]),
                jnp.where(step == 0, three_a[...], three_b[...]),
                jnp.where(step == 0, two_a[...], jnp.where(step == 1, two_b[...], two_c[...])),
            ]
            normalise(ids_ref[0], gain, pieces, held.at[slot], slice(0, rows))
            normed_ref[...] = held[slot]
        if do_product:
            write_key_value(held[1 - slot], w_kv, cos[...], sin[...], out_ref, slice(0, rows))

    pl.when(step == 0)(lambda: phase(True, False))
    pl.when((step > 0) & (step < last))(lambda: phase(True, True))
    pl.when(step == last)(lambda: phase(False, True))


def project_text(ids, arrays, gain, w_kv, tables, after):
    rows = arrays[0].shape[0]
    steps = 4
    tile = rows // steps

    def block(skipped):
        return pl.BlockSpec(
            (tile, D // 4), lambda r: (jnp.clip(r - skipped, 0, steps - 1 - skipped), 0)
        )

    whole = pl.BlockSpec(memory_space=VMEM)
    only = pl.BlockSpec((tile, D // 4), lambda r: (0, 0))
    table = pl.BlockSpec((tile, HD // 2), lambda r: (jnp.maximum(r - 1, 0), 0))
    return pl.pallas_call(
        text_kernel,
        out_shape=[
            jax.ShapeDtypeStruct((rows, D), BF16),
            jax.ShapeDtypeStruct((rows, 2 * HD), BF16),
        ],
        grid=(steps + 1,),
        in_specs=[pl.BlockSpec(memory_space=SMEM)]
        + [block(0), only, block(1), only, block(1), only, only, block(2)]
        + [whole] * 2
        + [table] * 2
        + [pl.BlockSpec(memory_space=pl.ANY)] * len(after),
        out_specs=[
            pl.BlockSpec((tile, D), lambda r: (jnp.minimum(r, steps - 1), 0)),
            pl.BlockSpec((tile, 2 * HD), lambda r: (jnp.maximum(r - 1, 0), 0)),
        ],
        scratch_shapes=[pltpu.VMEM((2, tile, D), BF16)],
        compiler_params=pltpu.CompilerParams(vmem_limit_bytes=58 * 2**20),
        cost_estimate=pl.CostEstimate(flops=0, bytes_accessed=0, transcendentals=0),
        name="project_text",
    )(ids, *arrays, gain, w_kv, *tables, *after)


def query_kernel(x_ref, w_ref, cos, sin, q_ref):
    product = jnp.dot(x_ref[...], w_ref[...], preferred_element_type=F32)
    for h in range(w_ref.shape[1] // HD):
        span = slice(h * HD, (h + 1) * HD)
        q_ref[:, span] = rotate(product[:, span], cos[...], sin[...]).astype(BF16)


def query(normed, w_query, tables, part, parts):
    rows, tile = normed.shape[0], 2 * HD
    columns = w_query.shape[1] // parts
    first = part * (columns // tile)
    whole = pl.BlockSpec(memory_space=VMEM)
    return pl.pallas_call(
        query_kernel,
        out_shape=jax.ShapeDtypeStruct((rows, columns), BF16),
        grid=(columns // tile,),
        in_specs=[whole, pl.BlockSpec((D, tile), lambda n: (0, first + n))] + [whole] * 2,
        out_specs=pl.BlockSpec((rows, tile), lambda n: (0, n)),
        compiler_params=pltpu.CompilerParams(vmem_limit_bytes=58 * 2**20),
        cost_estimate=pl.CostEstimate(flops=6 * 10**9, bytes_accessed=2**20, transcendentals=0),
        name="query",
    )(normed, w_query, *tables)


def images_before(counts_ref, sample):
    total = jnp.int32(0)
    for i in range(SHARDS):
        total = total + jnp.where(i < sample, counts_ref[i], 0)
    return total


def image_starts_of(ids_ref, counts_ref, starts_ref):
    sample = ids_ref[2]
    before = images_before(counts_ref, sample)
    for c in range(SHARDS):
        slot = (c - before) & (MAX_IMG - 1)
        yield c, jnp.where(slot < counts_ref[sample], starts_ref[sample, slot], -1)


def attention_kernel(tok, heads, ids_ref, counts_ref, starts_ref, *refs):
    q_one, q_two, own_e, own_l, f1, f2, f3, f4, b1, b2, b3, b4 = refs[:12]
    q_buf, img_kv, acc_out, max_out, sum_out = refs[12:17]
    kv_buf, img_buf, s_buf, max_buf, sum_buf, acc_buf, sems = refs[17:]
    ctx = ids_ref[1]
    factor = math.log2(math.e) / math.sqrt(HD)
    shift_by = tok.bit_length() - 1
    rows_e, rows_l = own_e.shape[0], own_l.shape[0]
    cut = rows_e // 2

    middle = heads * HD // 2
    moves = [(q_one, q_buf.at[:, :middle]), (q_two, q_buf.at[:, middle:])]
    for d, array, base, first, count in (
        (0, own_e, 0, 0, rows_e),
        (1, f1, 0, 0, rows_e),
        (2, f2, 0, 0, rows_e),
        (3, f3, 0, 0, rows_e),
        (4, f4, 0, cut, cut),
        (4, b4, rows_l, 0, cut),
        (5, b3, rows_l, 0, rows_e),
        (6, b2, rows_l, 0, rows_e),
        (7, b1, 0, 0, rows_e),
    ):
        shard = (ctx - d) & (SHARDS - 1)
        moves.append((array.at[pl.ds(base, count), :], img_buf.at[shard, pl.ds(first, count), :]))
    texts = ((own_l, 0), (f2, rows_e), (f3, rows_e), (f4, cut), (b4, 0), (b3, 0), (b2, 0))
    for n, (array, base) in enumerate(texts):
        moves.append((array.at[pl.ds(base, rows_l), :], kv_buf.at[pl.ds(n * tok, tok), :]))
    copies = [
        pltpu.make_async_copy(source, target, sems.at[n])
        for n, (source, target) in enumerate(moves)
    ]
    for copy in copies:
        copy.start()
    for copy in copies[:-3]:
        copy.wait()

    def place_images(near):
        for c, start in image_starts_of(ids_ref, counts_ref, starts_ref):
            shard, row = start >> shift_by, start & (tok - 1)
            distance = ctx - shard
            taken = (distance >= 0) & (distance < 4) if near else distance > 4

            @pl.when((start >= 0) & taken)
            def _():
                place = (distance if near else distance - 1) * tok + row
                rows = pl.ds(pl.multiple_of(place, IMG_TOK), IMG_TOK)
                kv_buf[rows, :] = img_buf[c, :IMG_TOK, :]

            if near:
                img_kv[c] = img_buf[c, :IMG_TOK, :]

                @pl.when((start >= 0) & (distance == 0))
                def _():
                    rows = pl.ds(pl.multiple_of(row, IMG_TOK), IMG_TOK)
                    for n in range(heads // 2):
                        q_buf[rows, n * 2 * HD : (n + 1) * 2 * HD] = img_buf[
                            c, IMG_TOK * (n + 1) : IMG_TOK * (n + 2), :
                        ]

    place_images(True)
    max_out[...] = jnp.zeros((tok, HD), F32)
    sum_out[...] = jnp.zeros((tok, HD), F32)

    def phase(step, do_score, do_mix):
        slot = lax.rem(step, 2)
        other = 1 - slot

        def block(j):
            keys = pl.ds(pl.multiple_of(j * BLOCK, BLOCK), BLOCK)
            if do_score:
                columns = pl.ds(pl.multiple_of(step * HD, HD), HD)
                s = lax.dot_general(
                    q_buf[:, columns],
                    kv_buf[keys, :HD],
                    (((1,), (1,)), ((), ())),
                    preferred_element_type=F32,
                )
                row = lax.broadcasted_iota(jnp.int32, (tok, HD), 0)
                column = lax.broadcasted_iota(jnp.int32, (tok, HD), 1)
                top = max_buf[slot]
                for g in range(BLOCK // HD):
                    place = j * BLOCK + g * HD
                    nth = place >> shift_by
                    earlier = nth + jnp.where(nth > 3, 1, 0) <= ctx
                    ahead = jnp.where(nth == 0, place, jnp.where(earlier, -tok, tok))
                    seen = s[:, g * HD : (g + 1) * HD]
                    seen = jnp.where(column + ahead <= row, seen, -1e30)
                    s_buf[slot, j, :, g * HD : (g + 1) * HD] = seen
                    top = jnp.maximum(top, seen)
                max_buf[slot] = top
            if do_mix:
                shared = max_buf[other]
                total = sum_buf[...]
                weights = []
                for g in range(BLOCK // HD):
                    w = jnp.exp2(s_buf[other, j, :, g * HD : (g + 1) * HD] * factor - shared)
                    total = total + w
                    weights.append(w.astype(BF16))
                sum_buf[...] = total
                acc_buf[...] += jnp.dot(
                    jnp.concatenate(weights, axis=1), kv_buf[keys, HD:], preferred_element_type=F32
                )

        if do_score:
            max_buf[slot] = jnp.full((tok, HD), -1e30, F32)
        if do_mix:
            sum_buf[...] = jnp.zeros((tok, HD), F32)
            acc_buf[...] = jnp.zeros((tok, HD), F32)
        blocks = jnp.where(ctx * tok + tok > BLOCK, 2, 1)
        if do_mix:
            pl.loop(0, blocks)(block)
        else:
            block(jnp.int32(0))
            for copy in copies[-3:]:
                copy.wait()
            place_images(False)
            pl.loop(1, blocks)(block)
        if do_score:
            top = jnp.max(max_buf[slot], axis=1, keepdims=True) * factor
            max_buf[slot] = jnp.broadcast_to(top, (tok, HD))
        if do_mix:
            head = step - 1
            here = lax.broadcasted_iota(jnp.int32, (tok, HD), 1) == head
            max_out[...] = jnp.where(here, max_buf[other], max_out[...])
            total = jnp.sum(sum_buf[...], axis=1, keepdims=True)
            sum_out[...] = jnp.where(here, total, sum_out[...])
            acc_out[:, pl.ds(pl.multiple_of(head * HD, HD), HD)] = acc_buf[...]

    phase(jnp.int32(0), True, False)
    pl.loop(1, heads)(lambda step: phase(step, True, True))
    phase(jnp.int32(heads), False, True)


def attention(tok, heads, scalars, arrays):
    img_rows = IMG_TOK * (1 + heads // 2)
    keys = (SHARDS - 1) * tok
    return pl.pallas_call(
        functools.partial(attention_kernel, tok, heads),
        out_shape=[
            jax.ShapeDtypeStruct((tok, heads * HD), BF16),
            jax.ShapeDtypeStruct((SHARDS, IMG_TOK, 2 * HD), BF16),
            jax.ShapeDtypeStruct((tok, heads * HD), F32),
            jax.ShapeDtypeStruct((tok, HD), F32),
            jax.ShapeDtypeStruct((tok, HD), F32),
        ],
        in_specs=[pl.BlockSpec(memory_space=SMEM)] * 3
        + [pl.BlockSpec(memory_space=pl.ANY)] * len(arrays),
        out_specs=[pl.BlockSpec(memory_space=VMEM)] * 5,
        scratch_shapes=[
            pltpu.VMEM((keys, 2 * HD), BF16),
            pltpu.VMEM((SHARDS, img_rows, 2 * HD), BF16),
            pltpu.VMEM((2, keys // BLOCK, tok, BLOCK), F32),
            pltpu.VMEM((2, tok, HD), F32),
            pltpu.VMEM((tok, HD), F32),
            pltpu.VMEM((tok, HD), F32),
            pltpu.SemaphoreType.DMA((32,)),
        ],
        compiler_params=pltpu.CompilerParams(vmem_limit_bytes=34 * 2**20),
        cost_estimate=pl.CostEstimate(
            flops=4 * tok * heads * keys * HD,
            bytes_accessed=8 * 2**20,
            transcendentals=tok * heads * keys,
        ),
        name="attention",
    )(*scalars, *arrays)


def finish_kernel(tok, ids_ref, counts_ref, starts_ref, *refs):
    q_ref, img_kv, lower, upper, acc_ref, max_ref, sum_ref, out_ref, kv_buf = refs
    ctx = ids_ref[1]
    step = pl.program_id(0)
    factor = math.log2(math.e) / math.sqrt(HD)
    shift_by = tok.bit_length() - 1

    @pl.when(step == 0)
    def _():
        half = lower.shape[0]
        kv_buf[:half, :] = lower[...]
        kv_buf[half:, :] = upper[...]
        for c, start in image_starts_of(ids_ref, counts_ref, starts_ref):
            @pl.when((start >= 0) & (ctx - (start >> shift_by) == 4))
            def _():
                rows = pl.ds(pl.multiple_of(start & (tok - 1), IMG_TOK), IMG_TOK)
                kv_buf[rows, :] = img_kv[c]

    def of_head(ref, head):
        here = lax.broadcasted_iota(jnp.int32, (tok, HD), 1) == head
        return jnp.sum(jnp.where(here, ref[...], 0.0), axis=1, keepdims=True)

    count = out_ref.shape[1] // HD

    @pl.when(ctx >= 4)
    def _():
        for n in range(count):
            span = slice(n * HD, (n + 1) * HD)
            s = lax.dot_general(
                q_ref[:, span],
                kv_buf[:, :HD],
                (((1,), (1,)), ((), ())),
                preferred_element_type=F32,
            )
            before = of_head(max_ref, step * count + n)
            top = jnp.maximum(before, jnp.max(s, axis=1, keepdims=True) * factor)
            scale = jnp.exp2(before - top)
            w = jnp.exp2(s * factor - top)
            total = of_head(sum_ref, step * count + n) * scale + jnp.sum(w, axis=1, keepdims=True)
            mixed = jnp.dot(w.astype(BF16), kv_buf[:, HD:], preferred_element_type=F32)
            out_ref[:, span] = ((acc_ref[:, span] * scale + mixed) / total).astype(BF16)

    @pl.when(ctx < 4)
    def _():
        for n in range(count):
            span = slice(n * HD, (n + 1) * HD)
            total = of_head(sum_ref, step * count + n)
            out_ref[:, span] = (acc_ref[:, span] / total).astype(BF16)


def finish(tok, heads, scalars, q_all, img_kv, lower, upper, state):
    width = 4 * HD
    whole = pl.BlockSpec(memory_space=VMEM)
    block = pl.BlockSpec((tok, width), lambda n: (0, n))
    return pl.pallas_call(
        functools.partial(finish_kernel, tok),
        out_shape=jax.ShapeDtypeStruct((tok, heads * HD), BF16),
        grid=(heads * HD // width,),
        in_specs=[pl.BlockSpec(memory_space=SMEM)] * 3 + [block] + [whole] * 3 + [block] + [whole] * 2,
        out_specs=block,
        scratch_shapes=[pltpu.VMEM((tok, 2 * HD), BF16)],
        compiler_params=pltpu.CompilerParams(vmem_limit_bytes=24 * 2**20),
        cost_estimate=pl.CostEstimate(
            flops=4 * tok * heads * tok * HD, bytes_accessed=6 * 2**20, transcendentals=0
        ),
        name="finish",
    )(*scalars, q_all, img_kv, lower, upper, *state)


def on_device(
    text_rows, visual_rows, image_counts, image_starts, norm_gain, w_query, w_key, w_value
):
    ctx = lax.axis_index("ctx").astype(jnp.int32)
    sample = lax.axis_index("dp").astype(jnp.int32)
    mp = lax.axis_index("mp").astype(jnp.int32)
    tok = text_rows.shape[0]
    heads = w_query.shape[1] // HD
    ids = jnp.stack([mp, ctx, sample])

    w_kv = jnp.concatenate([w_key, w_value], axis=1)
    gain = norm_gain[None, :]
    every = jnp.arange(SHARDS, dtype=jnp.int32)

    def source(who):
        before = jnp.sum(jnp.where(every < who, image_counts, 0))
        slot = (ctx - before) & (MAX_IMG - 1)
        owner = jnp.minimum((before + slot) >> 3, SHARDS - 1)
        return slot, (owner ^ who) & 1, jnp.clip((who >> 1) - (owner >> 1), 0, 3)

    def choose(which, choices):
        chosen = choices[0]
        for n, choice in enumerate(choices[1:], 1):
            chosen = jnp.where(which == n, choice, chosen)
        return chosen

    my_slot, my_across, my_distance = source(sample)
    _, _, its_distance = source(sample ^ 1)
    mine = (every[:, None] == sample) & (every[None, :] == my_slot)
    my_start = jnp.sum(jnp.where(mine, image_starts, 0))
    text_tables = rotary_tables(ctx * tok + jnp.arange(tok, dtype=jnp.int32))
    image_tables = rotary_tables(my_start + jnp.arange(IMG_TOK, dtype=jnp.int32))
    quarter = tok // 4
    group_a, group_b = text_rows[:quarter], text_rows[quarter:]
    one_a, three_a = first_hop(group_a)
    one_b, three_b = first_hop(group_b)
    leaving = hold(visual_rows, (one_a, three_a, ids, *image_tables, *text_tables))
    routed = [visual_rows] + [shift(leaving, "dp", 2 * d, False) for d in (1, 2, 3)]
    for_other = choose(its_distance, routed)
    from_other = lax.ppermute(for_other, "dp", [(i, i ^ 1) for i in range(SHARDS)])
    image = choose(jnp.where(my_across == 1, 4, my_distance), routed + [from_other])
    image_parts = [image] + [exchange(image, mask) for mask in (1, 3, 2)]
    two_a = exchange(one_a, 3)
    two_b = exchange(one_b[:quarter], 3)
    two_c = exchange(three_b[quarter:], 1)

    own_e = project_image(
        ids, image_parts, gain, w_kv, w_query, image_tables,
        (one_a, three_a, *text_tables),
    )
    normed, own_l = project_text(
        ids, [text_rows, one_a, one_b, three_a, three_b, two_a, two_b, two_c],
        gain, w_kv, text_tables, (own_e,)
    )
    queries = [query(normed, w_query, text_tables, n, 2) for n in range(2)]

    cut, part = own_e.shape[0] // 2, tok // 2
    f1, b1 = shift(own_e, "ctx", 1, True), shift(own_e, "ctx", -1, True)
    f2 = shift(jnp.concatenate([f1, own_l], axis=0), "ctx", 1, True)
    b2 = shift(jnp.concatenate([own_l, b1], axis=0), "ctx", -1, True)
    f3, b3 = shift(f2, "ctx", 1, True), shift(b2, "ctx", -1, True)
    f4, b4 = shift(f3[cut:], "ctx", 1, True), shift(b3[: tok + cut], "ctx", -1, True)
    f5 = shift(f4[cut : cut + part], "ctx", 1, True)
    b5 = shift(b4[part:tok], "ctx", -1, True)
    scalars = (ids, image_counts, image_starts)
    q_all, img_kv, *state = attention(
        tok, heads, scalars, [*queries, own_e, own_l, f1, f2, f3, f4, b1, b2, b3, b4]
    )
    return finish(tok, heads, scalars, q_all, img_kv, f5, b5, state)


def solution(mesh):
    in_specs = (
        P(("dp", "ctx"), "mp"),
        P(("dp", "ctx"), "mp"),
        P(),
        P(),
        P(),
        P(None, "mp"),
        P(None, "mp"),
        P(None, "mp"),
    )
    out_specs = P(("dp", "ctx"), "mp")
    return jax.shard_map(
        on_device, mesh=mesh, in_specs=in_specs, out_specs=out_specs, check_vma=False
    )
```

```python
import functools
import math

import jax
import jax.numpy as jnp
from jax import lax
from jax.experimental import pallas as pl
from jax.experimental.pallas import tpu as pltpu
from jax.sharding import PartitionSpec as P

HD = 128
IMG_TOK = 64
MAX_IMG = 8
D = 4096
SHARDS = 8
BLOCK = 1792
rope_base = 500000.0
eps = 1e-05
BF16 = jnp.bfloat16
F32 = jnp.float32
VMEM = pltpu.VMEM
SMEM = pltpu.SMEM


def rotary_tables(positions):
    half_size = HD // 2
    exponent = jnp.arange(half_size, dtype=F32) * (2.0 / HD)
    frequency = jnp.exp(-exponent * math.log(rope_base))
    angles = positions.astype(F32)[:, None] * frequency[None, :]
    return jnp.cos(angles), jnp.sin(angles)


def rotate(u, cosine, sine):
    cosine = jnp.concatenate([cosine, cosine], axis=1)
    sine = jnp.concatenate([-sine, sine], axis=1)
    return u * cosine + pltpu.roll(u, HD // 2, 1) * sine


def shift(x, axis, d, wrap):
    pairs = [(i, (i + d) % SHARDS) for i in range(SHARDS) if wrap or 0 <= i + d < SHARDS]
    return lax.ppermute(x, axis, pairs)


def exchange(x, mask):
    return lax.ppermute(x, "mp", [(i, i ^ mask) for i in range(4)])


def first_hop(x):
    return exchange(x, 1), exchange(x, 3)


def normalise(mp, gain_ref, pieces, out_ref, rows):
    total = 0.0
    for piece in pieces:
        wide = piece.astype(F32)
        total = total + jnp.sum(wide * wide, axis=1, keepdims=True)
    scale = lax.rsqrt(total * (1.0 / D) + eps)
    for mask, piece in zip((0, 1, 3, 2), pieces):
        columns = pl.ds(pl.multiple_of((mp ^ mask) * 1024, 1024), 1024)
        value = piece.astype(F32) * scale * gain_ref[:, columns]
        out_ref[rows, columns] = value.astype(BF16)


def write_key_value(x, w_ref, cos, sin, out_ref, rows):
    product = jnp.dot(x, w_ref[...], preferred_element_type=F32)
    out_ref[rows, :HD] = rotate(product[:, :HD], cos, sin).astype(BF16)
    out_ref[rows, HD:] = product[:, HD:].astype(BF16)


def image_kernel(ids_ref, own, one, three, two, gain, w_kv, w_q, cos, sin, *refs):
    out_ref, normed = refs[-2:]
    rows = own.shape[0]
    step = pl.program_id(0)

    @pl.when(step == 0)
    def _():
        pieces = [own[...], one[...], three[...], two[...]]
        normalise(ids_ref[0], gain, pieces, normed, slice(0, rows))
        write_key_value(normed[...], w_kv, cos[...], sin[...], out_ref, slice(0, rows))

    product = jnp.dot(normed[...], w_q[...], preferred_element_type=F32)
    span = pl.ds(pl.multiple_of((step + 1) * rows, IMG_TOK), rows)
    for h in range(2):
        columns = slice(h * HD, (h + 1) * HD)
        out_ref[span, columns] = rotate(product[:, columns], cos[...], sin[...]).astype(BF16)


def project_image(ids, arrays, gain, w_kv, w_query, tables, after):
    rows, tile = arrays[0].shape[0], 2 * HD
    steps = w_query.shape[1] // tile
    whole = pl.BlockSpec(memory_space=VMEM)
    return pl.pallas_call(
        image_kernel,
        out_shape=jax.ShapeDtypeStruct(((1 + steps) * rows, tile), BF16),
        grid=(steps,),
        in_specs=[pl.BlockSpec(memory_space=SMEM)]
        + [whole] * (len(arrays) + 2)
        + [pl.BlockSpec((D, tile), lambda n: (0, n))]
        + [whole] * 2
        + [pl.BlockSpec(memory_space=pl.ANY)] * len(after),
        out_specs=pl.BlockSpec(((1 + steps) * rows, tile), lambda n: (0, 0)),
        scratch_shapes=[pltpu.VMEM((rows, D), BF16)],
        compiler_params=pltpu.CompilerParams(vmem_limit_bytes=58 * 2**20),
        cost_estimate=pl.CostEstimate(flops=8 * 10**9, bytes_accessed=10 * 2**20, transcendentals=0),
        name="project_image",
    )(ids, *arrays, gain, w_kv, w_query, *tables, *after)


def hold_kernel(x_ref, *refs):
    refs[-1][...] = x_ref[...]


def hold(x, after):
    whole = pl.BlockSpec(memory_space=VMEM)
    return pl.pallas_call(
        hold_kernel,
        out_shape=jax.ShapeDtypeStruct(x.shape, x.dtype),
        in_specs=[whole] + [pl.BlockSpec(memory_space=pl.ANY)] * len(after),
        out_specs=whole,
        cost_estimate=pl.CostEstimate(flops=0, bytes_accessed=0, transcendentals=0),
        name="hold",
    )(x, *after)


def text_kernel(ids_ref, own, one_a, one_b, three_a, three_b, two_a, two_b, two_c, *refs):
    gain, w_kv, cos, sin = refs[:4]
    normed_ref, out_ref = refs[-2:]
    rows = own.shape[0]
    for n, others in enumerate(
        ((one_a, three_a, two_a), (one_b, three_b, two_b), (one_b, three_b, two_c))
    ):
        @pl.when(jnp.minimum(pl.program_id(0), 2) == n)
        def _():
            pieces = [own[...]] + [other[...] for other in others]
            normalise(ids_ref[0], gain, pieces, normed_ref, slice(0, rows))

    write_key_value(normed_ref[...], w_kv, cos[...], sin[...], out_ref, slice(0, rows))


def project_text(ids, arrays, gain, w_kv, tables, after):
    rows = arrays[0].shape[0]
    steps = 4
    tile = rows // steps

    def block(skipped):
        return pl.BlockSpec((tile, D // 4), lambda r: (jnp.maximum(r - skipped, 0), 0))

    whole = pl.BlockSpec(memory_space=VMEM)
    only = pl.BlockSpec((tile, D // 4), lambda r: (0, 0))
    table = pl.BlockSpec((tile, HD // 2), lambda r: (r, 0))
    return pl.pallas_call(
        text_kernel,
        out_shape=[
            jax.ShapeDtypeStruct((rows, D), BF16),
            jax.ShapeDtypeStruct((rows, 2 * HD), BF16),
        ],
        grid=(steps,),
        in_specs=[pl.BlockSpec(memory_space=SMEM)]
        + [block(0), only, block(1), only, block(1), only, only, block(2)]
        + [whole] * 2
        + [table] * 2
        + [pl.BlockSpec(memory_space=pl.ANY)] * len(after),
        out_specs=[
            pl.BlockSpec((tile, D), lambda r: (r, 0)),
            pl.BlockSpec((tile, 2 * HD), lambda r: (r, 0)),
        ],
        compiler_params=pltpu.CompilerParams(vmem_limit_bytes=58 * 2**20),
        cost_estimate=pl.CostEstimate(flops=0, bytes_accessed=0, transcendentals=0),
        name="project_text",
    )(ids, *arrays, gain, w_kv, *tables, *after)


def query_kernel(x_ref, w_ref, cos, sin, q_ref):
    product = jnp.dot(x_ref[...], w_ref[...], preferred_element_type=F32)
    for h in range(w_ref.shape[1] // HD):
        span = slice(h * HD, (h + 1) * HD)
        q_ref[:, span] = rotate(product[:, span], cos[...], sin[...]).astype(BF16)


def query(normed, w_query, tables, part, parts):
    rows, tile = normed.shape[0], 2 * HD
    columns = w_query.shape[1] // parts
    first = part * (columns // tile)
    whole = pl.BlockSpec(memory_space=VMEM)
    return pl.pallas_call(
        query_kernel,
        out_shape=jax.ShapeDtypeStruct((rows, columns), BF16),
        grid=(columns // tile,),
        in_specs=[whole, pl.BlockSpec((D, tile), lambda n: (0, first + n))] + [whole] * 2,
        out_specs=pl.BlockSpec((rows, tile), lambda n: (0, n)),
        compiler_params=pltpu.CompilerParams(vmem_limit_bytes=58 * 2**20),
        cost_estimate=pl.CostEstimate(flops=6 * 10**9, bytes_accessed=2**20, transcendentals=0),
        name="query",
    )(normed, w_query, *tables)


def images_before(counts_ref, sample):
    total = jnp.int32(0)
    for i in range(SHARDS):
        total = total + jnp.where(i < sample, counts_ref[i], 0)
    return total


def image_starts_of(ids_ref, counts_ref, starts_ref):
    sample = ids_ref[2]
    before = images_before(counts_ref, sample)
    for c in range(SHARDS):
        slot = (c - before) & (MAX_IMG - 1)
        yield c, jnp.where(slot < counts_ref[sample], starts_ref[sample, slot], -1)


def attention_kernel(tok, heads, ids_ref, counts_ref, starts_ref, *refs):
    q_one, q_two, own_e, own_l, f1, f2, f3, f4, b1, b2, b3, b4 = refs[:12]
    q_buf, img_kv, acc_out, max_out, sum_out = refs[12:17]
    kv_buf, img_buf, s_buf, max_buf, sum_buf, acc_buf, sems = refs[17:]
    ctx = ids_ref[1]
    factor = math.log2(math.e) / math.sqrt(HD)
    shift_by = tok.bit_length() - 1
    rows_e, rows_l = own_e.shape[0], own_l.shape[0]
    cut = rows_e // 2

    middle = heads * HD // 2
    moves = [(q_one, q_buf.at[:, :middle]), (q_two, q_buf.at[:, middle:])]
    for d, array, base, first, count in (
        (0, own_e, 0, 0, rows_e),
        (1, f1, 0, 0, rows_e),
        (2, f2, 0, 0, rows_e),
        (3, f3, 0, 0, rows_e),
        (4, f4, 0, cut, cut),
        (4, b4, rows_l, 0, cut),
        (5, b3, rows_l, 0, rows_e),
        (6, b2, rows_l, 0, rows_e),
        (7, b1, 0, 0, rows_e),
    ):
        shard = (ctx - d) & (SHARDS - 1)
        moves.append((array.at[pl.ds(base, count), :], img_buf.at[shard, pl.ds(first, count), :]))
    texts = ((own_l, 0), (f2, rows_e), (f3, rows_e), (f4, cut), (b4, 0), (b3, 0), (b2, 0))
    for n, (array, base) in enumerate(texts):
        moves.append((array.at[pl.ds(base, rows_l), :], kv_buf.at[pl.ds(n * tok, tok), :]))
    copies = [
        pltpu.make_async_copy(source, target, sems.at[n])
        for n, (source, target) in enumerate(moves)
    ]
    for copy in copies:
        copy.start()
    for copy in copies[:-3]:
        copy.wait()

    def place_images(near):
        for c, start in image_starts_of(ids_ref, counts_ref, starts_ref):
            shard, row = start >> shift_by, start & (tok - 1)
            distance = ctx - shard
            taken = (distance >= 0) & (distance < 4) if near else distance > 4

            @pl.when((start >= 0) & taken)
            def _():
                place = (distance if near else distance - 1) * tok + row
                rows = pl.ds(pl.multiple_of(place, IMG_TOK), IMG_TOK)
                kv_buf[rows, :] = img_buf[c, :IMG_TOK, :]

            if near:
                img_kv[c] = img_buf[c, :IMG_TOK, :]

                @pl.when((start >= 0) & (distance == 0))
                def _():
                    rows = pl.ds(pl.multiple_of(row, IMG_TOK), IMG_TOK)
                    for n in range(heads // 2):
                        q_buf[rows, n * 2 * HD : (n + 1) * 2 * HD] = img_buf[
                            c, IMG_TOK * (n + 1) : IMG_TOK * (n + 2), :
                        ]

    place_images(True)
    max_out[...] = jnp.zeros((tok, HD), F32)
    sum_out[...] = jnp.zeros((tok, HD), F32)

    def phase(step, do_score, do_mix):
        slot = lax.rem(step, 2)
        other = 1 - slot

        def block(j):
            keys = pl.ds(pl.multiple_of(j * BLOCK, BLOCK), BLOCK)
            if do_score:
                columns = pl.ds(pl.multiple_of(step * HD, HD), HD)
                s = lax.dot_general(
                    q_buf[:, columns],
                    kv_buf[keys, :HD],
                    (((1,), (1,)), ((), ())),
                    preferred_element_type=F32,
                )
                row = lax.broadcasted_iota(jnp.int32, (tok, HD), 0)
                column = lax.broadcasted_iota(jnp.int32, (tok, HD), 1)
                top = max_buf[slot]
                for g in range(BLOCK // HD):
                    place = j * BLOCK + g * HD
                    nth = place >> shift_by
                    earlier = nth + jnp.where(nth > 3, 1, 0) <= ctx
                    ahead = jnp.where(nth == 0, place, jnp.where(earlier, -tok, tok))
                    seen = s[:, g * HD : (g + 1) * HD]
                    seen = jnp.where(column + ahead <= row, seen, -1e30)
                    s_buf[slot, j, :, g * HD : (g + 1) * HD] = seen
                    top = jnp.maximum(top, seen)
                max_buf[slot] = top
            if do_mix:
                shared = max_buf[other]
                total = sum_buf[...]
                weights = []
                for g in range(BLOCK // HD):
                    w = jnp.exp2(s_buf[other, j, :, g * HD : (g + 1) * HD] * factor - shared)
                    total = total + w
                    weights.append(w.astype(BF16))
                sum_buf[...] = total
                acc_buf[...] += jnp.dot(
                    jnp.concatenate(weights, axis=1), kv_buf[keys, HD:], preferred_element_type=F32
                )

        if do_score:
            max_buf[slot] = jnp.full((tok, HD), -1e30, F32)
        if do_mix:
            sum_buf[...] = jnp.zeros((tok, HD), F32)
            acc_buf[...] = jnp.zeros((tok, HD), F32)
        blocks = jnp.where(ctx * tok + tok > BLOCK, 2, 1)
        if do_mix:
            pl.loop(0, blocks)(block)
        else:
            block(jnp.int32(0))
            for copy in copies[-3:]:
                copy.wait()
            place_images(False)
            pl.loop(1, blocks)(block)
        if do_score:
            top = jnp.max(max_buf[slot], axis=1, keepdims=True) * factor
            max_buf[slot] = jnp.broadcast_to(top, (tok, HD))
        if do_mix:
            head = step - 1
            here = lax.broadcasted_iota(jnp.int32, (tok, HD), 1) == head
            max_out[...] = jnp.where(here, max_buf[other], max_out[...])
            total = jnp.sum(sum_buf[...], axis=1, keepdims=True)
            sum_out[...] = jnp.where(here, total, sum_out[...])
            acc_out[:, pl.ds(pl.multiple_of(head * HD, HD), HD)] = acc_buf[...]

    phase(jnp.int32(0), True, False)
    pl.loop(1, heads)(lambda step: phase(step, True, True))
    phase(jnp.int32(heads), False, True)


def attention(tok, heads, scalars, arrays):
    img_rows = IMG_TOK * (1 + heads // 2)
    keys = (SHARDS - 1) * tok
    return pl.pallas_call(
        functools.partial(attention_kernel, tok, heads),
        out_shape=[
            jax.ShapeDtypeStruct((tok, heads * HD), BF16),
            jax.ShapeDtypeStruct((SHARDS, IMG_TOK, 2 * HD), BF16),
            jax.ShapeDtypeStruct((tok, heads * HD), F32),
            jax.ShapeDtypeStruct((tok, HD), F32),
            jax.ShapeDtypeStruct((tok, HD), F32),
        ],
        in_specs=[pl.BlockSpec(memory_space=SMEM)] * 3
        + [pl.BlockSpec(memory_space=pl.ANY)] * len(arrays),
        out_specs=[pl.BlockSpec(memory_space=VMEM)] * 5,
        scratch_shapes=[
            pltpu.VMEM((keys, 2 * HD), BF16),
            pltpu.VMEM((SHARDS, img_rows, 2 * HD), BF16),
            pltpu.VMEM((2, keys // BLOCK, tok, BLOCK), F32),
            pltpu.VMEM((2, tok, HD), F32),
            pltpu.VMEM((tok, HD), F32),
            pltpu.VMEM((tok, HD), F32),
            pltpu.SemaphoreType.DMA((32,)),
        ],
        compiler_params=pltpu.CompilerParams(vmem_limit_bytes=34 * 2**20),
        cost_estimate=pl.CostEstimate(
            flops=4 * tok * heads * keys * HD,
            bytes_accessed=8 * 2**20,
            transcendentals=tok * heads * keys,
        ),
        name="attention",
    )(*scalars, *arrays)


def finish_kernel(tok, ids_ref, counts_ref, starts_ref, *refs):
    q_ref, img_kv, lower, upper, acc_ref, max_ref, sum_ref, out_ref, kv_buf = refs
    ctx = ids_ref[1]
    step = pl.program_id(0)
    factor = math.log2(math.e) / math.sqrt(HD)
    shift_by = tok.bit_length() - 1

    @pl.when(step == 0)
    def _():
        half = lower.shape[0]
        kv_buf[:half, :] = lower[...]
        kv_buf[half:, :] = upper[...]
        for c, start in image_starts_of(ids_ref, counts_ref, starts_ref):
            @pl.when((start >= 0) & (ctx - (start >> shift_by) == 4))
            def _():
                rows = pl.ds(pl.multiple_of(start & (tok - 1), IMG_TOK), IMG_TOK)
                kv_buf[rows, :] = img_kv[c]

    def of_head(ref, head):
        here = lax.broadcasted_iota(jnp.int32, (tok, HD), 1) == head
        return jnp.sum(jnp.where(here, ref[...], 0.0), axis=1, keepdims=True)

    count = out_ref.shape[1] // HD

    @pl.when(ctx >= 4)
    def _():
        for n in range(count):
            span = slice(n * HD, (n + 1) * HD)
            s = lax.dot_general(
                q_ref[:, span],
                kv_buf[:, :HD],
                (((1,), (1,)), ((), ())),
                preferred_element_type=F32,
            )
            before = of_head(max_ref, step * count + n)
            top = jnp.maximum(before, jnp.max(s, axis=1, keepdims=True) * factor)
            scale = jnp.exp2(before - top)
            w = jnp.exp2(s * factor - top)
            total = of_head(sum_ref, step * count + n) * scale + jnp.sum(w, axis=1, keepdims=True)
            mixed = jnp.dot(w.astype(BF16), kv_buf[:, HD:], preferred_element_type=F32)
            out_ref[:, span] = ((acc_ref[:, span] * scale + mixed) / total).astype(BF16)

    @pl.when(ctx < 4)
    def _():
        for n in range(count):
            span = slice(n * HD, (n + 1) * HD)
            total = of_head(sum_ref, step * count + n)
            out_ref[:, span] = (acc_ref[:, span] / total).astype(BF16)


def finish(tok, heads, scalars, q_all, img_kv, lower, upper, state):
    width = 4 * HD
    whole = pl.BlockSpec(memory_space=VMEM)
    block = pl.BlockSpec((tok, width), lambda n: (0, n))
    return pl.pallas_call(
        functools.partial(finish_kernel, tok),
        out_shape=jax.ShapeDtypeStruct((tok, heads * HD), BF16),
        grid=(heads * HD // width,),
        in_specs=[pl.BlockSpec(memory_space=SMEM)] * 3 + [block] + [whole] * 3 + [block] + [whole] * 2,
        out_specs=block,
        scratch_shapes=[pltpu.VMEM((tok, 2 * HD), BF16)],
        compiler_params=pltpu.CompilerParams(vmem_limit_bytes=24 * 2**20),
        cost_estimate=pl.CostEstimate(
            flops=4 * tok * heads * tok * HD, bytes_accessed=6 * 2**20, transcendentals=0
        ),
        name="finish",
    )(*scalars, q_all, img_kv, lower, upper, *state)


def on_device(
    text_rows, visual_rows, image_counts, image_starts, norm_gain, w_query, w_key, w_value
):
    ctx = lax.axis_index("ctx").astype(jnp.int32)
    sample = lax.axis_index("dp").astype(jnp.int32)
    mp = lax.axis_index("mp").astype(jnp.int32)
    tok = text_rows.shape[0]
    heads = w_query.shape[1] // HD
    ids = jnp.stack([mp, ctx, sample])

    w_kv = jnp.concatenate([w_key, w_value], axis=1)
    gain = norm_gain[None, :]
    every = jnp.arange(SHARDS, dtype=jnp.int32)

    def source(who):
        before = jnp.sum(jnp.where(every < who, image_counts, 0))
        slot = (ctx - before) & (MAX_IMG - 1)
        owner = jnp.minimum((before + slot) >> 3, SHARDS - 1)
        return slot, (owner ^ who) & 1, jnp.clip((who >> 1) - (owner >> 1), 0, 3)

    def choose(which, choices):
        chosen = choices[0]
        for n, choice in enumerate(choices[1:], 1):
            chosen = jnp.where(which == n, choice, chosen)
        return chosen

    my_slot, my_across, my_distance = source(sample)
    _, _, its_distance = source(sample ^ 1)
    mine = (every[:, None] == sample) & (every[None, :] == my_slot)
    my_start = jnp.sum(jnp.where(mine, image_starts, 0))
    text_tables = rotary_tables(ctx * tok + jnp.arange(tok, dtype=jnp.int32))
    image_tables = rotary_tables(my_start + jnp.arange(IMG_TOK, dtype=jnp.int32))
    quarter = tok // 4
    group_a, group_b = text_rows[:quarter], text_rows[quarter:]
    one_a, three_a = first_hop(group_a)
    one_b, three_b = first_hop(group_b)
    leaving = hold(visual_rows, (one_a, three_a, ids, *image_tables))
    routed = [visual_rows] + [shift(leaving, "dp", 2 * d, False) for d in (1, 2, 3)]
    for_other = choose(its_distance, routed)
    from_other = lax.ppermute(for_other, "dp", [(i, i ^ 1) for i in range(SHARDS)])
    image = choose(jnp.where(my_across == 1, 4, my_distance), routed + [from_other])
    image_parts = [image] + [exchange(image, mask) for mask in (1, 3, 2)]
    two_a = exchange(one_a, 3)
    two_b = exchange(one_b[:quarter], 3)
    two_c = exchange(three_b[quarter:], 1)

    own_e = project_image(
        ids, image_parts, gain, w_kv, w_query, image_tables,
        (one_a, three_a, *text_tables),
    )
    normed, own_l = project_text(
        ids, [text_rows, one_a, one_b, three_a, three_b, two_a, two_b, two_c],
        gain, w_kv, text_tables, (own_e,)
    )
    queries = [query(normed, w_query, text_tables, n, 2) for n in range(2)]

    cut, part = own_e.shape[0] // 2, tok // 2
    f1, b1 = shift(own_e, "ctx", 1, True), shift(own_e, "ctx", -1, True)
    f2 = shift(jnp.concatenate([f1, own_l], axis=0), "ctx", 1, True)
    b2 = shift(jnp.concatenate([own_l, b1], axis=0), "ctx", -1, True)
    f3, b3 = shift(f2, "ctx", 1, True), shift(b2, "ctx", -1, True)
    f4, b4 = shift(f3[cut:], "ctx", 1, True), shift(b3[: tok + cut], "ctx", -1, True)
    f5 = shift(f4[cut : cut + part], "ctx", 1, True)
    b5 = shift(b4[part:tok], "ctx", -1, True)
    scalars = (ids, image_counts, image_starts)
    q_all, img_kv, *state = attention(
        tok, heads, scalars, [*queries, own_e, own_l, f1, f2, f3, f4, b1, b2, b3, b4]
    )
    return finish(tok, heads, scalars, q_all, img_kv, f5, b5, state)


def solution(mesh):
    in_specs = (
        P(("dp", "ctx"), "mp"),
        P(("dp", "ctx"), "mp"),
        P(),
        P(),
        P(),
        P(None, "mp"),
        P(None, "mp"),
        P(None, "mp"),
    )
    out_specs = P(("dp", "ctx"), "mp")
    return jax.shard_map(
        on_device, mesh=mesh, in_specs=in_specs, out_specs=out_specs, check_vma=False
    )
```

```python
import functools
import math

import jax
import jax.numpy as jnp
from jax import lax
from jax.experimental import pallas as pl
from jax.experimental.pallas import tpu as pltpu
from jax.sharding import PartitionSpec as P

HD = 128
IMG_TOK = 64
MAX_IMG = 8
D = 4096
SHARDS = 8
BLOCK = 1792
rope_base = 500000.0
eps = 1e-05
BF16 = jnp.bfloat16
F32 = jnp.float32
VMEM = pltpu.VMEM
SMEM = pltpu.SMEM


def rotary_tables(positions):
    half_size = HD // 2
    exponent = jnp.arange(half_size, dtype=F32) * (2.0 / HD)
    frequency = jnp.exp(-exponent * math.log(rope_base))
    angles = positions.astype(F32)[:, None] * frequency[None, :]
    return jnp.cos(angles), jnp.sin(angles)


def rotate(u, cosine, sine):
    cosine = jnp.concatenate([cosine, cosine], axis=1)
    sine = jnp.concatenate([-sine, sine], axis=1)
    return u * cosine + pltpu.roll(u, HD // 2, 1) * sine


def shift(x, axis, d, wrap):
    pairs = [(i, (i + d) % SHARDS) for i in range(SHARDS) if wrap or 0 <= i + d < SHARDS]
    return lax.ppermute(x, axis, pairs)


def exchange(x, mask):
    return lax.ppermute(x, "mp", [(i, i ^ mask) for i in range(4)])


def first_hop(x):
    return exchange(x, 1), exchange(x, 3)


def normalise(mp, gain_ref, pieces, out_ref, rows):
    total = 0.0
    for piece in pieces:
        wide = piece.astype(F32)
        total = total + jnp.sum(wide * wide, axis=1, keepdims=True)
    scale = lax.rsqrt(total * (1.0 / D) + eps)
    for mask, piece in zip((0, 1, 3, 2), pieces):
        columns = pl.ds(pl.multiple_of((mp ^ mask) * 1024, 1024), 1024)
        value = piece.astype(F32) * scale * gain_ref[:, columns]
        out_ref[rows, columns] = value.astype(BF16)


def write_key_value(x, w_ref, cos, sin, out_ref, rows):
    product = jnp.dot(x, w_ref[...], preferred_element_type=F32)
    out_ref[rows, :HD] = rotate(product[:, :HD], cos, sin).astype(BF16)
    out_ref[rows, HD:] = product[:, HD:].astype(BF16)


def image_kernel(ids_ref, own, one, three, two, gain, w_kv, w_q, cos, sin, *refs):
    out_ref, normed = refs[-2:]
    rows = own.shape[0]
    step = pl.program_id(0)

    @pl.when(step == 0)
    def _():
        pieces = [own[...], one[...], three[...], two[...]]
        normalise(ids_ref[0], gain, pieces, normed, slice(0, rows))
        write_key_value(normed[...], w_kv, cos[...], sin[...], out_ref, slice(0, rows))

    product = jnp.dot(normed[...], w_q[...], preferred_element_type=F32)
    span = pl.ds(pl.multiple_of((step + 1) * rows, IMG_TOK), rows)
    for h in range(2):
        columns = slice(h * HD, (h + 1) * HD)
        out_ref[span, columns] = rotate(product[:, columns], cos[...], sin[...]).astype(BF16)


def project_image(ids, arrays, gain, w_kv, w_query, tables, after):
    rows, tile = arrays[0].shape[0], 2 * HD
    steps = w_query.shape[1] // tile
    whole = pl.BlockSpec(memory_space=VMEM)
    return pl.pallas_call(
        image_kernel,
        out_shape=jax.ShapeDtypeStruct(((1 + steps) * rows, tile), BF16),
        grid=(steps,),
        in_specs=[pl.BlockSpec(memory_space=SMEM)]
        + [whole] * (len(arrays) + 2)
        + [pl.BlockSpec((D, tile), lambda n: (0, n))]
        + [whole] * 2
        + [pl.BlockSpec(memory_space=pl.ANY)] * len(after),
        out_specs=pl.BlockSpec(((1 + steps) * rows, tile), lambda n: (0, 0)),
        scratch_shapes=[pltpu.VMEM((rows, D), BF16)],
        compiler_params=pltpu.CompilerParams(vmem_limit_bytes=58 * 2**20),
        cost_estimate=pl.CostEstimate(flops=8 * 10**9, bytes_accessed=10 * 2**20, transcendentals=0),
        name="project_image",
    )(ids, *arrays, gain, w_kv, w_query, *tables, *after)


def hold_kernel(x_ref, *refs):
    refs[-1][...] = x_ref[...]


def hold(x, after):
    whole = pl.BlockSpec(memory_space=VMEM)
    return pl.pallas_call(
        hold_kernel,
        out_shape=jax.ShapeDtypeStruct(x.shape, x.dtype),
        in_specs=[whole] + [pl.BlockSpec(memory_space=pl.ANY)] * len(after),
        out_specs=whole,
        cost_estimate=pl.CostEstimate(flops=0, bytes_accessed=0, transcendentals=0),
        name="hold",
    )(x, *after)


def text_kernel(ids_ref, own, one_a, one_b, three_a, three_b, two_a, two_b, two_c, *refs):
    gain, w_kv, cos, sin = refs[:4]
    normed_ref, out_ref = refs[-2:]
    rows = own.shape[0]
    for n, others in enumerate(
        ((one_a, three_a, two_a), (one_b, three_b, two_b), (one_b, three_b, two_c))
    ):
        @pl.when(jnp.minimum(pl.program_id(0), 2) == n)
        def _():
            pieces = [own[...]] + [other[...] for other in others]
            normalise(ids_ref[0], gain, pieces, normed_ref, slice(0, rows))

    write_key_value(normed_ref[...], w_kv, cos[...], sin[...], out_ref, slice(0, rows))


def project_text(ids, arrays, gain, w_kv, tables, after):
    rows = arrays[0].shape[0]
    steps = 4
    tile = rows // steps

    def block(skipped):
        return pl.BlockSpec((tile, D // 4), lambda r: (jnp.maximum(r - skipped, 0), 0))

    whole = pl.BlockSpec(memory_space=VMEM)
    only = pl.BlockSpec((tile, D // 4), lambda r: (0, 0))
    table = pl.BlockSpec((tile, HD // 2), lambda r: (r, 0))
    return pl.pallas_call(
        text_kernel,
        out_shape=[
            jax.ShapeDtypeStruct((rows, D), BF16),
            jax.ShapeDtypeStruct((rows, 2 * HD), BF16),
        ],
        grid=(steps,),
        in_specs=[pl.BlockSpec(memory_space=SMEM)]
        + [block(0), only, block(1), only, block(1), only, only, block(2)]
        + [whole] * 2
        + [table] * 2
        + [pl.BlockSpec(memory_space=pl.ANY)] * len(after),
        out_specs=[
            pl.BlockSpec((tile, D), lambda r: (r, 0)),
            pl.BlockSpec((tile, 2 * HD), lambda r: (r, 0)),
        ],
        compiler_params=pltpu.CompilerParams(vmem_limit_bytes=58 * 2**20),
        cost_estimate=pl.CostEstimate(flops=0, bytes_accessed=0, transcendentals=0),
        name="project_text",
    )(ids, *arrays, gain, w_kv, *tables, *after)


def query_kernel(x_ref, w_ref, cos, sin, q_ref):
    product = jnp.dot(x_ref[...], w_ref[...], preferred_element_type=F32)
    for h in range(w_ref.shape[1] // HD):
        span = slice(h * HD, (h + 1) * HD)
        q_ref[:, span] = rotate(product[:, span], cos[...], sin[...]).astype(BF16)


def query(normed, w_query, tables, part, parts):
    rows, tile = normed.shape[0], 2 * HD
    columns = w_query.shape[1] // parts
    first = part * (columns // tile)
    whole = pl.BlockSpec(memory_space=VMEM)
    return pl.pallas_call(
        query_kernel,
        out_shape=jax.ShapeDtypeStruct((rows, columns), BF16),
        grid=(columns // tile,),
        in_specs=[whole, pl.BlockSpec((D, tile), lambda n: (0, first + n))] + [whole] * 2,
        out_specs=pl.BlockSpec((rows, tile), lambda n: (0, n)),
        compiler_params=pltpu.CompilerParams(vmem_limit_bytes=58 * 2**20),
        cost_estimate=pl.CostEstimate(flops=6 * 10**9, bytes_accessed=2**20, transcendentals=0),
        name="query",
    )(normed, w_query, *tables)


def images_before(counts_ref, sample):
    total = jnp.int32(0)
    for i in range(SHARDS):
        total = total + jnp.where(i < sample, counts_ref[i], 0)
    return total


def image_starts_of(ids_ref, counts_ref, starts_ref):
    sample = ids_ref[2]
    before = images_before(counts_ref, sample)
    for c in range(SHARDS):
        slot = (c - before) & (MAX_IMG - 1)
        yield c, jnp.where(slot < counts_ref[sample], starts_ref[sample, slot], -1)


def attention_kernel(tok, heads, ids_ref, counts_ref, starts_ref, *refs):
    q_one, q_two, own_e, own_l, f1, f2, f3, f4, b1, b2, b3, b4 = refs[:12]
    q_buf, img_kv, acc_out, max_out, sum_out = refs[12:17]
    kv_buf, img_buf, s_buf, max_buf, sum_buf, acc_buf, sems = refs[17:]
    ctx = ids_ref[1]
    factor = math.log2(math.e) / math.sqrt(HD)
    shift_by = tok.bit_length() - 1
    rows_e, rows_l = own_e.shape[0], own_l.shape[0]
    cut = rows_e // 2

    middle = heads * HD // 2
    moves = [(q_one, q_buf.at[:, :middle]), (q_two, q_buf.at[:, middle:])]
    for d, array, base, first, count in (
        (0, own_e, 0, 0, rows_e),
        (1, f1, 0, 0, rows_e),
        (2, f2, 0, 0, rows_e),
        (3, f3, 0, 0, rows_e),
        (4, f4, 0, cut, cut),
        (4, b4, rows_l, 0, cut),
        (5, b3, rows_l, 0, rows_e),
        (6, b2, rows_l, 0, rows_e),
        (7, b1, 0, 0, rows_e),
    ):
        shard = (ctx - d) & (SHARDS - 1)
        moves.append((array.at[pl.ds(base, count), :], img_buf.at[shard, pl.ds(first, count), :]))
    texts = ((own_l, 0), (f2, rows_e), (f3, rows_e), (f4, cut), (b4, 0), (b3, 0), (b2, 0))
    for n, (array, base) in enumerate(texts):
        moves.append((array.at[pl.ds(base, rows_l), :], kv_buf.at[pl.ds(n * tok, tok), :]))
    copies = [
        pltpu.make_async_copy(source, target, sems.at[n])
        for n, (source, target) in enumerate(moves)
    ]
    for copy in copies:
        copy.start()
    for copy in copies[:-3]:
        copy.wait()

    def place_images(near):
        for c, start in image_starts_of(ids_ref, counts_ref, starts_ref):
            shard, row = start >> shift_by, start & (tok - 1)
            distance = ctx - shard
            taken = (distance >= 0) & (distance < 4) if near else distance > 4

            @pl.when((start >= 0) & taken)
            def _():
                place = (distance if near else distance - 1) * tok + row
                rows = pl.ds(pl.multiple_of(place, IMG_TOK), IMG_TOK)
                kv_buf[rows, :] = img_buf[c, :IMG_TOK, :]

            if near:
                img_kv[c] = img_buf[c, :IMG_TOK, :]

                @pl.when((start >= 0) & (distance == 0))
                def _():
                    rows = pl.ds(pl.multiple_of(row, IMG_TOK), IMG_TOK)
                    for n in range(heads // 2):
                        q_buf[rows, n * 2 * HD : (n + 1) * 2 * HD] = img_buf[
                            c, IMG_TOK * (n + 1) : IMG_TOK * (n + 2), :
                        ]

    place_images(True)
    max_out[...] = jnp.zeros((tok, HD), F32)
    sum_out[...] = jnp.zeros((tok, HD), F32)

    def phase(step, do_score, do_mix):
        slot = lax.rem(step, 2)
        other = 1 - slot

        def block(j):
            keys = pl.ds(pl.multiple_of(j * BLOCK, BLOCK), BLOCK)
            if do_score:
                columns = pl.ds(pl.multiple_of(step * HD, HD), HD)
                s = lax.dot_general(
                    q_buf[:, columns],
                    kv_buf[keys, :HD],
                    (((1,), (1,)), ((), ())),
                    preferred_element_type=F32,
                )
                row = lax.broadcasted_iota(jnp.int32, (tok, HD), 0)
                column = lax.broadcasted_iota(jnp.int32, (tok, HD), 1)
                top = max_buf[slot]
                for g in range(BLOCK // HD):
                    place = j * BLOCK + g * HD
                    nth = place >> shift_by
                    earlier = nth + jnp.where(nth > 3, 1, 0) <= ctx
                    ahead = jnp.where(nth == 0, place, jnp.where(earlier, -tok, tok))
                    seen = s[:, g * HD : (g + 1) * HD] * factor
                    seen = jnp.where(column + ahead <= row, seen, -1e30)
                    s_buf[slot, j, :, g * HD : (g + 1) * HD] = seen
                    top = jnp.maximum(top, seen)
                max_buf[slot] = top
            if do_mix:
                shared = max_buf[other]
                total = sum_buf[...]
                weights = []
                for g in range(BLOCK // HD):
                    w = jnp.exp2(s_buf[other, j, :, g * HD : (g + 1) * HD] - shared)
                    total = total + w
                    weights.append(w.astype(BF16))
                sum_buf[...] = total
                acc_buf[...] += jnp.dot(
                    jnp.concatenate(weights, axis=1), kv_buf[keys, HD:], preferred_element_type=F32
                )

        if do_score:
            max_buf[slot] = jnp.full((tok, HD), -1e30, F32)
        if do_mix:
            sum_buf[...] = jnp.zeros((tok, HD), F32)
            acc_buf[...] = jnp.zeros((tok, HD), F32)
        blocks = jnp.where(ctx * tok + tok > BLOCK, 2, 1)
        if do_mix:
            pl.loop(0, blocks)(block)
        else:
            block(jnp.int32(0))
            for copy in copies[-3:]:
                copy.wait()
            place_images(False)
            pl.loop(1, blocks)(block)
        if do_score:
            top = jnp.max(max_buf[slot], axis=1, keepdims=True)
            max_buf[slot] = jnp.broadcast_to(top, (tok, HD))
        if do_mix:
            head = step - 1
            here = lax.broadcasted_iota(jnp.int32, (tok, HD), 1) == head
            max_out[...] = jnp.where(here, max_buf[other], max_out[...])
            total = jnp.sum(sum_buf[...], axis=1, keepdims=True)
            sum_out[...] = jnp.where(here, total, sum_out[...])
            acc_out[:, pl.ds(pl.multiple_of(head * HD, HD), HD)] = acc_buf[...]

    phase(jnp.int32(0), True, False)
    pl.loop(1, heads)(lambda step: phase(step, True, True))
    phase(jnp.int32(heads), False, True)


def attention(tok, heads, scalars, arrays):
    img_rows = IMG_TOK * (1 + heads // 2)
    keys = (SHARDS - 1) * tok
    return pl.pallas_call(
        functools.partial(attention_kernel, tok, heads),
        out_shape=[
            jax.ShapeDtypeStruct((tok, heads * HD), BF16),
            jax.ShapeDtypeStruct((SHARDS, IMG_TOK, 2 * HD), BF16),
            jax.ShapeDtypeStruct((tok, heads * HD), F32),
            jax.ShapeDtypeStruct((tok, HD), F32),
            jax.ShapeDtypeStruct((tok, HD), F32),
        ],
        in_specs=[pl.BlockSpec(memory_space=SMEM)] * 3
        + [pl.BlockSpec(memory_space=pl.ANY)] * len(arrays),
        out_specs=[pl.BlockSpec(memory_space=VMEM)] * 5,
        scratch_shapes=[
            pltpu.VMEM((keys, 2 * HD), BF16),
            pltpu.VMEM((SHARDS, img_rows, 2 * HD), BF16),
            pltpu.VMEM((2, keys // BLOCK, tok, BLOCK), F32),
            pltpu.VMEM((2, tok, HD), F32),
            pltpu.VMEM((tok, HD), F32),
            pltpu.VMEM((tok, HD), F32),
            pltpu.SemaphoreType.DMA((32,)),
        ],
        compiler_params=pltpu.CompilerParams(vmem_limit_bytes=34 * 2**20),
        cost_estimate=pl.CostEstimate(
            flops=4 * tok * heads * keys * HD,
            bytes_accessed=8 * 2**20,
            transcendentals=tok * heads * keys,
        ),
        name="attention",
    )(*scalars, *arrays)


def finish_kernel(tok, ids_ref, counts_ref, starts_ref, *refs):
    q_ref, img_kv, lower, upper, acc_ref, max_ref, sum_ref, out_ref, kv_buf = refs
    ctx = ids_ref[1]
    step = pl.program_id(0)
    factor = math.log2(math.e) / math.sqrt(HD)
    shift_by = tok.bit_length() - 1

    @pl.when(step == 0)
    def _():
        half = lower.shape[0]
        kv_buf[:half, :] = lower[...]
        kv_buf[half:, :] = upper[...]
        for c, start in image_starts_of(ids_ref, counts_ref, starts_ref):
            @pl.when((start >= 0) & (ctx - (start >> shift_by) == 4))
            def _():
                rows = pl.ds(pl.multiple_of(start & (tok - 1), IMG_TOK), IMG_TOK)
                kv_buf[rows, :] = img_kv[c]

    def of_head(ref, head):
        here = lax.broadcasted_iota(jnp.int32, (tok, HD), 1) == head
        return jnp.sum(jnp.where(here, ref[...], 0.0), axis=1, keepdims=True)

    count = out_ref.shape[1] // HD

    @pl.when(ctx >= 4)
    def _():
        for n in range(count):
            span = slice(n * HD, (n + 1) * HD)
            s = lax.dot_general(
                q_ref[:, span],
                kv_buf[:, :HD],
                (((1,), (1,)), ((), ())),
                preferred_element_type=F32,
            )
            before = of_head(max_ref, step * count + n)
            top = jnp.maximum(before, jnp.max(s, axis=1, keepdims=True) * factor)
            scale = jnp.exp2(before - top)
            w = jnp.exp2(s * factor - top)
            total = of_head(sum_ref, step * count + n) * scale + jnp.sum(w, axis=1, keepdims=True)
            mixed = jnp.dot(w.astype(BF16), kv_buf[:, HD:], preferred_element_type=F32)
            out_ref[:, span] = ((acc_ref[:, span] * scale + mixed) / total).astype(BF16)

    @pl.when(ctx < 4)
    def _():
        for n in range(count):
            span = slice(n * HD, (n + 1) * HD)
            total = of_head(sum_ref, step * count + n)
            out_ref[:, span] = (acc_ref[:, span] / total).astype(BF16)


def finish(tok, heads, scalars, q_all, img_kv, lower, upper, state):
    width = 4 * HD
    whole = pl.BlockSpec(memory_space=VMEM)
    block = pl.BlockSpec((tok, width), lambda n: (0, n))
    return pl.pallas_call(
        functools.partial(finish_kernel, tok),
        out_shape=jax.ShapeDtypeStruct((tok, heads * HD), BF16),
        grid=(heads * HD // width,),
        in_specs=[pl.BlockSpec(memory_space=SMEM)] * 3 + [block] + [whole] * 3 + [block] + [whole] * 2,
        out_specs=block,
        scratch_shapes=[pltpu.VMEM((tok, 2 * HD), BF16)],
        compiler_params=pltpu.CompilerParams(vmem_limit_bytes=24 * 2**20),
        cost_estimate=pl.CostEstimate(
            flops=4 * tok * heads * tok * HD, bytes_accessed=6 * 2**20, transcendentals=0
        ),
        name="finish",
    )(*scalars, q_all, img_kv, lower, upper, *state)


def on_device(
    text_rows, visual_rows, image_counts, image_starts, norm_gain, w_query, w_key, w_value
):
    ctx = lax.axis_index("ctx").astype(jnp.int32)
    sample = lax.axis_index("dp").astype(jnp.int32)
    mp = lax.axis_index("mp").astype(jnp.int32)
    tok = text_rows.shape[0]
    heads = w_query.shape[1] // HD
    ids = jnp.stack([mp, ctx, sample])

    w_kv = jnp.concatenate([w_key, w_value], axis=1)
    gain = norm_gain[None, :]
    every = jnp.arange(SHARDS, dtype=jnp.int32)

    def source(who):
        before = jnp.sum(jnp.where(every < who, image_counts, 0))
        slot = (ctx - before) & (MAX_IMG - 1)
        owner = jnp.minimum((before + slot) >> 3, SHARDS - 1)
        return slot, (owner ^ who) & 1, jnp.clip((who >> 1) - (owner >> 1), 0, 3)

    def choose(which, choices):
        chosen = choices[0]
        for n, choice in enumerate(choices[1:], 1):
            chosen = jnp.where(which == n, choice, chosen)
        return chosen

    my_slot, my_across, my_distance = source(sample)
    _, _, its_distance = source(sample ^ 1)
    mine = (every[:, None] == sample) & (every[None, :] == my_slot)
    my_start = jnp.sum(jnp.where(mine, image_starts, 0))
    text_tables = rotary_tables(ctx * tok + jnp.arange(tok, dtype=jnp.int32))
    image_tables = rotary_tables(my_start + jnp.arange(IMG_TOK, dtype=jnp.int32))
    quarter = tok // 4
    group_a, group_b = text_rows[:quarter], text_rows[quarter:]
    one_a, three_a = first_hop(group_a)
    one_b, three_b = first_hop(group_b)
    leaving = hold(visual_rows, (one_a, three_a, ids, *image_tables))
    routed = [visual_rows] + [shift(leaving, "dp", 2 * d, False) for d in (1, 2, 3)]
    for_other = choose(its_distance, routed)
    from_other = lax.ppermute(for_other, "dp", [(i, i ^ 1) for i in range(SHARDS)])
    image = choose(jnp.where(my_across == 1, 4, my_distance), routed + [from_other])
    image_parts = [image] + [exchange(image, mask) for mask in (1, 3, 2)]
    two_a = exchange(one_a, 3)
    two_b = exchange(one_b[:quarter], 3)
    two_c = exchange(three_b[quarter:], 1)

    own_e = project_image(
        ids, image_parts, gain, w_kv, w_query, image_tables,
        (one_a, three_a, *text_tables),
    )
    normed, own_l = project_text(
        ids, [text_rows, one_a, one_b, three_a, three_b, two_a, two_b, two_c],
        gain, w_kv, text_tables, (own_e,)
    )
    queries = [query(normed, w_query, text_tables, n, 2) for n in range(2)]

    cut, part = own_e.shape[0] // 2, tok // 2
    f1, b1 = shift(own_e, "ctx", 1, True), shift(own_e, "ctx", -1, True)
    f2 = shift(jnp.concatenate([f1, own_l], axis=0), "ctx", 1, True)
    b2 = shift(jnp.concatenate([own_l, b1], axis=0), "ctx", -1, True)
    f3, b3 = shift(f2, "ctx", 1, True), shift(b2, "ctx", -1, True)
    f4, b4 = shift(f3[cut:], "ctx", 1, True), shift(b3[: tok + cut], "ctx", -1, True)
    f5 = shift(f4[cut : cut + part], "ctx", 1, True)
    b5 = shift(b4[part:tok], "ctx", -1, True)
    scalars = (ids, image_counts, image_starts)
    q_all, img_kv, *state = attention(
        tok, heads, scalars, [*queries, own_e, own_l, f1, f2, f3, f4, b1, b2, b3, b4]
    )
    return finish(tok, heads, scalars, q_all, img_kv, f5, b5, state)


def solution(mesh):
    in_specs = (
        P(("dp", "ctx"), "mp"),
        P(("dp", "ctx"), "mp"),
        P(),
        P(),
        P(),
        P(None, "mp"),
        P(None, "mp"),
        P(None, "mp"),
    )
    out_specs = P(("dp", "ctx"), "mp")
    return jax.shard_map(
        on_device, mesh=mesh, in_specs=in_specs, out_specs=out_specs, check_vma=False
    )
```
